512 devices in a mesh: lat: 16 (over y_hi, z), lon: 32 (over y_lo, x, core).
Axes of the slice: x: 4, y: 8 (y_hi: 2, y_lo: 4; y = y_hi * 4 + y_lo), z: 8, core: 2. Of those that a mesh axis runs over, the one named last changes fastest.
Arguments:
- tokens: bfloat16 [128, 512, 1152], P('lat', 'lon'), may hold values from -8 to 8
- gain: float32 [1152], replicated, may hold values from 0.25 to 1.75
- w_query: bfloat16 [1152, 576], P('lat'), may hold values from -1 to 1
- w_key: bfloat16 [1152, 576], P('lat'), may hold values from -1 to 1
- w_value: bfloat16 [1152, 576], P('lat'), may hold values from -0.1875 to 0.1875
- w_out: bfloat16 [576, 1152], P('lat'), may hold values from -0.25 to 0.25
- w_pixel: bfloat16 [1152, 192], replicated, may hold values from -0.1875 to 0.1875
- measured: float32 [128, 512, 64], P('lat', 'lon'), may hold values from -6 to 6
- filter_color: int32 [128, 512, 64], P('lat', 'lon'), may hold values from 0 to 2
- block_mask: int32 [16, 64, 3, 5], P('lat', 'lon'), may hold values from 0 to 1, as said below
Outputs:
- denoised: bfloat16 [128, 512, 1152], P('lat', 'lon')
- guidance: float32 [128, 512, 1152], P('lat', 'lon')
The draws below stay inside these ranges and needn't reach their ends.
Inputs may be any that keep to these rules, and one draw needn't show every extreme that they name: For each query block and row offset r the ones form one run of offsets centred on o = 2, of half-length 0 to 2; entries whose key block row a + r - 1 lies outside 0..15 are 0; block_mask[a, c, 1, 2] is 1.
All inputs are finite; a program needn't handle non-finite values.
Results may differ from the reference program's by a relative error of at most 0.028.
Values may be sent and summed in bfloat16 or wider, within the bound.
No kernel may reach another device: no remote copies, remote signals or barrier semaphores. Data moves between devices by JAX's collectives and lax.ppermute only.
A program may use at most 64 MiB of HBM per device.

```python
import math
import jax
import jax.numpy as jnp
from jax import lax

D = 1152
H = 8
P_SIZE = 64
ROWS = 8
COLS = 16
HW = 576
QBD = 2
NRB = 16
NCB = 64
HT = 128
WT = 512
N_LAT = 16
N_LON = 32


def drawn_weight(key):
    return jax.random.truncated_normal(key, -6.0, 6.0, (D, HW), jnp.float32) / math.sqrt(D)


def draw_w_query(key, part):
    key = jax.random.fold_in(key, 21)
    weight = drawn_weight(key)
    result = weight
    return jnp.clip(result, -1.0, 1.0).astype(jnp.bfloat16)


def draw_w_key(key, part):
    key = jax.random.fold_in(key, 22)
    weight = drawn_weight(key)
    result = weight
    return jnp.clip(result, -1.0, 1.0).astype(jnp.bfloat16)


def draw_tokens(key, part):
    key = jax.random.fold_in(key, 23)
    subkeys = jax.random.split(key, 1)
    noise_field = jax.random.truncated_normal(subkeys[0], -6.0, 6.0, (HT, WT, D), jnp.float32)
    result = noise_field
    return jnp.clip(result, -8.0, 8.0).astype(jnp.bfloat16)


def draw_block_mask(key, part):
    key = jax.random.fold_in(key, 11)
    radius = jax.random.randint(key, (NRB, NCB, 3, 1), 0, QBD + 1)
    offsets = jnp.arange(2 * QBD + 1, dtype=jnp.int32)[None, None, None, :] - QBD
    live_runs = jnp.abs(offsets) <= radius
    band_rows = jnp.arange(NRB, dtype=jnp.int32)[:, None, None, None] + jnp.arange(3, dtype=jnp.int32)[None, None, :, None] - 1
    inside = (band_rows >= 0) & (band_rows < NRB)
    return jnp.where(live_runs & inside, 1, 0).astype(jnp.int32)


def set_ends(values, own_key, smallest, largest):
    spot = [jax.random.randint(jax.random.fold_in(own_key, axis), (), 0, length) for axis, length in enumerate(values.shape)]
    main_axis = values.shape.index(max(values.shape))
    neighbour = spot[:main_axis] + [(spot[main_axis] + 1) % values.shape[main_axis]] + spot[main_axis + 1:]
    return values.at[tuple(spot)].set(smallest).at[tuple(neighbour)].set(largest)


def block_levels(key, extent, shards, low, top_value):
    loudness = 1.0
    for position, shards_of in shards:
        heights = jax.random.uniform(jax.random.fold_in(jax.random.fold_in(key, 6), position), (shards_of,), jnp.float32, low / len(shards), top_value / len(shards))
        loudness = loudness * jnp.repeat(jnp.exp(heights), extent[position] // shards_of).reshape((-1,) + (1,) * (len(extent) - 1 - position))
    return loudness


def scatter_about(rng, dims, scale, reach, cuts=(), kind=jnp.bfloat16):
    values = jax.random.normal(rng, dims, jnp.float32) * scale
    if len(cuts) > 0:
        values = block_levels(rng, dims, cuts, -0.22, 0.18) * values
    return jnp.clip(values, min=-reach, max=reach).astype(kind)


def setup_inputs(seed: int = 0) -> dict:
    seeds = jax.random.split(jax.random.key(seed), 11)
    tokens = draw_tokens(jax.random.fold_in(seeds[10], 71), 0)
    gain = jnp.clip(1.0 + 0.15 * jax.random.normal(seeds[1], (D,), jnp.float32), 0.25, 1.75)
    w_query = draw_w_query(jax.random.fold_in(seeds[10], 71), 0)
    w_key = draw_w_key(jax.random.fold_in(seeds[10], 71), 0)
    w_value = scatter_about(seeds[4], (D, HW), D ** -0.5, 0.1875, ((0, 16),))
    w_out = scatter_about(seeds[5], (HW, D), HW ** -0.5, 0.25, ((0, 16),))
    w_pixel = scatter_about(seeds[6], (D, 3 * P_SIZE), D ** -0.5, 0.1875)
    measured = scatter_about(seeds[7], (HT, WT, P_SIZE), 1.0, 6.0, ((0, 16), (1, 32)), jnp.float32)
    filter_color = set_ends(jax.random.randint(seeds[8], (HT, WT, P_SIZE), 0, 3), jax.random.fold_in(seeds[8], 1), 0, 2).astype(jnp.int32)
    block_mask = draw_block_mask(jax.random.fold_in(seeds[10], 71), 0)
    return dict(tokens=tokens, gain=gain, w_query=w_query, w_key=w_key, w_value=w_value, w_out=w_out, w_pixel=w_pixel, measured=measured, filter_color=filter_color, block_mask=block_mask)


def layer_norm(values, gain):
    center = values - lax.optimization_barrier(jnp.mean(values, axis=-1, keepdims=True))
    spread = lax.optimization_barrier(jnp.mean(center * center, axis=-1, keepdims=True))
    return center * lax.rsqrt(spread + 1e-06) * gain

def token_mask(blocks, row_count, col_count):
    groups = col_count // 8
    spanned = 2 * groups + 1
    placed = jnp.zeros((groups, 3, 3 * groups), jnp.int32)
    for column in range(groups):
        placed = placed.at[column, :, column:column + spanned].set(blocks[column])
    placed = jnp.repeat(jnp.repeat(jnp.repeat(placed, 8, axis=0), 8, axis=1), 8, axis=2)
    placed = jnp.broadcast_to(placed[None], (row_count, col_count, 3 * row_count, 3 * col_count))
    return placed.reshape(row_count * col_count, 9 * row_count * col_count) > 0

def tile_terms(queries, keys, values, inputs, measured, filter_color, allowed, w_out, w_pixel):
    token_count = queries.shape[0]
    inner_width = queries.shape[1]
    head_dim = inner_width // H
    factor = head_dim ** (-0.5)
    query_h = queries.astype(jnp.float32).reshape(token_count, H, head_dim)
    key_h = keys.astype(jnp.float32).reshape(-1, H, head_dim)
    value_h = values.astype(jnp.float32).reshape(-1, H, head_dim)
    scores = jnp.einsum('qhd,khd->hqk', query_h, key_h) * factor
    scores = jnp.where(allowed[None], scores, -1e+30)
    row_peak = lax.optimization_barrier(jnp.max(scores, axis=2, keepdims=True))
    row_total = lax.optimization_barrier(jnp.sum(jnp.where(allowed[None], jnp.exp(scores - row_peak), 0.0), axis=2, keepdims=True))
    logsum = row_peak + jnp.log(row_total)
    probability = jnp.where(allowed[None], jnp.exp(scores - logsum), 0.0)
    probability_low = probability.astype(jnp.bfloat16)
    attended = jnp.einsum('hqk,khd->qhd', probability_low.astype(jnp.float32), value_h)
    attended = attended.reshape(token_count, inner_width).astype(jnp.bfloat16)
    denoised = (inputs.astype(jnp.float32) + jnp.dot(attended, w_out, preferred_element_type=jnp.float32)).astype(jnp.bfloat16)
    colors = jnp.dot(denoised, w_pixel, preferred_element_type=jnp.float32).reshape(token_count, 3, -1)
    picked = filter_color[:, None, :] == jnp.arange(3, dtype=jnp.int32)[None, :, None]
    predicted = lax.optimization_barrier(jnp.sum(jnp.where(picked, colors, 0.0), axis=1))
    misfit = predicted - measured
    spread_back = jnp.where(picked, misfit[:, None, :], 0.0).astype(jnp.bfloat16).reshape(token_count, -1)
    outer_grad = jnp.dot(spread_back, w_pixel.T, preferred_element_type=jnp.float32)
    upstream = jnp.dot(outer_grad.astype(jnp.bfloat16), w_out.T, preferred_element_type=jnp.float32).astype(jnp.bfloat16)
    up_h = upstream.astype(jnp.float32).reshape(token_count, H, head_dim)
    att_h = attended.astype(jnp.float32).reshape(token_count, H, head_dim)
    inner_sum = jnp.einsum('qhd,qhd->hq', up_h, att_h)
    dprob = jnp.einsum('qhd,khd->hqk', up_h, value_h)
    dscore = (probability * (dprob - inner_sum[:, :, None]) * factor).astype(jnp.bfloat16)
    dscore_f = dscore.astype(jnp.float32)
    grad_query = jnp.einsum('hqk,khd->qhd', dscore_f, key_h).reshape(token_count, inner_width).astype(jnp.bfloat16)
    grad_key = jnp.einsum('hqk,qhd->khd', dscore_f, query_h).reshape(-1, inner_width).astype(jnp.bfloat16)
    grad_value = jnp.einsum('hqk,qhd->khd', probability_low.astype(jnp.float32), up_h).reshape(-1, inner_width).astype(jnp.bfloat16)
    return (denoised, outer_grad, grad_query, grad_key, grad_value)

def reference(tokens, gain, w_query, w_key, w_value, w_out, w_pixel, measured, filter_color, block_mask):
    height, breadth, model_width = tokens.shape
    inner_width = w_query.shape[1]
    flat_tokens = tokens.astype(jnp.float32).reshape(-1, model_width)
    normed, norm_back = jax.vjp(lambda entries: layer_norm(entries, gain), flat_tokens)
    hidden = normed.astype(jnp.bfloat16)

    def project(weight):
        return jnp.dot(hidden, weight, preferred_element_type=jnp.float32).astype(jnp.bfloat16).reshape(height, breadth, inner_width)
    queries = project(w_query)
    keys = project(w_key)
    values = project(w_value)

    def widen_cycle(plane):
        plane = jnp.concatenate([plane[:, breadth - COLS:], plane, plane[:, :COLS]], axis=1)
        return jnp.pad(plane, ((ROWS, ROWS), (0, 0), (0, 0)))
    key_pad = widen_cycle(keys)
    value_pad = widen_cycle(values)
    groups = COLS // 8

    def tile_step(carry, tile_index):
        key_acc, value_acc = carry
        band_index = tile_index // N_LON
        cycle_index = tile_index % N_LON
        row_start = band_index * ROWS
        col_start = cycle_index * COLS
        root = jnp.int32(0)

        def cut_out(plane, size_rows, size_cols):
            piece = lax.dynamic_slice(plane, (row_start, col_start, root), (size_rows, size_cols, plane.shape[2]))
            return piece.reshape(size_rows * size_cols, plane.shape[2])
        blocks = lax.dynamic_slice(block_mask, (band_index, cycle_index * groups, root, root), (1, groups, 3, 2 * groups + 1))[0]
        allowed = token_mask(blocks, ROWS, COLS)
        results = tile_terms(cut_out(queries, ROWS, COLS), cut_out(key_pad, 3 * ROWS, 3 * COLS), cut_out(value_pad, 3 * ROWS, 3 * COLS), cut_out(tokens, ROWS, COLS), cut_out(measured, ROWS, COLS), cut_out(filter_color, ROWS, COLS), allowed, w_out, w_pixel)
        denoised, outer_grad, grad_query, grad_key, grad_value = results

        def accumulate(accumulated, gradient):
            shaped = gradient.astype(jnp.float32).reshape(3 * ROWS, 3 * COLS, inner_width)
            before = lax.dynamic_slice(accumulated, (row_start, col_start, root), shaped.shape)
            return lax.dynamic_update_slice(accumulated, before + shaped, (row_start, col_start, root))
        return ((accumulate(key_acc, grad_key), accumulate(value_acc, grad_value)), (denoised, outer_grad, grad_query))
    zeros_pad = jnp.zeros(key_pad.shape, jnp.float32)
    carried, stacked = lax.scan(tile_step, (zeros_pad, zeros_pad), jnp.arange(N_LAT * N_LON, dtype=jnp.int32))
    key_acc, value_acc = carried
    denoised, outer_grad, grad_query = stacked

    def regrid(tiles):
        return tiles.reshape(N_LAT, N_LON, ROWS, COLS, -1).transpose(0, 2, 1, 3, 4).reshape(height * breadth, -1)

    def fold_back(accumulated):
        middle = accumulated[ROWS:ROWS + height]
        core_part = middle[:, COLS:COLS + breadth]
        core_part = core_part.at[:, breadth - COLS:].add(middle[:, :COLS])
        core_part = core_part.at[:, :COLS].add(middle[:, COLS + breadth:])
        return core_part.reshape(-1, inner_width).astype(jnp.bfloat16)
    grad_key = fold_back(key_acc)
    grad_value = fold_back(value_acc)
    grad_hidden = jnp.dot(regrid(grad_query), w_query.T, preferred_element_type=jnp.float32)
    grad_hidden = grad_hidden + jnp.dot(grad_key, w_key.T, preferred_element_type=jnp.float32)
    grad_hidden = grad_hidden + jnp.dot(grad_value, w_value.T, preferred_element_type=jnp.float32)
    guidance = norm_back(grad_hidden)[0] + regrid(outer_grad)
    return (regrid(denoised).reshape(height, breadth, model_width), guidance.reshape(height, breadth, model_width))
```

```python
import functools

import jax
import jax.numpy as jnp
import numpy as np
from jax import lax
from jax.experimental import pallas as pl
from jax.experimental.pallas import tpu as pltpu
from jax.sharding import Mesh, PartitionSpec as P

H = 8
HD = 72
HW = 576
D = 1152
T = 128
QKV = 3 * HW
FACTOR = HD ** (-0.5)
SCALE2 = FACTOR * 1.4426950408889634
OFF = -1e30
BF = jnp.bfloat16
F32 = jnp.float32
VMEM = pl.BlockSpec(memory_space=pltpu.VMEM)
SMEM = pl.BlockSpec(memory_space=pltpu.SMEM)
ANY = pl.BlockSpec(memory_space=pl.ANY)
K0, V0, Q0 = 0, HW, 2 * HW
VB = 512


def params(limit=40):
    return pltpu.CompilerParams(vmem_limit_bytes=limit * 1024 * 1024)


def nt(left, right):
    return lax.dot_general(left, right, (((1,), (1,)), ((), ())), preferred_element_type=F32)


def nn(left, right):
    return jnp.dot(left, right, preferred_element_type=F32)


def window(first):
    return first // 128 * 128, -(-(first + HD) // 128) * 128


def head_only(x, first, start):
    lane = lax.broadcasted_iota(jnp.int32, x.shape, 1) + start
    return jnp.where((lane >= first) & (lane < first + HD), x, jnp.zeros_like(x))


def norm_parts(x):
    center = x - jnp.mean(x, axis=-1, keepdims=True)
    rstd = lax.rsqrt(jnp.mean(center * center, axis=-1, keepdims=True) + 1e-6)
    return center, rstd


def order_kernel(target_ref, order_ref):
    rows = lax.broadcasted_iota(jnp.int32, (D, D), 0)
    order_ref[...] = jnp.where(rows == target_ref[...], 1.0, 0.0).astype(BF)


def hidden_kernel(x_ref, gain_ref, order_ref, out_ref):
    for i in range(x_ref.shape[0] // T):
        center, rstd = norm_parts(x_ref[i * T : (i + 1) * T, :].astype(F32))
        hidden = (center * rstd * gain_ref[...]).astype(BF)
        out_ref[i * T : (i + 1) * T, :] = nn(hidden, order_ref[...]).astype(BF)


def forward_kernel(
    core_ref, blocks_ref, hw_ref, hc_ref, he_ref, u0, m1, m2, m3, t1, t2, t3, mh, th, wout_ref, wpix_ref,
    x_ref, meas_ref, filt_ref,
    w_ref, win_ref, e_ref, den_ref, og_ref, pack_ref, stat_ref,
    wo_ref, bias_ref, att_ref, sems,
):
    core = core_ref[0]
    copies = [
        pltpu.make_async_copy(src, w_ref.at[pl.ds(144 * i, 144)], sems.at[i])
        for i, src in enumerate((u0, m1, m2, m3, t1, t2, t3))
    ]
    copies.append(pltpu.make_async_copy(mh, w_ref.at[pl.ds(1008, 80)], sems.at[7]))
    first = pl.multiple_of(16 * (1 - core), 16)
    copies.append(pltpu.make_async_copy(th.at[pl.ds(first, 64)], w_ref.at[pl.ds(1088, 64)], sems.at[8]))
    copies.append(pltpu.make_async_copy(wout_ref, wo_ref.at[pl.ds(64, HW)], sems.at[9]))
    for c in copies:
        c.start()
    wo_ref[0:64, :] = jnp.zeros((64, D), BF)
    att_ref[...] = jnp.zeros_like(att_ref)

    qc = (lax.broadcasted_iota(jnp.int32, (T, T), 0) & 8) > 0
    kc = (lax.broadcasted_iota(jnp.int32, (T, T), 1) & 8) > 0

    def allowed(c, r, w):
        return blocks_ref[(c * 3 + r) * 5 + w - c].astype(F32) if 0 <= w - c < 5 else jnp.float32(0.0)

    lane_c = (lax.broadcasted_iota(jnp.int32, (1, T), 1) & 8) > 0
    rows = []
    for r in range(3):
        for w in range(6):
            rows.append(jnp.where(lane_c, allowed(1, r, w), allowed(0, r, w)))
    for t in range(3):
        for r in range(3):
            seen = jnp.where(
                qc,
                jnp.where(kc, allowed(1, r, 2 * t + 1), allowed(1, r, 2 * t)),
                jnp.where(kc, allowed(0, r, 2 * t + 1), allowed(0, r, 2 * t)),
            )
            j = 3 * t + r
            bias_ref[:, j * T : (j + 1) * T] = (1.0 - seen) * OFF
    for c in copies[:9]:
        c.wait()
    for g, h_ref in enumerate((hw_ref, hc_ref, he_ref)):
        for part in range(3):
            s = slice(part * T, (part + 1) * T)
            win_ref[(g * 3 + part) * T : (g * 3 + part + 1) * T, :] = nn(h_ref[s, :], w_ref[...]).astype(BF)

    own = slice(4 * T, 5 * T)
    lanes = lax.broadcasted_iota(jnp.int32, (T, T), 1)
    stats = jnp.zeros((T, T), F32)
    for e in range(H):
        a, b = window(K0 + HD * e)
        q = head_only(win_ref[own, Q0 + a : Q0 + b], HD * e, a) if Q0 + b <= QKV else head_only(
            jnp.concatenate([win_ref[own, Q0 + a : QKV], jnp.zeros((T, Q0 + b - QKV), BF)], axis=1), HD * e, a)
        s = nt(q, win_ref[:, a:b]) * SCALE2 + bias_ref[...]
        peak = jnp.max(s, axis=1, keepdims=True)
        p = jnp.exp2(s - peak)
        total = jnp.sum(p, axis=1, keepdims=True)
        low = p.astype(BF)
        e_ref[e * T : (e + 1) * T, :] = low
        inv = 1.0 / total
        stats = jnp.where(lanes == e, peak + jnp.log2(total), stats)
        stats = jnp.where(lanes == 16 + e, inv, stats)
        a, b = window(V0 + HD * e)
        o = nn(low, win_ref[:, a:b]) * inv
        att_ref[:, a - VB : b - VB] += head_only(o, V0 + HD * e, a)
    copies[9].wait()
    att = att_ref[...].astype(BF)
    den = (x_ref[...].astype(F32) + nn(att, wo_ref[...])).astype(BF)
    den_ref[...] = den
    colors = nn(den, wpix_ref[...])
    filt = filt_ref[...]
    misfit = -meas_ref[...]
    for c in range(3):
        misfit = misfit + jnp.where(filt == c, colors[:, 64 * c : 64 * c + 64], 0.0)
    spread = jnp.concatenate([jnp.where(filt == c, misfit, 0.0) for c in range(3)], axis=1).astype(BF)
    og = nt(spread, wpix_ref[...])
    og_ref[...] = og
    up = nt(og.astype(BF), wo_ref[...]).astype(BF)
    pack_ref[0:T, :] = up
    prod = up.astype(F32) * att.astype(F32)
    for e in range(H):
        a, b = window(V0 + HD * e)
        inner = jnp.sum(head_only(prod[:, a - VB : b - VB], V0 + HD * e, a), axis=1, keepdims=True)
        stats = jnp.where(lanes == 8 + e, inner, stats)
    stat_ref[...] = stats
    turned = stats.T[0:16, :]
    high = turned.astype(BF)
    rest = turned - high.astype(F32)
    mid = rest.astype(BF)
    low = (rest - mid.astype(F32)).astype(BF)
    pack_ref[T : T + 16, :] = jnp.concatenate(
        [
            high,
            mid,
            low,
            jnp.concatenate(rows[:16], axis=0).astype(BF),
            jnp.concatenate(rows[16:] + [jnp.zeros((14, T), F32)], axis=0).astype(BF),
        ],
        axis=1,
    )


def query_kernel(win_ref, e_ref, up_ref, stat_ref, gq_ref, acc_ref):
    acc_ref[...] = jnp.zeros_like(acc_ref)
    for e in range(H):
        a, b = window(V0 + HD * e)
        up = head_only(up_ref[0:T, a - VB : b - VB], V0 + HD * e, a)
        dprob = nt(up, win_ref[:, a:b])
        p = e_ref[e * T : (e + 1) * T, :].astype(F32)
        ds = (p * (dprob - stat_ref[:, 8 + e : 9 + e])).astype(BF)
        a, b = window(K0 + HD * e)
        dq = nn(ds, win_ref[:, a:b]) * (stat_ref[:, 16 + e : 17 + e] * FACTOR)
        acc_ref[:, a:b] += head_only(dq, HD * e, a)
    gq_ref[...] = acc_ref[:, 0:HW].astype(BF)


def key_side(win_ref, groups, gk_ref, gv_ref):
    own = slice(4 * T, 5 * T)
    kc = (lax.broadcasted_iota(jnp.int32, (T, T), 0) & 8) > 0
    for t, pack_ref in groups:
        bias, stats, ups = [], [], []
        for r in range(3):
            base = r * 144
            ups.append(pack_ref[base : base + T, :])
            extra = pack_ref[base + T : base + T + 16, :].astype(F32)
            stats.append(extra[:, 0:128] + extra[:, 128:256] + extra[:, 256:384])
            seen = []
            for w in range(2):
                i = (2 - r) * 6 + (2 - t) * 2 + w
                seen.append(extra[i : i + 1, 384:512] if i < 16 else extra[i - 16 : i - 15, 512:640])
            bias.append((1.0 - jnp.where(kc, seen[1], seen[0])) * OFF)
        bias = jnp.concatenate(bias, axis=1)
        stats = jnp.concatenate(stats, axis=1)
        ups = jnp.concatenate(ups, axis=0)
        q_rows = slice(t * 3 * T, (t + 1) * 3 * T)
        for e in range(H):
            a, b = window(K0 + HD * e)
            if Q0 + b <= QKV:
                q = win_ref[q_rows, Q0 + a : Q0 + b]
            else:
                q = jnp.concatenate([win_ref[q_rows, Q0 + a : QKV], jnp.zeros((3 * T, Q0 + b - QKV), BF)], axis=1)
            k = head_only(win_ref[own, a:b], HD * e, a)
            s = nt(k, q) * SCALE2 + bias
            p = jnp.exp2(s - stats[e : e + 1, :])
            c, d = window(V0 + HD * e)
            v = head_only(win_ref[own, c:d], V0 + HD * e, c)
            up = ups[:, c - VB : d - VB]
            ds = (p * (nt(v, up) - stats[8 + e : 9 + e, :])).astype(BF)
            gk_ref[:, a:b] += head_only(nn(ds, q), HD * e, a)
            gv_ref[:, c - VB : d - VB] += head_only(nn(p.astype(BF), up), V0 + HD * e, c)


def key_centre_kernel(win_ref, pack_ref, gk_ref, gv_ref):
    gk_ref[...] = jnp.zeros_like(gk_ref)
    gv_ref[...] = jnp.zeros_like(gv_ref)
    key_side(win_ref, ((1, pack_ref),), gk_ref, gv_ref)


def finish_kernel(
    win_ref, packw_ref, packe_ref, gk0_ref, gv0_ref, gq_ref, w_ref, order_ref, x_ref, gain_ref, og_ref,
    out_ref, gk_ref, gv_ref,
):
    gk_ref[...] = gk0_ref[...]
    gv_ref[...] = gv0_ref[...]
    key_side(win_ref, ((0, packw_ref), (2, packe_ref)), gk_ref, gv_ref)
    gk = (gk_ref[:, 0:HW] * FACTOR).astype(BF)
    gv = gv_ref[:, 64:640].astype(BF)
    grads = jnp.concatenate([gk, gv, gq_ref[...]], axis=1)
    moved = nt(grads, w_ref[...])
    high = moved.astype(BF)
    rest = moved - high.astype(F32)
    mid = rest.astype(BF)
    low = (rest - mid.astype(F32)).astype(BF)
    order = order_ref[...]
    grad = (nt(high, order) + nt(mid, order) + nt(low, order)) * gain_ref[...]
    center, rstd = norm_parts(x_ref[...].astype(F32))
    xhat = center * rstd
    mean_g = jnp.mean(grad, axis=-1, keepdims=True)
    mean_gx = jnp.mean(grad * xhat, axis=-1, keepdims=True)
    out_ref[...] = rstd * (grad - mean_g - xhat * mean_gx) + og_ref[...]


def shaped(shape, dtype=BF):
    return jax.ShapeDtypeStruct(shape, dtype)


def weight_targets(z, yh, core):
    place = np.arange(D)
    block, row = place // 144, place % 144
    step = np.select([block == 7], [4], np.where(block > 3, block - 3, block))
    sign = np.where(block > 3, 1, -1)
    last0 = row
    last1 = np.where(row < 80, row + 64, row - 80)
    zs = jnp.where(core == 0, z + jnp.asarray(sign * step), z - jnp.asarray(sign * step)) & 7
    inside = jnp.where(core == 0, jnp.asarray(last0), jnp.asarray(np.where(block == 7, last1, row)))
    other = inside >= 72
    ys = jnp.where(other, 1 - yh, yh)
    return ((ys * 8 + zs) * 72 + inside - 72 * other.astype(jnp.int32)).astype(jnp.int32).reshape(1, D)


def on_device(tokens, gain, w_query, w_key, w_value, w_out, w_pixel, measured, filter_color, block_mask):
    yh, z, core = lax.axis_index("yh"), lax.axis_index("z"), lax.axis_index("core")
    x = tokens.reshape(T, D)
    gain = gain.reshape(1, D)
    ring = [(2 * i, 2 * ((i + 1) % 8)) for i in range(8)] + [(2 * i + 1, 2 * ((i + 7) % 8) + 1) for i in range(8)]
    south = [(i, i + 1) for i in range(15)]
    north = [(j, i) for i, j in south]
    east = [(i, (i + 1) % 32) for i in range(32)]
    west = [(j, i) for i, j in east]
    lat, lon = ("yh", "z"), ("yl", "x", "core")

    def swap(v):
        return lax.ppermute(v, "core", [(0, 1), (1, 0)])

    def step(v):
        return lax.ppermute(v, ("z", "core"), ring)

    def columns(own):
        before = lax.ppermute(own, lat, south)
        after = lax.ppermute(own, lat, north)
        return jnp.concatenate([before, own, after], axis=0)

    def sides(column):
        return lax.ppermute(column, lon, east), lax.ppermute(column, lon, west)

    mine = jnp.concatenate([w_key, w_value, w_query], axis=1)
    other = lax.ppermute(mine, "yh", [(0, 1), (1, 0)])
    out_other = lax.ppermute(w_out, "yh", [(0, 1), (1, 0)])
    both = jnp.concatenate([mine, other], axis=0)
    out_both = jnp.stack([jnp.where(yh == 0, w_out, out_other), jnp.where(yh == 0, out_other, w_out)])
    full_out = lax.all_gather(out_both, "z", axis=1).reshape(HW, D)
    m1 = step(both)
    t1 = swap(m1)
    m2 = step(m1)
    t2 = swap(m2)
    m3 = step(m2)
    t3 = swap(m3)
    mh = step(jnp.where(core == 0, m3[0:80], m3[64:144]))
    th = swap(mh)

    column = columns(x)
    from_west, from_east = sides(column)
    order = pl.pallas_call(
        order_kernel, out_shape=shaped((D, D)), in_specs=[VMEM], out_specs=VMEM, compiler_params=params(),
    )(weight_targets(z, yh, core))

    def hidden(v):
        return pl.pallas_call(
            hidden_kernel, out_shape=shaped((3 * T, D)), in_specs=[VMEM] * 3, out_specs=VMEM, compiler_params=params(),
        )(v, gain, order)

    hw, hc, he = hidden(from_west), hidden(column), hidden(from_east)
    w, win, e, den, og, pack, stat = pl.pallas_call(
        forward_kernel,
        out_shape=(
            shaped((D, QKV)), shaped((9 * T, QKV)), shaped((H * T, 9 * T)), shaped((T, D)), shaped((T, D), F32),
            shaped((144, 640)), shaped((T, T), F32),
        ),
        in_specs=[SMEM, SMEM] + [VMEM] * 3 + [ANY] * 10 + [VMEM] * 4,
        out_specs=(VMEM,) * 7,
        scratch_shapes=[
            pltpu.VMEM((640, D), BF), pltpu.VMEM((T, 9 * T), F32), pltpu.VMEM((T, 640), F32),
            pltpu.SemaphoreType.DMA((10,)),
        ],
        compiler_params=params(),
    )(
        core.reshape(1).astype(jnp.int32), block_mask.reshape(30), hw, hc, he, both, m1, m2, m3, t1, t2, t3, mh, th,
        full_out, w_pixel, x, measured.reshape(T, 64), filter_color.reshape(T, 64),
    )
    packs = columns(pack)
    gq = pl.pallas_call(
        query_kernel, out_shape=shaped((T, HW)), in_specs=[VMEM] * 4, out_specs=VMEM,
        scratch_shapes=[pltpu.VMEM((T, 640), F32)], compiler_params=params(),
        cost_estimate=pl.CostEstimate(flops=8_000_000_000, bytes_accessed=6_000_000, transcendentals=0),
    )(win, e, pack, stat)
    packs_west, packs_east = sides(packs)
    gk, gv = pl.pallas_call(
        key_centre_kernel, out_shape=(shaped((T, 640), F32),) * 2, in_specs=[VMEM] * 2, out_specs=(VMEM,) * 2,
        compiler_params=params(),
        cost_estimate=pl.CostEstimate(flops=8_000_000_000, bytes_accessed=6_000_000, transcendentals=0),
    )(win, packs)
    guidance = pl.pallas_call(
        finish_kernel, out_shape=shaped((T, D), F32), in_specs=[VMEM] * 11, out_specs=VMEM,
        scratch_shapes=[pltpu.VMEM((T, 640), F32)] * 2, compiler_params=params(),
    )(win, packs_west, packs_east, gk, gv, gq, w, order, x, gain, og)
    return den.reshape(tokens.shape), guidance.reshape(tokens.shape)


def solution(mesh):
    split = Mesh(mesh.devices.reshape(2, 8, 4, 4, 2), ("yh", "z", "yl", "x", "core"))
    lat, lon = ("yh", "z"), ("yl", "x", "core")
    return jax.shard_map(
        on_device,
        mesh=split,
        in_specs=(
            P(lat, lon, None), P(), P(lat, None), P(lat, None), P(lat, None), P(lat, None), P(),
            P(lat, lon, None), P(lat, lon, None), P(lat, lon, None, None),
        ),
        out_specs=(P(lat, lon, None), P(lat, lon, None)),
        check_vma=False,
    )
```

```python
import functools

import jax
import jax.numpy as jnp
import numpy as np
from jax import lax
from jax.experimental import pallas as pl
from jax.experimental.pallas import tpu as pltpu
from jax.sharding import Mesh, PartitionSpec as P

H = 8
HD = 72
HW = 576
D = 1152
T = 128
QKV = 3 * HW
FACTOR = HD ** (-0.5)
SCALE2 = FACTOR * 1.4426950408889634
OFF = -1e30
BF = jnp.bfloat16
F32 = jnp.float32
VMEM = pl.BlockSpec(memory_space=pltpu.VMEM)
SMEM = pl.BlockSpec(memory_space=pltpu.SMEM)
ANY = pl.BlockSpec(memory_space=pl.ANY)
K0, V0, Q0 = 0, HW, 2 * HW
VB = 512


def params(limit=40):
    return pltpu.CompilerParams(vmem_limit_bytes=limit * 1024 * 1024)


def nt(left, right):
    return lax.dot_general(left, right, (((1,), (1,)), ((), ())), preferred_element_type=F32)


def nn(left, right):
    return jnp.dot(left, right, preferred_element_type=F32)


def window(first):
    return first // 128 * 128, -(-(first + HD) // 128) * 128


def head_only(x, first, start):
    lane = lax.broadcasted_iota(jnp.int32, x.shape, 1) + start
    return jnp.where((lane >= first) & (lane < first + HD), x, jnp.zeros_like(x))


def norm_parts(x):
    center = x - jnp.mean(x, axis=-1, keepdims=True)
    rstd = lax.rsqrt(jnp.mean(center * center, axis=-1, keepdims=True) + 1e-6)
    return center, rstd


def order_kernel(target_ref, order_ref):
    rows = lax.broadcasted_iota(jnp.int32, (D, D), 0)
    order_ref[...] = jnp.where(rows == target_ref[...], 1.0, 0.0).astype(BF)


def hidden_kernel(x_ref, gain_ref, order_ref, out_ref):
    for i in range(x_ref.shape[0] // T):
        center, rstd = norm_parts(x_ref[i * T : (i + 1) * T, :].astype(F32))
        hidden = (center * rstd * gain_ref[...]).astype(BF)
        out_ref[i * T : (i + 1) * T, :] = nn(hidden, order_ref[...]).astype(BF)


def collect(blocks, w_ref, sems):
    copies = [
        pltpu.make_async_copy(src, w_ref.at[pl.ds(144 * i, 144)], sems.at[i]) for i, src in enumerate(blocks)
    ]
    for c in copies:
        c.start()
    return copies


def forward_kernel(
    blocks_ref, hw_ref, hc_ref, he_ref, b0, b1, b2, b3, b4, b5, b6, b7,
    win_ref, e_ref, att_ref, stat_ref, rows_ref,
    w_ref, bias_ref, acc_ref, sems,
):
    copies = collect((b0, b1, b2, b3, b4, b5, b6, b7), w_ref, sems)
    acc_ref[...] = jnp.zeros_like(acc_ref)

    qc = (lax.broadcasted_iota(jnp.int32, (T, T), 0) & 8) > 0
    kc = (lax.broadcasted_iota(jnp.int32, (T, T), 1) & 8) > 0

    def allowed(c, r, w):
        return blocks_ref[(c * 3 + r) * 5 + w - c].astype(F32) if 0 <= w - c < 5 else jnp.float32(0.0)

    lane_c = (lax.broadcasted_iota(jnp.int32, (1, T), 1) & 8) > 0
    rows = []
    for r in range(3):
        for w in range(6):
            rows.append(jnp.where(lane_c, allowed(1, r, w), allowed(0, r, w)))
    rows_ref[...] = jnp.concatenate(rows + [jnp.zeros((14, T), F32)], axis=0)
    for t in range(3):
        for r in range(3):
            seen = jnp.where(
                qc,
                jnp.where(kc, allowed(1, r, 2 * t + 1), allowed(1, r, 2 * t)),
                jnp.where(kc, allowed(0, r, 2 * t + 1), allowed(0, r, 2 * t)),
            )
            j = 3 * t + r
            bias_ref[:, j * T : (j + 1) * T] = (1.0 - seen) * OFF
    for c in copies:
        c.wait()
    for g, h_ref in enumerate((hw_ref, hc_ref, he_ref)):
        for part in range(3):
            s = slice(part * T, (part + 1) * T)
            win_ref[(g * 3 + part) * T : (g * 3 + part + 1) * T, :] = nn(h_ref[s, :], w_ref[...]).astype(BF)

    own = slice(4 * T, 5 * T)
    lanes = lax.broadcasted_iota(jnp.int32, (T, T), 1)
    stats = jnp.zeros((T, T), F32)
    for e in range(H):
        a, b = window(K0 + HD * e)
        q = head_only(win_ref[own, Q0 + a : Q0 + b], HD * e, a) if Q0 + b <= QKV else head_only(
            jnp.concatenate([win_ref[own, Q0 + a : QKV], jnp.zeros((T, Q0 + b - QKV), BF)], axis=1), HD * e, a)
        s = nt(q, win_ref[:, a:b]) * SCALE2 + bias_ref[...]
        peak = jnp.max(s, axis=1, keepdims=True)
        p = jnp.exp2(s - peak)
        total = jnp.sum(p, axis=1, keepdims=True)
        low = p.astype(BF)
        e_ref[e * T : (e + 1) * T, :] = low
        inv = 1.0 / total
        stats = jnp.where(lanes == e, peak + jnp.log2(total), stats)
        stats = jnp.where(lanes == 16 + e, inv, stats)
        a, b = window(V0 + HD * e)
        o = nn(low, win_ref[:, a:b]) * inv
        acc_ref[:, a - VB : b - VB] += head_only(o, V0 + HD * e, a)
    att_ref[...] = acc_ref[...].astype(BF)
    stat_ref[...] = stats


def pixel_kernel(
    att_ref, stat0_ref, rows_ref, place_ref, wout_ref, wpix_ref, x_ref, meas_ref, filt_ref,
    den_ref, og_ref, pack_ref, stat_ref,
):
    lane_of = lax.broadcasted_iota(jnp.int32, (640, HW), 0)
    order = jnp.where(lane_of == place_ref[...], 1.0, 0.0).astype(BF)
    att = att_ref[...]
    den = (x_ref[...].astype(F32) + nn(nn(att, order).astype(BF), wout_ref[...])).astype(BF)
    den_ref[...] = den
    colors = nt(den, wpix_ref[...])
    filt = filt_ref[...]
    misfit = -meas_ref[...]
    for c in range(3):
        misfit = misfit + jnp.where(filt == c, colors[:, 64 * c : 64 * c + 64], 0.0)
    spread = jnp.concatenate([jnp.where(filt == c, misfit, 0.0) for c in range(3)], axis=1).astype(BF)
    og = nn(spread, wpix_ref[...])
    og_ref[...] = og
    up = nt(nt(og.astype(BF), wout_ref[...]).astype(BF), order).astype(BF)
    pack_ref[0:T, :] = up
    prod = up.astype(F32) * att.astype(F32)
    lanes = lax.broadcasted_iota(jnp.int32, (T, T), 1)
    stats = stat0_ref[...]
    for e in range(H):
        a, b = window(V0 + HD * e)
        inner = jnp.sum(head_only(prod[:, a - VB : b - VB], V0 + HD * e, a), axis=1, keepdims=True)
        stats = jnp.where(lanes == 8 + e, inner, stats)
    stat_ref[...] = stats
    turned = stats.T[0:16, :]
    high = turned.astype(BF)
    rest = turned - high.astype(F32)
    mid = rest.astype(BF)
    low = (rest - mid.astype(F32)).astype(BF)
    pack_ref[T : T + 16, :] = jnp.concatenate(
        [high, mid, low, rows_ref[0:16, :].astype(BF), rows_ref[16:32, :].astype(BF)], axis=1
    )


def query_kernel(win_ref, e_ref, up_ref, stat_ref, gq_ref, acc_ref):
    acc_ref[...] = jnp.zeros_like(acc_ref)
    for e in range(H):
        a, b = window(V0 + HD * e)
        up = head_only(up_ref[0:T, a - VB : b - VB], V0 + HD * e, a)
        dprob = nt(up, win_ref[:, a:b])
        p = e_ref[e * T : (e + 1) * T, :].astype(F32)
        ds = (p * (dprob - stat_ref[:, 8 + e : 9 + e])).astype(BF)
        a, b = window(K0 + HD * e)
        dq = nn(ds, win_ref[:, a:b]) * (stat_ref[:, 16 + e : 17 + e] * FACTOR)
        acc_ref[:, a:b] += head_only(dq, HD * e, a)
    gq_ref[...] = acc_ref[:, 0:HW].astype(BF)


def key_side(win_ref, groups, gk_ref, gv_ref):
    own = slice(4 * T, 5 * T)
    kc = (lax.broadcasted_iota(jnp.int32, (T, T), 0) & 8) > 0
    for t, pack_ref in groups:
        bias, stats, ups = [], [], []
        for r in range(3):
            base = r * 144
            ups.append(pack_ref[base : base + T, :])
            extra = pack_ref[base + T : base + T + 16, :].astype(F32)
            stats.append(extra[:, 0:128] + extra[:, 128:256] + extra[:, 256:384])
            seen = []
            for w in range(2):
                i = (2 - r) * 6 + (2 - t) * 2 + w
                seen.append(extra[i : i + 1, 384:512] if i < 16 else extra[i - 16 : i - 15, 512:640])
            bias.append((1.0 - jnp.where(kc, seen[1], seen[0])) * OFF)
        bias = jnp.concatenate(bias, axis=1)
        stats = jnp.concatenate(stats, axis=1)
        ups = jnp.concatenate(ups, axis=0)
        q_rows = slice(t * 3 * T, (t + 1) * 3 * T)
        for e in range(H):
            a, b = window(K0 + HD * e)
            if Q0 + b <= QKV:
                q = win_ref[q_rows, Q0 + a : Q0 + b]
            else:
                q = jnp.concatenate([win_ref[q_rows, Q0 + a : QKV], jnp.zeros((3 * T, Q0 + b - QKV), BF)], axis=1)
            k = head_only(win_ref[own, a:b], HD * e, a)
            s = nt(k, q) * SCALE2 + bias
            p = jnp.exp2(s - stats[e : e + 1, :])
            c, d = window(V0 + HD * e)
            v = head_only(win_ref[own, c:d], V0 + HD * e, c)
            up = ups[:, c - VB : d - VB]
            ds = (p * (nt(v, up) - stats[8 + e : 9 + e, :])).astype(BF)
            gk_ref[:, a:b] += head_only(nn(ds, q), HD * e, a)
            gv_ref[:, c - VB : d - VB] += head_only(nn(p.astype(BF), up), V0 + HD * e, c)


def key_centre_kernel(win_ref, pack_ref, gk_ref, gv_ref):
    gk_ref[...] = jnp.zeros_like(gk_ref)
    gv_ref[...] = jnp.zeros_like(gv_ref)
    key_side(win_ref, ((1, pack_ref),), gk_ref, gv_ref)


def finish_kernel(
    win_ref, packw_ref, packe_ref, gk0_ref, gv0_ref, gq_ref, order_ref, x_ref, gain_ref, og_ref,
    b0, b1, b2, b3, b4, b5, b6, b7,
    out_ref, gk_ref, gv_ref, w_ref, sems,
):
    copies = collect((b0, b1, b2, b3, b4, b5, b6, b7), w_ref, sems)
    gk_ref[...] = gk0_ref[...]
    gv_ref[...] = gv0_ref[...]
    key_side(win_ref, ((0, packw_ref), (2, packe_ref)), gk_ref, gv_ref)
    gk = (gk_ref[:, 0:HW] * FACTOR).astype(BF)
    gv = gv_ref[:, 64:640].astype(BF)
    grads = jnp.concatenate([gk, gv, gq_ref[...]], axis=1)
    for c in copies:
        c.wait()
    moved = nt(grads, w_ref[...])
    high = moved.astype(BF)
    rest = moved - high.astype(F32)
    mid = rest.astype(BF)
    low = (rest - mid.astype(F32)).astype(BF)
    order = order_ref[...]
    grad = (nt(high, order) + nt(mid, order) + nt(low, order)) * gain_ref[...]
    center, rstd = norm_parts(x_ref[...].astype(F32))
    xhat = center * rstd
    mean_g = jnp.mean(grad, axis=-1, keepdims=True)
    mean_gx = jnp.mean(grad * xhat, axis=-1, keepdims=True)
    out_ref[...] = rstd * (grad - mean_g - xhat * mean_gx) + og_ref[...]


def shaped(shape, dtype=BF):
    return jax.ShapeDtypeStruct(shape, dtype)


def weight_targets(yh, z, x, core):
    place = np.arange(D)
    block, row = place // 144, place % 144
    second = row >= 72
    xs = (x + jnp.asarray(np.array([0, 3, 1, 2] * 2)[block])) & 3
    cs = core ^ jnp.asarray((block >= 4).astype(np.int32))
    last = xs == 3
    hops = jnp.where(last & second, 0, xs + 1)
    zs = (z + jnp.where(cs == 0, -hops, hops)) & 7
    other = jnp.logical_xor(second, last & (cs == 1)).astype(jnp.int32)
    return (((yh ^ other) * 8 + zs) * 72 + row % 72).astype(jnp.int32).reshape(1, D)


def device(yh, z, yl, x, core):
    return (((yh * 8 + z % 8) * 4 + yl) * 4 + x) * 2 + core


def fetch_routes():
    first, second, mirrored = [], [], []
    for yh in range(2):
        for z in range(8):
            for yl in range(4):
                for x in range(4):
                    for core in range(2):
                        me = device(yh, z, yl, x, core)
                        far = z + (x + 1 if core else -x - 1)
                        partner = device(1 - yh, z, 3 - yl, x, core)
                        mirrored.append((partner, me))
                        if x < 3:
                            first.append((device(yh, far, yl, x, core), me))
                            second.append((device(1 - yh, far, 3 - yl, x, core), me))
                        elif core == 0:
                            first.append((device(yh, far, yl, x, core), me))
                            second.append((partner, me))
                        else:
                            first.append((device(1 - yh, far, 3 - yl, x, core), me))
                            second.append((me, me))
    return first, second, mirrored


def on_device(tokens, gain, w_query, w_key, w_value, w_out, w_pixel, measured, filter_color, block_mask):
    yh, z, xi, core = (lax.axis_index(n) for n in ("yh", "z", "x", "core"))
    x = tokens.reshape(T, D)
    gain = gain.reshape(1, D)
    south = [(i, i + 1) for i in range(15)]
    north = [(j, i) for i, j in south]
    east = [(i, (i + 1) % 32) for i in range(32)]
    west = [(j, i) for i, j in east]
    lat, lon = ("yh", "z"), ("yl", "x", "core")
    first, second, mirrored = fetch_routes()

    def swap(v):
        return lax.ppermute(v, "core", [(0, 1), (1, 0)])

    def along(v, shift):
        return lax.ppermute(v, "x", [(i, (i + shift) % 4) for i in range(4)])

    def columns(own):
        before = lax.ppermute(own, lat, south)
        after = lax.ppermute(own, lat, north)
        return jnp.concatenate([before, own, after], axis=0)

    def sides(column):
        return lax.ppermute(column, lon, east), lax.ppermute(column, lon, west)

    out_other = lax.ppermute(w_out, lat + lon, mirrored)
    out_both = jnp.concatenate([jnp.where(yh == 0, w_out, out_other), jnp.where(yh == 0, out_other, w_out)], axis=0)
    full_out = lax.all_gather(out_both, "z", axis=0, tiled=True)
    place = np.arange(HW)
    place = (64 + (place // 36 % 2 * 8 + place // 72) * 36 + place % 36).astype(np.int32).reshape(1, HW)
    mine = jnp.concatenate([w_key, w_value, w_query], axis=1)
    fetched = jnp.concatenate(
        [lax.ppermute(mine, lat + lon, first), lax.ppermute(mine, lat + lon, second)], axis=0
    )
    right, left = along(fetched, 1), along(fetched, 3)
    across = jnp.concatenate([along(right[:72], 1), along(left[72:], 3)], axis=0)
    held = (fetched, right, left, across)
    blocks = held + tuple(swap(v) for v in held)

    column = columns(x)
    from_west, from_east = sides(column)
    order = pl.pallas_call(
        order_kernel, out_shape=shaped((D, D)), in_specs=[VMEM], out_specs=VMEM, compiler_params=params(16),
        cost_estimate=pl.CostEstimate(flops=2_000_000_000, bytes_accessed=3_000_000, transcendentals=0),
    )(weight_targets(yh, z, xi, core))

    def hidden(v):
        return pl.pallas_call(
            hidden_kernel, out_shape=shaped((3 * T, D)), in_specs=[VMEM] * 3, out_specs=VMEM,
            compiler_params=params(16),
            cost_estimate=pl.CostEstimate(flops=3_000_000_000, bytes_accessed=5_000_000, transcendentals=0),
        )(v, gain, order)

    hw, hc, he = hidden(from_west), hidden(column), hidden(from_east)
    win, e, att, stat0, rows = pl.pallas_call(
        forward_kernel,
        out_shape=(
            shaped((9 * T, QKV)), shaped((H * T, 9 * T)), shaped((T, 640)), shaped((T, T), F32), shaped((32, T), F32),
        ),
        in_specs=[SMEM] + [VMEM] * 3 + [ANY] * 8,
        out_specs=(VMEM,) * 5,
        scratch_shapes=[
            pltpu.VMEM((D, QKV), BF), pltpu.VMEM((T, 9 * T), F32), pltpu.VMEM((T, 640), F32),
            pltpu.SemaphoreType.DMA((8,)),
        ],
        compiler_params=params(28),
        cost_estimate=pl.CostEstimate(flops=12_000_000_000, bytes_accessed=8_000_000, transcendentals=1_000_000),
    )(block_mask.reshape(30), hw, hc, he, *blocks)
    den, og, pack, stat = pl.pallas_call(
        pixel_kernel,
        out_shape=(shaped((T, D)), shaped((T, D), F32), shaped((144, 640)), shaped((T, T), F32)),
        in_specs=[VMEM] * 9, out_specs=(VMEM,) * 4,
        compiler_params=params(16),
    )(att, stat0, rows, jnp.asarray(place), full_out, w_pixel.T, x, measured.reshape(T, 64), filter_color.reshape(T, 64))
    packs = columns(pack)
    gq = pl.pallas_call(
        query_kernel, out_shape=shaped((T, HW)), in_specs=[VMEM] * 4, out_specs=VMEM,
        scratch_shapes=[pltpu.VMEM((T, 640), F32)], compiler_params=params(16),
        cost_estimate=pl.CostEstimate(flops=4_000_000_000, bytes_accessed=6_000_000, transcendentals=0),
    )(win, e, pack, stat)
    packs_west, packs_east = sides(packs)
    gk, gv = pl.pallas_call(
        key_centre_kernel, out_shape=(shaped((T, 640), F32),) * 2, in_specs=[VMEM] * 2, out_specs=(VMEM,) * 2,
        compiler_params=params(16),
        cost_estimate=pl.CostEstimate(flops=4_000_000_000, bytes_accessed=6_000_000, transcendentals=0),
    )(win, packs)
    guidance = pl.pallas_call(
        finish_kernel, out_shape=shaped((T, D), F32), in_specs=[VMEM] * 10 + [ANY] * 8, out_specs=VMEM,
        scratch_shapes=[pltpu.VMEM((T, 640), F32)] * 2 + [pltpu.VMEM((D, QKV), BF), pltpu.SemaphoreType.DMA((8,))],
        compiler_params=params(24),
    )(win, packs_west, packs_east, gk, gv, gq, order, x, gain, og, *blocks)
    return den.reshape(tokens.shape), guidance.reshape(tokens.shape)


def solution(mesh):
    split = Mesh(mesh.devices.reshape(2, 8, 4, 4, 2), ("yh", "z", "yl", "x", "core"))
    lat, lon = ("yh", "z"), ("yl", "x", "core")
    return jax.shard_map(
        on_device,
        mesh=split,
        in_specs=(
            P(lat, lon, None), P(), P(lat, None), P(lat, None), P(lat, None), P(lat, None), P(),
            P(lat, lon, None), P(lat, lon, None), P(lat, lon, None, None),
        ),
        out_specs=(P(lat, lon, None), P(lat, lon, None)),
        check_vma=False,
    )
```

```python
import functools

import jax
import jax.numpy as jnp
import numpy as np
from jax import lax
from jax.experimental import pallas as pl
from jax.experimental.pallas import tpu as pltpu
from jax.sharding import Mesh, PartitionSpec as P

H = 8
HD = 72
HW = 576
D = 1152
T = 128
QKV = 3 * HW
FACTOR = HD ** (-0.5)
SCALE2 = FACTOR * 1.4426950408889634
OFF = -1e30
BF = jnp.bfloat16
F32 = jnp.float32
VMEM = pl.BlockSpec(memory_space=pltpu.VMEM)
SMEM = pl.BlockSpec(memory_space=pltpu.SMEM)
ANY = pl.BlockSpec(memory_space=pl.ANY)
K0, V0, Q0 = 0, HW, 2 * HW
VB = 512


def params(limit=40):
    return pltpu.CompilerParams(vmem_limit_bytes=limit * 1024 * 1024)


def nt(left, right):
    return lax.dot_general(left, right, (((1,), (1,)), ((), ())), preferred_element_type=F32)


def nn(left, right):
    return jnp.dot(left, right, preferred_element_type=F32)


def window(first):
    return first // 128 * 128, -(-(first + HD) // 128) * 128


def head_only(x, first, start):
    lane = lax.broadcasted_iota(jnp.int32, x.shape, 1) + start
    return jnp.where((lane >= first) & (lane < first + HD), x, jnp.zeros_like(x))


def norm_parts(x):
    center = x - jnp.mean(x, axis=-1, keepdims=True)
    rstd = lax.rsqrt(jnp.mean(center * center, axis=-1, keepdims=True) + 1e-6)
    return center, rstd


def order_kernel(target_ref, order_ref):
    rows = lax.broadcasted_iota(jnp.int32, (D, D), 0)
    order_ref[...] = jnp.where(rows == target_ref[...], 1.0, 0.0).astype(BF)


def hidden_kernel(x_ref, gain_ref, order_ref, out_ref):
    for i in range(x_ref.shape[0] // T):
        center, rstd = norm_parts(x_ref[i * T : (i + 1) * T, :].astype(F32))
        hidden = (center * rstd * gain_ref[...]).astype(BF)
        out_ref[i * T : (i + 1) * T, :] = nn(hidden, order_ref[...]).astype(BF)


def collect(blocks, first, rows, w_ref, sems):
    copies = [
        pltpu.make_async_copy(src.at[pl.ds(first, rows)], w_ref.at[pl.ds(rows * i, rows)], sems.at[i])
        for i, src in enumerate(blocks)
    ]
    for c in copies:
        c.start()
    return copies


def forward_kernel(
    blocks_ref, hw_ref, hc_ref, he_ref, b0, b1, b2, b3, b4, b5, b6, b7,
    win_ref, e_ref, att_ref, stat_ref, rows_ref,
    w_ref, bias_ref, acc_ref, sems,
):
    copies = collect((b0, b1, b2, b3, b4, b5, b6, b7), 0, 144, w_ref, sems)
    acc_ref[...] = jnp.zeros_like(acc_ref)

    qc = (lax.broadcasted_iota(jnp.int32, (T, T), 0) & 8) > 0
    kc = (lax.broadcasted_iota(jnp.int32, (T, T), 1) & 8) > 0

    def allowed(c, r, w):
        return blocks_ref[(c * 3 + r) * 5 + w - c].astype(F32) if 0 <= w - c < 5 else jnp.float32(0.0)

    lane_c = (lax.broadcasted_iota(jnp.int32, (1, T), 1) & 8) > 0
    rows = []
    for r in range(3):
        for w in range(6):
            rows.append(jnp.where(lane_c, allowed(1, r, w), allowed(0, r, w)))
    rows_ref[...] = jnp.concatenate(rows + [jnp.zeros((14, T), F32)], axis=0)
    for t in range(3):
        for r in range(3):
            seen = jnp.where(
                qc,
                jnp.where(kc, allowed(1, r, 2 * t + 1), allowed(1, r, 2 * t)),
                jnp.where(kc, allowed(0, r, 2 * t + 1), allowed(0, r, 2 * t)),
            )
            j = 3 * t + r
            bias_ref[:, j * T : (j + 1) * T] = (1.0 - seen) * OFF
    for c in copies:
        c.wait()
    for g, h_ref in enumerate((hw_ref, hc_ref, he_ref)):
        for part in range(3):
            s = slice(part * T, (part + 1) * T)
            win_ref[(g * 3 + part) * T : (g * 3 + part + 1) * T, :] = nn(h_ref[s, :], w_ref[...]).astype(BF)

    own = slice(4 * T, 5 * T)
    lanes = lax.broadcasted_iota(jnp.int32, (T, T), 1)
    stats = jnp.zeros((T, T), F32)
    for e in range(H):
        a, b = window(K0 + HD * e)
        q = head_only(win_ref[own, Q0 + a : Q0 + b], HD * e, a) if Q0 + b <= QKV else head_only(
            jnp.concatenate([win_ref[own, Q0 + a : QKV], jnp.zeros((T, Q0 + b - QKV), BF)], axis=1), HD * e, a)
        s = nt(q, win_ref[:, a:b]) * SCALE2 + bias_ref[...]
        peak = jnp.max(s, axis=1, keepdims=True)
        p = jnp.exp2(s - peak)
        total = jnp.sum(p, axis=1, keepdims=True)
        low = p.astype(BF)
        e_ref[e * T : (e + 1) * T, :] = low
        inv = 1.0 / total
        stats = jnp.where(lanes == e, peak + jnp.log2(total), stats)
        stats = jnp.where(lanes == 16 + e, inv, stats)
        a, b = window(V0 + HD * e)
        o = nn(low, win_ref[:, a:b]) * inv
        acc_ref[:, a - VB : b - VB] += head_only(o, V0 + HD * e, a)
    att_ref[...] = acc_ref[...].astype(BF)
    stat_ref[...] = stats


def pixel_kernel(
    att_ref, stat0_ref, rows_ref, place_ref, wpix_ref, x_ref, meas_ref, filt_ref, b0, b1, b2, b3, b4, b5, b6, b7,
    den_ref, og_ref, pack_ref, stat_ref,
    wo_ref, sems,
):
    copies = collect((b0, b1, b2, b3, b4, b5, b6, b7), 144, 48, wo_ref, sems)
    lane_of = lax.broadcasted_iota(jnp.int32, (640, 384), 0)
    whole, lower, upper = (
        jnp.where(lane_of == place_ref[i : i + 1, :], 1.0, 0.0).astype(BF) for i in range(3)
    )
    att = att_ref[...]
    att_whole, att_lower, att_upper = (nn(att, g).astype(BF) for g in (whole, lower, upper))
    for c in copies:
        c.wait()
    mixed = nn(att_whole, wo_ref[:, 0:D]) + jnp.concatenate(
        [nn(att_lower, wo_ref[:, D:QKV]), nn(att_upper, wo_ref[:, D:QKV])], axis=1
    )
    den = (x_ref[...].astype(F32) + mixed).astype(BF)
    den_ref[...] = den
    colors = nt(den, wpix_ref[...])
    filt = filt_ref[...]
    misfit = -meas_ref[...]
    for c in range(3):
        misfit = misfit + jnp.where(filt == c, colors[:, 64 * c : 64 * c + 64], 0.0)
    spread = jnp.concatenate([jnp.where(filt == c, misfit, 0.0) for c in range(3)], axis=1).astype(BF)
    og = nn(spread, wpix_ref[...])
    og_ref[...] = og
    back = og.astype(BF)
    up = (
        nt(nt(back, wo_ref[:, 0:D]).astype(BF), whole)
        + nt(nt(back[:, 0:HW], wo_ref[:, D:QKV]).astype(BF), lower)
        + nt(nt(back[:, HW:D], wo_ref[:, D:QKV]).astype(BF), upper)
    ).astype(BF)
    pack_ref[0:T, :] = up
    prod = up.astype(F32) * att.astype(F32)
    lanes = lax.broadcasted_iota(jnp.int32, (T, T), 1)
    stats = stat0_ref[...]
    for e in range(H):
        a, b = window(V0 + HD * e)
        inner = jnp.sum(head_only(prod[:, a - VB : b - VB], V0 + HD * e, a), axis=1, keepdims=True)
        stats = jnp.where(lanes == 8 + e, inner, stats)
    stat_ref[...] = stats
    turned = stats.T[0:16, :]
    high = turned.astype(BF)
    rest = turned - high.astype(F32)
    mid = rest.astype(BF)
    low = (rest - mid.astype(F32)).astype(BF)
    pack_ref[T : T + 16, :] = jnp.concatenate(
        [high, mid, low, rows_ref[0:16, :].astype(BF), rows_ref[16:32, :].astype(BF)], axis=1
    )


def query_kernel(win_ref, e_ref, up_ref, stat_ref, gq_ref, acc_ref):
    acc_ref[...] = jnp.zeros_like(acc_ref)
    for e in range(H):
        a, b = window(V0 + HD * e)
        up = head_only(up_ref[0:T, a - VB : b - VB], V0 + HD * e, a)
        dprob = nt(up, win_ref[:, a:b])
        p = e_ref[e * T : (e + 1) * T, :].astype(F32)
        ds = (p * (dprob - stat_ref[:, 8 + e : 9 + e])).astype(BF)
        a, b = window(K0 + HD * e)
        dq = nn(ds, win_ref[:, a:b]) * (stat_ref[:, 16 + e : 17 + e] * FACTOR)
        acc_ref[:, a:b] += head_only(dq, HD * e, a)
    gq_ref[...] = acc_ref[:, 0:HW].astype(BF)


def key_side(win_ref, groups, gk_ref, gv_ref):
    own = slice(4 * T, 5 * T)
    kc = (lax.broadcasted_iota(jnp.int32, (T, T), 0) & 8) > 0
    for t, pack_ref in groups:
        bias, stats, ups = [], [], []
        for r in range(3):
            base = r * 144
            ups.append(pack_ref[base : base + T, :])
            extra = pack_ref[base + T : base + T + 16, :].astype(F32)
            stats.append(extra[:, 0:128] + extra[:, 128:256] + extra[:, 256:384])
            seen = []
            for w in range(2):
                i = (2 - r) * 6 + (2 - t) * 2 + w
                seen.append(extra[i : i + 1, 384:512] if i < 16 else extra[i - 16 : i - 15, 512:640])
            bias.append((1.0 - jnp.where(kc, seen[1], seen[0])) * OFF)
        bias = jnp.concatenate(bias, axis=1)
        stats = jnp.concatenate(stats, axis=1)
        ups = jnp.concatenate(ups, axis=0)
        q_rows = slice(t * 3 * T, (t + 1) * 3 * T)
        for e in range(H):
            a, b = window(K0 + HD * e)
            if Q0 + b <= QKV:
                q = win_ref[q_rows, Q0 + a : Q0 + b]
            else:
                q = jnp.concatenate([win_ref[q_rows, Q0 + a : QKV], jnp.zeros((3 * T, Q0 + b - QKV), BF)], axis=1)
            k = head_only(win_ref[own, a:b], HD * e, a)
            s = nt(k, q) * SCALE2 + bias
            p = jnp.exp2(s - stats[e : e + 1, :])
            c, d = window(V0 + HD * e)
            v = head_only(win_ref[own, c:d], V0 + HD * e, c)
            up = ups[:, c - VB : d - VB]
            ds = (p * (nt(v, up) - stats[8 + e : 9 + e, :])).astype(BF)
            gk_ref[:, a:b] += head_only(nn(ds, q), HD * e, a)
            gv_ref[:, c - VB : d - VB] += head_only(nn(p.astype(BF), up), V0 + HD * e, c)


def key_centre_kernel(win_ref, pack_ref, gk_ref, gv_ref):
    gk_ref[...] = jnp.zeros_like(gk_ref)
    gv_ref[...] = jnp.zeros_like(gv_ref)
    key_side(win_ref, ((1, pack_ref),), gk_ref, gv_ref)


def finish_kernel(
    win_ref, packw_ref, packe_ref, gk0_ref, gv0_ref, gq_ref, order_ref, x_ref, gain_ref, og_ref,
    b0, b1, b2, b3, b4, b5, b6, b7,
    out_ref, gk_ref, gv_ref, w_ref, sems,
):
    copies = collect((b0, b1, b2, b3, b4, b5, b6, b7), 0, 144, w_ref, sems)
    gk_ref[...] = gk0_ref[...]
    gv_ref[...] = gv0_ref[...]
    key_side(win_ref, ((0, packw_ref), (2, packe_ref)), gk_ref, gv_ref)
    gk = (gk_ref[:, 0:HW] * FACTOR).astype(BF)
    gv = gv_ref[:, 64:640].astype(BF)
    grads = jnp.concatenate([gk, gv, gq_ref[...]], axis=1)
    for c in copies:
        c.wait()
    moved = nt(grads, w_ref[...])
    high = moved.astype(BF)
    rest = moved - high.astype(F32)
    mid = rest.astype(BF)
    low = (rest - mid.astype(F32)).astype(BF)
    order = order_ref[...]
    grad = (nt(high, order) + nt(mid, order) + nt(low, order)) * gain_ref[...]
    center, rstd = norm_parts(x_ref[...].astype(F32))
    xhat = center * rstd
    mean_g = jnp.mean(grad, axis=-1, keepdims=True)
    mean_gx = jnp.mean(grad * xhat, axis=-1, keepdims=True)
    out_ref[...] = rstd * (grad - mean_g - xhat * mean_gx) + og_ref[...]


def shaped(shape, dtype=BF):
    return jax.ShapeDtypeStruct(shape, dtype)


def shards_held(yh, z, x, core, block, second):
    xs = (x + jnp.asarray(np.array([0, 3, 1, 2] * 2)[block])) & 3
    cs = core ^ jnp.asarray((block >= 4).astype(np.int32))
    hops = jnp.where(second, 3 - xs, xs + 1)
    zs = (z + jnp.where(cs == 0, -hops, hops)) & 7
    other = jnp.logical_xor(second, (xs == 3) & (cs == 1)).astype(jnp.int32)
    return (yh ^ other) * 8 + zs


def weight_targets(yh, z, x, core):
    place = np.arange(D)
    block, row = place // 144, place % 144
    held = shards_held(yh, z, x, core, block, row >= 72)
    return (held * 72 + row % 72).astype(jnp.int32).reshape(1, D)


def out_targets(yh, z, x, core):
    place = np.arange(384)
    block, row = place // 48, place % 48
    held = shards_held(yh, z, x, core, block, row >= 24) * 36 + 64
    row = row % 24
    whole = held + row
    lower = jnp.where(row < 12, held + 24 + row, -1)
    upper = jnp.where(row >= 12, held + 12 + row, -1)
    return jnp.stack([whole, lower, upper]).astype(jnp.int32)


def device(yh, z, yl, x, core):
    return (((yh * 8 + z % 8) * 4 + yl) * 4 + x) * 2 + core


def fetch_routes():
    first, second = [], []
    for yh in range(2):
        for z in range(8):
            for yl in range(4):
                for x in range(4):
                    for core in range(2):
                        me = device(yh, z, yl, x, core)
                        way = 1 if core else -1
                        near, far = z + way * (x + 1), z + way * (3 - x)
                        if x == 3 and core == 1:
                            first.append((device(1 - yh, near, 3 - yl, x, core), me))
                            second.append((me, me))
                        else:
                            first.append((device(yh, near, yl, x, core), me))
                            second.append((device(1 - yh, far, 3 - yl, x, core), me))
    return first, second


def on_device(tokens, gain, w_query, w_key, w_value, w_out, w_pixel, measured, filter_color, block_mask):
    yh, z, xi, core = (lax.axis_index(n) for n in ("yh", "z", "x", "core"))
    x = tokens.reshape(T, D)
    gain = gain.reshape(1, D)
    south = [(i, i + 1) for i in range(15)]
    north = [(j, i) for i, j in south]
    east = [(i, (i + 1) % 32) for i in range(32)]
    west = [(j, i) for i, j in east]
    lat, lon = ("yh", "z"), ("yl", "x", "core")
    first, second = fetch_routes()

    def swap(v):
        return lax.ppermute(v, "core", [(0, 1), (1, 0)])

    def along(v, shift):
        return lax.ppermute(v, "x", [(i, (i + shift) % 4) for i in range(4)])

    def columns(own):
        before = lax.ppermute(own, lat, south)
        after = lax.ppermute(own, lat, north)
        return jnp.concatenate([before, own, after], axis=0)

    def sides(column):
        return lax.ppermute(column, lon, east), lax.ppermute(column, lon, west)

    out_rows = jnp.concatenate(
        [w_out[:24], jnp.concatenate([w_out[24:, :HW], w_out[24:, HW:]], axis=0)], axis=1
    )
    mine = jnp.concatenate([jnp.concatenate([w_key, w_value, w_query], axis=1), out_rows], axis=0)
    one, two = lax.ppermute(mine, lat + lon, first), lax.ppermute(mine, lat + lon, second)
    fetched = jnp.concatenate([one[:72], two[:72], one[72:], two[72:]], axis=0)
    column = columns(x)
    from_west, from_east = sides(column)
    order = pl.pallas_call(
        order_kernel, out_shape=shaped((D, D)), in_specs=[VMEM], out_specs=VMEM, compiler_params=params(16),
        cost_estimate=pl.CostEstimate(flops=2_000_000_000, bytes_accessed=3_000_000, transcendentals=0),
    )(weight_targets(yh, z, xi, core))

    def hidden(v):
        return pl.pallas_call(
            hidden_kernel, out_shape=shaped((3 * T, D)), in_specs=[VMEM] * 3, out_specs=VMEM,
            compiler_params=params(16),
            cost_estimate=pl.CostEstimate(flops=3_000_000_000, bytes_accessed=5_000_000, transcendentals=0),
        )(v, gain, order)

    fetched, hc = lax.optimization_barrier((fetched, hidden(column)))
    right, left = along(fetched, 1), along(fetched, 3)
    right, left, hw, he = lax.optimization_barrier((right, left, hidden(from_west), hidden(from_east)))
    across = jnp.concatenate([along(right[:96], 1), along(left[96:], 3)], axis=0)
    held = (fetched, right, left, across)
    blocks = held + tuple(swap(v) for v in held)

    win, e, att, stat0, rows = pl.pallas_call(
        forward_kernel,
        out_shape=(
            shaped((9 * T, QKV)), shaped((H * T, 9 * T)), shaped((T, 640)), shaped((T, T), F32), shaped((32, T), F32),
        ),
        in_specs=[SMEM] + [VMEM] * 3 + [ANY] * 8,
        out_specs=(VMEM,) * 5,
        scratch_shapes=[
            pltpu.VMEM((D, QKV), BF), pltpu.VMEM((T, 9 * T), F32), pltpu.VMEM((T, 640), F32),
            pltpu.SemaphoreType.DMA((8,)),
        ],
        compiler_params=params(20),
        cost_estimate=pl.CostEstimate(flops=12_000_000_000, bytes_accessed=8_000_000, transcendentals=1_000_000),
    )(block_mask.reshape(30), hw, hc, he, *blocks)
    den, og, pack, stat = pl.pallas_call(
        pixel_kernel,
        out_shape=(shaped((T, D)), shaped((T, D), F32), shaped((144, 640)), shaped((T, T), F32)),
        in_specs=[VMEM] * 8 + [ANY] * 8, out_specs=(VMEM,) * 4,
        scratch_shapes=[pltpu.VMEM((384, QKV), BF), pltpu.SemaphoreType.DMA((8,))],
        compiler_params=params(14),
    )(
        att, stat0, rows, out_targets(yh, z, xi, core), w_pixel.T, x, measured.reshape(T, 64),
        filter_color.reshape(T, 64), *blocks,
    )
    packs = columns(pack)
    gq = pl.pallas_call(
        query_kernel, out_shape=shaped((T, HW)), in_specs=[VMEM] * 4, out_specs=VMEM,
        scratch_shapes=[pltpu.VMEM((T, 640), F32)], compiler_params=params(16),
        cost_estimate=pl.CostEstimate(flops=4_000_000_000, bytes_accessed=6_000_000, transcendentals=0),
    )(win, e, pack, stat)
    packs, gq = lax.optimization_barrier((packs, gq))
    packs_west, packs_east = sides(packs)
    gk, gv = pl.pallas_call(
        key_centre_kernel, out_shape=(shaped((T, 640), F32),) * 2, in_specs=[VMEM] * 2, out_specs=(VMEM,) * 2,
        compiler_params=params(16),
        cost_estimate=pl.CostEstimate(flops=4_000_000_000, bytes_accessed=6_000_000, transcendentals=0),
    )(win, packs)
    guidance = pl.pallas_call(
        finish_kernel, out_shape=shaped((T, D), F32), in_specs=[VMEM] * 10 + [ANY] * 8, out_specs=VMEM,
        scratch_shapes=[pltpu.VMEM((T, 640), F32)] * 2 + [pltpu.VMEM((D, QKV), BF), pltpu.SemaphoreType.DMA((8,))],
        compiler_params=params(20),
    )(win, packs_west, packs_east, gk, gv, gq, order, x, gain, og, *blocks)
    return den.reshape(tokens.shape), guidance.reshape(tokens.shape)


def solution(mesh):
    split = Mesh(mesh.devices.reshape(2, 8, 4, 4, 2), ("yh", "z", "yl", "x", "core"))
    lat, lon = ("yh", "z"), ("yl", "x", "core")
    return jax.shard_map(
        on_device,
        mesh=split,
        in_specs=(
            P(lat, lon, None), P(), P(lat, None), P(lat, None), P(lat, None), P(lat, None), P(),
            P(lat, lon, None), P(lat, lon, None), P(lat, lon, None, None),
        ),
        out_specs=(P(lat, lon, None), P(lat, lon, None)),
        check_vma=False,
    )
```

```python
import functools

import jax
import jax.numpy as jnp
import numpy as np
from jax import lax
from jax.experimental import pallas as pl
from jax.experimental.pallas import tpu as pltpu
from jax.sharding import Mesh, PartitionSpec as P

H = 8
HD = 72
HW = 576
D = 1152
T = 128
QKV = 3 * HW
FACTOR = HD ** (-0.5)
SCALE2 = FACTOR * 1.4426950408889634
OFF = -1e30
BF = jnp.bfloat16
F32 = jnp.float32
VMEM = pl.BlockSpec(memory_space=pltpu.VMEM)
SMEM = pl.BlockSpec(memory_space=pltpu.SMEM)
ANY = pl.BlockSpec(memory_space=pl.ANY)
HBM = pl.BlockSpec(memory_space=pltpu.HBM)
K0, V0, Q0 = 0, HW, 2 * HW
VB = 512


def params(limit=40):
    return pltpu.CompilerParams(vmem_limit_bytes=limit * 1024 * 1024)


def nt(left, right):
    return lax.dot_general(left, right, (((1,), (1,)), ((), ())), preferred_element_type=F32)


def nn(left, right):
    return jnp.dot(left, right, preferred_element_type=F32)


def window(first):
    return first // 128 * 128, -(-(first + HD) // 128) * 128


def head_only(x, first, start):
    lane = lax.broadcasted_iota(jnp.int32, x.shape, 1) + start
    return jnp.where((lane >= first) & (lane < first + HD), x, jnp.zeros_like(x))


def norm_parts(x):
    center = x - jnp.mean(x, axis=-1, keepdims=True)
    rstd = lax.rsqrt(jnp.mean(center * center, axis=-1, keepdims=True) + 1e-6)
    return center, rstd


def order_kernel(target_ref, order_ref):
    rows = lax.broadcasted_iota(jnp.int32, (D, D), 0)
    order_ref[...] = jnp.where(rows == target_ref[...], 1.0, 0.0).astype(BF)


def hidden_kernel(x_ref, gain_ref, order_ref, out_ref):
    for i in range(x_ref.shape[0] // T):
        center, rstd = norm_parts(x_ref[i * T : (i + 1) * T, :].astype(F32))
        hidden = (center * rstd * gain_ref[...]).astype(BF)
        out_ref[i * T : (i + 1) * T, :] = nn(hidden, order_ref[...]).astype(BF)


def gather_kernel(k_any, v_any, q_any, o_any, out_ref, k_ref, v_ref, q_ref, o_ref, sems):
    pairs = ((k_any, k_ref), (v_any, v_ref), (q_any, q_ref), (o_any, o_ref))
    copies = [pltpu.make_async_copy(a, b, sems.at[i]) for i, (a, b) in enumerate(pairs)]
    for c in copies:
        c.start()
    for c in copies:
        c.wait()
    lasts = jnp.concatenate([o_ref[24:36, 0:HW], o_ref[24:36, HW:D]], axis=0)
    rows = jnp.concatenate([o_ref[0:24, :], lasts], axis=1)
    out_ref[...] = jnp.concatenate(
        [jnp.concatenate([k_ref[...], v_ref[...], q_ref[...]], axis=1), rows], axis=0
    )


def collect(blocks, first, rows, w_ref, sems):
    copies = [
        pltpu.make_async_copy(src.at[pl.ds(first, rows)], w_ref.at[pl.ds(rows * i, rows)], sems.at[i])
        for i, src in enumerate(blocks)
    ]
    for c in copies:
        c.start()
    return copies


def table_kernel(blocks_ref, hw_any, hc_any, he_any, out_ref):
    for i in range(30):
        out_ref[i] = blocks_ref[i]


def forward_kernel(
    blocks_ref, hw_any, hc_any, he_any, place_ref, wpix_ref, x_ref, meas_ref, filt_ref,
    b0, b1, b2, b3, b4, b5, b6, b7,
    win_ref, e_ref, den_ref, og_ref, pack_ref, stat_ref,
    wo_ref, w_ref, wn_ref, h_ref, bias_ref, acc_ref, sems_o, sems, sems_h,
):
    copies_o = collect((b0, b1, b2, b3, b4, b5, b6, b7), 144, 48, wo_ref, sems_o)
    copies = collect((b0, b1, b2, b3, b4, b5, b6, b7), 0, 144, w_ref, sems)
    copies += collect((hw_any, hc_any, he_any), 0, 3 * T, h_ref, sems_h)
    acc_ref[...] = jnp.zeros_like(acc_ref)

    qc = (lax.broadcasted_iota(jnp.int32, (T, T), 0) & 8) > 0
    kc = (lax.broadcasted_iota(jnp.int32, (T, T), 1) & 8) > 0

    def allowed(c, r, w):
        return blocks_ref[(c * 3 + r) * 5 + w - c].astype(F32) if 0 <= w - c < 5 else jnp.float32(0.0)

    lane_c = (lax.broadcasted_iota(jnp.int32, (1, T), 1) & 8) > 0
    rows = []
    for r in range(3):
        for w in range(6):
            rows.append(jnp.where(lane_c, allowed(1, r, w), allowed(0, r, w)))
    for t in range(3):
        for r in range(3):
            seen = jnp.where(
                qc,
                jnp.where(kc, allowed(1, r, 2 * t + 1), allowed(1, r, 2 * t)),
                jnp.where(kc, allowed(0, r, 2 * t + 1), allowed(0, r, 2 * t)),
            )
            j = 3 * t + r
            bias_ref[:, j * T : (j + 1) * T] = (1.0 - seen) * OFF
    lane_of = lax.broadcasted_iota(jnp.int32, (640, 384), 0)
    whole, lower, upper = (
        jnp.where(lane_of == place_ref[i : i + 1, :], 1.0, 0.0).astype(BF) for i in range(3)
    )
    for c in copies_o:
        c.wait()
    halves = wo_ref[:, D:QKV]
    wn_ref[...] = (
        nn(whole, wo_ref[:, 0:D]) + jnp.concatenate([nn(lower, halves), nn(upper, halves)], axis=1)
    ).astype(BF)
    for c in copies:
        c.wait()
    for i in range(9):
        s = slice(i * T, (i + 1) * T)
        win_ref[s, :] = nn(h_ref[s, :], w_ref[...]).astype(BF)

    own = slice(4 * T, 5 * T)
    lanes = lax.broadcasted_iota(jnp.int32, (T, T), 1)
    stats = jnp.zeros((T, T), F32)
    for e in range(H):
        a, b = window(K0 + HD * e)
        q = head_only(win_ref[own, Q0 + a : Q0 + b], HD * e, a) if Q0 + b <= QKV else head_only(
            jnp.concatenate([win_ref[own, Q0 + a : QKV], jnp.zeros((T, Q0 + b - QKV), BF)], axis=1), HD * e, a)
        s = nt(q, win_ref[:, a:b]) * SCALE2 + bias_ref[...]
        peak = jnp.max(s, axis=1, keepdims=True)
        p = jnp.exp2(s - peak)
        total = jnp.sum(p, axis=1, keepdims=True)
        low = p.astype(BF)
        e_ref[e * T : (e + 1) * T, :] = low
        inv = 1.0 / total
        stats = jnp.where(lanes == e, peak + jnp.log2(total), stats)
        stats = jnp.where(lanes == 16 + e, inv, stats)
        a, b = window(V0 + HD * e)
        o = nn(low, win_ref[:, a:b]) * inv
        acc_ref[:, a - VB : b - VB] += head_only(o, V0 + HD * e, a)

    att = acc_ref[...].astype(BF)
    den = (x_ref[...].astype(F32) + nn(att, wn_ref[...])).astype(BF)
    den_ref[...] = den
    colors = nt(den, wpix_ref[...])
    filt = filt_ref[...]
    misfit = -meas_ref[...]
    for c in range(3):
        misfit = misfit + jnp.where(filt == c, colors[:, 64 * c : 64 * c + 64], 0.0)
    spread = jnp.concatenate([jnp.where(filt == c, misfit, 0.0) for c in range(3)], axis=1).astype(BF)
    og = nn(spread, wpix_ref[...])
    og_ref[...] = og
    up = nt(og.astype(BF), wn_ref[...]).astype(BF)
    pack_ref[0:T, :] = up
    prod = up.astype(F32) * att.astype(F32)
    for e in range(H):
        a, b = window(V0 + HD * e)
        inner = jnp.sum(head_only(prod[:, a - VB : b - VB], V0 + HD * e, a), axis=1, keepdims=True)
        stats = jnp.where(lanes == 8 + e, inner, stats)
    stat_ref[...] = stats
    turned = stats.T[0:16, :]
    high = turned.astype(BF)
    rest = turned - high.astype(F32)
    mid = rest.astype(BF)
    low = (rest - mid.astype(F32)).astype(BF)
    pack_ref[T : T + 16, :] = jnp.concatenate(
        [
            high, mid, low, jnp.concatenate(rows[:16], axis=0).astype(BF),
            jnp.concatenate(rows[16:] + [jnp.zeros((14, T), F32)], axis=0).astype(BF),
        ],
        axis=1,
    )


def query_kernel(win_ref, e_ref, up_ref, stat_ref, gq_ref, acc_ref):
    acc_ref[...] = jnp.zeros_like(acc_ref)
    for e in range(H):
        a, b = window(V0 + HD * e)
        up = head_only(up_ref[0:T, a - VB : b - VB], V0 + HD * e, a)
        dprob = nt(up, win_ref[:, a:b])
        p = e_ref[e * T : (e + 1) * T, :].astype(F32)
        ds = (p * (dprob - stat_ref[:, 8 + e : 9 + e])).astype(BF)
        a, b = window(K0 + HD * e)
        dq = nn(ds, win_ref[:, a:b]) * (stat_ref[:, 16 + e : 17 + e] * FACTOR)
        acc_ref[:, a:b] += head_only(dq, HD * e, a)
    gq_ref[...] = acc_ref[:, 0:HW].astype(BF)


def key_side(win_ref, groups, gk_ref, gv_ref):
    own = slice(4 * T, 5 * T)
    kc = (lax.broadcasted_iota(jnp.int32, (T, T), 0) & 8) > 0
    for t, pack_ref in groups:
        bias, stats, ups = [], [], []
        for r in range(3):
            base = r * 144
            ups.append(pack_ref[base : base + T, :])
            extra = pack_ref[base + T : base + T + 16, :].astype(F32)
            stats.append(extra[:, 0:128] + extra[:, 128:256] + extra[:, 256:384])
            seen = []
            for w in range(2):
                i = (2 - r) * 6 + (2 - t) * 2 + w
                seen.append(extra[i : i + 1, 384:512] if i < 16 else extra[i - 16 : i - 15, 512:640])
            bias.append((1.0 - jnp.where(kc, seen[1], seen[0])) * OFF)
        bias = jnp.concatenate(bias, axis=1)
        stats = jnp.concatenate(stats, axis=1)
        ups = jnp.concatenate(ups, axis=0)
        q_rows = slice(t * 3 * T, (t + 1) * 3 * T)
        for e in range(H):
            a, b = window(K0 + HD * e)
            if Q0 + b <= QKV:
                q = win_ref[q_rows, Q0 + a : Q0 + b]
            else:
                q = jnp.concatenate([win_ref[q_rows, Q0 + a : QKV], jnp.zeros((3 * T, Q0 + b - QKV), BF)], axis=1)
            k = head_only(win_ref[own, a:b], HD * e, a)
            s = nt(k, q) * SCALE2 + bias
            p = jnp.exp2(s - stats[e : e + 1, :])
            c, d = window(V0 + HD * e)
            v = head_only(win_ref[own, c:d], V0 + HD * e, c)
            up = ups[:, c - VB : d - VB]
            ds = (p * (nt(v, up) - stats[8 + e : 9 + e, :])).astype(BF)
            gk_ref[:, a:b] += head_only(nn(ds, q), HD * e, a)
            gv_ref[:, c - VB : d - VB] += head_only(nn(p.astype(BF), up), V0 + HD * e, c)


def key_centre_kernel(win_ref, pack_ref, gk_ref, gv_ref):
    gk_ref[...] = jnp.zeros_like(gk_ref)
    gv_ref[...] = jnp.zeros_like(gv_ref)
    key_side(win_ref, ((1, pack_ref),), gk_ref, gv_ref)


def finish_kernel(
    win_ref, packw_ref, packe_ref, gk0_ref, gv0_ref, gq_ref, order_ref, x_ref, gain_ref, og_ref,
    b0, b1, b2, b3, b4, b5, b6, b7,
    out_ref, gk_ref, gv_ref, w_ref, sems,
):
    copies = collect((b0, b1, b2, b3, b4, b5, b6, b7), 0, 144, w_ref, sems)
    gk_ref[...] = gk0_ref[...]
    gv_ref[...] = gv0_ref[...]
    key_side(win_ref, ((0, packw_ref), (2, packe_ref)), gk_ref, gv_ref)
    gk = (gk_ref[:, 0:HW] * FACTOR).astype(BF)
    gv = gv_ref[:, 64:640].astype(BF)
    grads = jnp.concatenate([gk, gv, gq_ref[...]], axis=1)
    for c in copies:
        c.wait()
    moved = nt(grads, w_ref[...])
    high = moved.astype(BF)
    low = (moved - high.astype(F32)).astype(BF)
    both = nt(jnp.concatenate([high, low], axis=0), order_ref[...])
    grad = (both[0:T, :] + both[T : 2 * T, :]) * gain_ref[...]
    center, rstd = norm_parts(x_ref[...].astype(F32))
    xhat = center * rstd
    mean_g = jnp.mean(grad, axis=-1, keepdims=True)
    mean_gx = jnp.mean(grad * xhat, axis=-1, keepdims=True)
    out_ref[...] = rstd * (grad - mean_g - xhat * mean_gx) + og_ref[...]


def shaped(shape, dtype=BF):
    return jax.ShapeDtypeStruct(shape, dtype)


def shards_held(yh, z, x, core, block, second):
    xs = (x + jnp.asarray(np.array([0, 3, 1, 2] * 2)[block])) & 3
    cs = core ^ jnp.asarray((block >= 4).astype(np.int32))
    hops = jnp.where(second, 3 - xs, xs + 1)
    zs = (z + jnp.where(cs == 0, -hops, hops)) & 7
    other = jnp.logical_xor(second, (xs == 3) & (cs == 1)).astype(jnp.int32)
    return (yh ^ other) * 8 + zs


def weight_targets(yh, z, x, core):
    place = np.arange(D)
    block, row = place // 144, place % 144
    held = shards_held(yh, z, x, core, block, row >= 72)
    return (held * 72 + row % 72).astype(jnp.int32).reshape(1, D)


def out_targets(yh, z, x, core):
    place = np.arange(384)
    block, row = place // 48, place % 48
    held = shards_held(yh, z, x, core, block, row >= 24) * 36 + 64
    row = row % 24
    whole = held + row
    lower = jnp.where(row < 12, held + 24 + row, -1)
    upper = jnp.where(row >= 12, held + 12 + row, -1)
    return jnp.stack([whole, lower, upper]).astype(jnp.int32)


def device(yh, z, yl, x, core):
    return (((yh * 8 + z % 8) * 4 + yl) * 4 + x) * 2 + core


def fetch_routes():
    first, second = [], []
    for yh in range(2):
        for z in range(8):
            for yl in range(4):
                for x in range(4):
                    for core in range(2):
                        me = device(yh, z, yl, x, core)
                        way = 1 if core else -1
                        near, far = z + way * (x + 1), z + way * (3 - x)
                        if x == 3 and core == 1:
                            first.append((device(1 - yh, near, 3 - yl, x, core), me))
                            second.append((me, me))
                        else:
                            first.append((device(yh, near, yl, x, core), me))
                            second.append((device(1 - yh, far, 3 - yl, x, core), me))
    return first, second


def on_device(tokens, gain, w_query, w_key, w_value, w_out, w_pixel, measured, filter_color, block_mask):
    yh, z, xi, core = (lax.axis_index(n) for n in ("yh", "z", "x", "core"))
    x = tokens.reshape(T, D)
    gain = gain.reshape(1, D)
    south = [(i, i + 1) for i in range(15)]
    north = [(j, i) for i, j in south]
    east = [(i, (i + 1) % 32) for i in range(32)]
    west = [(j, i) for i, j in east]
    lat, lon = ("yh", "z"), ("yl", "x", "core")
    first, second = fetch_routes()

    def swap(v):
        return lax.ppermute(v, "core", [(0, 1), (1, 0)])

    def along(v, shift):
        return lax.ppermute(v, "x", [(i, (i + shift) % 4) for i in range(4)])

    def columns(own):
        before = lax.ppermute(own, lat, south)
        after = lax.ppermute(own, lat, north)
        return jnp.concatenate([before, own, after], axis=0)

    def sides(column):
        return lax.ppermute(column, lon, east), lax.ppermute(column, lon, west)

    mine = pl.pallas_call(
        gather_kernel, out_shape=shaped((96, QKV)), in_specs=[HBM] * 4, out_specs=VMEM,
        scratch_shapes=[pltpu.VMEM((72, HW), BF)] * 3 + [pltpu.VMEM((36, D), BF), pltpu.SemaphoreType.DMA((4,))],
        compiler_params=params(8),
    )(w_key, w_value, w_query, w_out)
    one, two = lax.ppermute(mine, lat + lon, first), lax.ppermute(mine, lat + lon, second)
    fetched = jnp.concatenate([one[:72], two[:72], one[72:], two[72:]], axis=0)
    column = columns(x)
    from_west, from_east = sides(column)
    target = weight_targets(yh, z, xi, core)

    def ordering(target):
        return pl.pallas_call(
            order_kernel, out_shape=shaped((D, D)), in_specs=[VMEM], out_specs=VMEM, compiler_params=params(8),
            cost_estimate=pl.CostEstimate(flops=2_000_000_000, bytes_accessed=3_000_000, transcendentals=0),
        )(target)

    order = ordering(target)

    def hidden(v):
        return pl.pallas_call(
            hidden_kernel, out_shape=shaped((3 * T, D)), in_specs=[VMEM] * 3, out_specs=VMEM,
            compiler_params=params(16),
            cost_estimate=pl.CostEstimate(flops=3_000_000_000, bytes_accessed=5_000_000, transcendentals=0),
        )(v, gain, order)

    fetched, hc = lax.optimization_barrier((fetched, hidden(column)))
    right, left = along(fetched, 1), along(fetched, 3)
    right, left, hw, he = lax.optimization_barrier((right, left, hidden(from_west), hidden(from_east)))
    across = jnp.concatenate([along(right[:96], 1), along(left[96:], 3)], axis=0)
    held = (fetched, right, left, across)
    blocks = held + tuple(swap(v) for v in held)

    table = pl.pallas_call(
        table_kernel, out_shape=shaped((30,), jnp.int32), in_specs=[SMEM] + [ANY] * 3, out_specs=SMEM,
        compiler_params=params(4),
        cost_estimate=pl.CostEstimate(flops=2_000_000_000, bytes_accessed=3_000_000, transcendentals=0),
    )(block_mask.reshape(30), hw, hc, he)
    win, e, den, og, pack, stat = pl.pallas_call(
        forward_kernel,
        out_shape=(
            shaped((9 * T, QKV)), shaped((H * T, 9 * T)), shaped((T, D)), shaped((T, D), F32), shaped((144, 640)),
            shaped((T, T), F32),
        ),
        in_specs=[SMEM] + [HBM] * 3 + [VMEM] * 5 + [ANY] * 8,
        out_specs=(VMEM,) * 6,
        scratch_shapes=[
            pltpu.VMEM((384, QKV), BF), pltpu.VMEM((D, QKV), BF), pltpu.VMEM((640, D), BF),
            pltpu.VMEM((9 * T, D), BF), pltpu.VMEM((T, 9 * T), F32), pltpu.VMEM((T, 640), F32),
            pltpu.SemaphoreType.DMA((8,)), pltpu.SemaphoreType.DMA((8,)), pltpu.SemaphoreType.DMA((3,)),
        ],
        compiler_params=params(22),
        cost_estimate=pl.CostEstimate(flops=12_000_000_000, bytes_accessed=8_000_000, transcendentals=1_000_000),
    )(
        table, hw, hc, he, out_targets(yh, z, xi, core), w_pixel.T, x, measured.reshape(T, 64),
        filter_color.reshape(T, 64), *blocks,
    )
    packs = columns(pack)
    gq = pl.pallas_call(
        query_kernel, out_shape=shaped((T, HW)), in_specs=[VMEM] * 4, out_specs=VMEM,
        scratch_shapes=[pltpu.VMEM((T, 640), F32)], compiler_params=params(16),
        cost_estimate=pl.CostEstimate(flops=4_000_000_000, bytes_accessed=6_000_000, transcendentals=0),
    )(win, e, pack, stat)
    packs, gq, target = lax.optimization_barrier((packs, gq, target))
    packs_west, packs_east = sides(packs)
    gk, gv = pl.pallas_call(
        key_centre_kernel, out_shape=(shaped((T, 640), F32),) * 2, in_specs=[VMEM] * 2, out_specs=(VMEM,) * 2,
        compiler_params=params(16),
        cost_estimate=pl.CostEstimate(flops=4_000_000_000, bytes_accessed=6_000_000, transcendentals=0),
    )(win, packs)
    guidance = pl.pallas_call(
        finish_kernel, out_shape=shaped((T, D), F32), in_specs=[VMEM] * 10 + [ANY] * 8, out_specs=VMEM,
        scratch_shapes=[pltpu.VMEM((T, 640), F32)] * 2 + [pltpu.VMEM((D, QKV), BF), pltpu.SemaphoreType.DMA((8,))],
        compiler_params=params(20),
    )(win, packs_west, packs_east, gk, gv, gq, ordering(target), x, gain, og, *blocks)
    return den.reshape(tokens.shape), guidance.reshape(tokens.shape)


def solution(mesh):
    split = Mesh(mesh.devices.reshape(2, 8, 4, 4, 2), ("yh", "z", "yl", "x", "core"))
    lat, lon = ("yh", "z"), ("yl", "x", "core")
    return jax.shard_map(
        on_device,
        mesh=split,
        in_specs=(
            P(lat, lon, None), P(), P(lat, None), P(lat, None), P(lat, None), P(lat, None), P(),
            P(lat, lon, None), P(lat, lon, None), P(lat, lon, None, None),
        ),
        out_specs=(P(lat, lon, None), P(lat, lon, None)),
        check_vma=False,
    )
```

```python
import functools

import jax
import jax.numpy as jnp
import numpy as np
from jax import lax
from jax.experimental import pallas as pl
from jax.experimental.pallas import tpu as pltpu
from jax.sharding import Mesh, PartitionSpec as P

H = 8
HD = 72
HW = 576
D = 1152
T = 128
QKV = 3 * HW
FACTOR = HD ** (-0.5)
SCALE2 = FACTOR * 1.4426950408889634
OFF = -1e30
BF = jnp.bfloat16
F32 = jnp.float32
VMEM = pl.BlockSpec(memory_space=pltpu.VMEM)
SMEM = pl.BlockSpec(memory_space=pltpu.SMEM)
ANY = pl.BlockSpec(memory_space=pl.ANY)
HBM = pl.BlockSpec(memory_space=pltpu.HBM)
K0, V0, Q0 = 0, HW, 2 * HW
VB = 512


def params(limit=40):
    return pltpu.CompilerParams(vmem_limit_bytes=limit * 1024 * 1024)


def nt(left, right):
    return lax.dot_general(left, right, (((1,), (1,)), ((), ())), preferred_element_type=F32)


def nn(left, right):
    return jnp.dot(left, right, preferred_element_type=F32)


def window(first):
    return first // 128 * 128, -(-(first + HD) // 128) * 128


def head_only(x, first, start):
    lane = lax.broadcasted_iota(jnp.int32, x.shape, 1) + start
    return jnp.where((lane >= first) & (lane < first + HD), x, jnp.zeros_like(x))


def norm_parts(x):
    center = x - jnp.mean(x, axis=-1, keepdims=True)
    rstd = lax.rsqrt(jnp.mean(center * center, axis=-1, keepdims=True) + 1e-6)
    return center, rstd


def order_kernel(target_ref, order_ref):
    rows = lax.broadcasted_iota(jnp.int32, (D, D), 0)
    order_ref[...] = jnp.where(rows == target_ref[...], 1.0, 0.0).astype(BF)


def hidden_kernel(x_ref, gain_ref, order_ref, out_ref):
    for i in range(x_ref.shape[0] // T):
        center, rstd = norm_parts(x_ref[i * T : (i + 1) * T, :].astype(F32))
        hidden = (center * rstd * gain_ref[...]).astype(BF)
        out_ref[i * T : (i + 1) * T, :] = nn(hidden, order_ref[...]).astype(BF)


def gather_kernel(k_any, v_any, q_any, o_any, out_ref, k_ref, v_ref, q_ref, o_ref, sems):
    pairs = ((k_any, k_ref), (v_any, v_ref), (q_any, q_ref), (o_any, o_ref))
    copies = [pltpu.make_async_copy(a, b, sems.at[i]) for i, (a, b) in enumerate(pairs)]
    for c in copies:
        c.start()
    for c in copies:
        c.wait()
    lasts = jnp.concatenate([o_ref[24:36, 0:HW], o_ref[24:36, HW:D]], axis=0)
    rows = jnp.concatenate([o_ref[0:24, :], lasts], axis=1)
    out_ref[...] = jnp.concatenate(
        [jnp.concatenate([k_ref[...], v_ref[...], q_ref[...]], axis=1), rows], axis=0
    )


def collect(blocks, first, rows, w_ref):
    for i, block in enumerate(blocks):
        w_ref[rows * i : rows * (i + 1), :] = block[first : first + rows, :]


def position(slot_t, slot_r):
    turned = 2 - slot_r
    return (slot_r if slot_t == 1 else turned, slot_t), (turned if slot_t == 1 else slot_r, 2 - slot_t)


def project_kernel(
    place_ref, hw_ref, hc_ref, he_ref, b0, b1, b2, b3, b4, b5, b6, b7, win_ref, wn_ref, wo_ref, w_ref
):
    collect((b0, b1, b2, b3, b4, b5, b6, b7), 144, 48, wo_ref)
    collect((b0, b1, b2, b3, b4, b5, b6, b7), 0, 144, w_ref)
    for g, h_ref in enumerate((hw_ref, hc_ref, he_ref)):
        for part in range(3):
            s = slice(part * T, (part + 1) * T)
            win_ref[(g * 3 + part) * T : (g * 3 + part + 1) * T, :] = nn(h_ref[s, :], w_ref[...]).astype(BF)
    lane_of = lax.broadcasted_iota(jnp.int32, (640, 384), 0)
    whole, lower, upper = (
        jnp.where(lane_of == place_ref[i : i + 1, :], 1.0, 0.0).astype(BF) for i in range(3)
    )
    halves = wo_ref[:, D:QKV]
    wn_ref[...] = (
        nn(whole, wo_ref[:, 0:D]) + jnp.concatenate([nn(lower, halves), nn(upper, halves)], axis=1)
    ).astype(BF)


def forward_kernel(
    blocks_ref, win_ref, wn_ref, wpix_ref, x_ref, meas_ref, filt_ref,
    e_ref, den_ref, og_ref, pack_ref, stat_ref,
    bias_ref, acc_ref,
):
    acc_ref[...] = jnp.zeros_like(acc_ref)

    qc = (lax.broadcasted_iota(jnp.int32, (T, T), 0) & 8) > 0
    kc = (lax.broadcasted_iota(jnp.int32, (T, T), 1) & 8) > 0

    core = blocks_ref[30]

    def allowed(c, r, w):
        there = jnp.logical_and(w - c >= 0, w - c < 5)
        value = blocks_ref[(c * 3 + r) * 5 + jnp.clip(w - c, 0, 4)]
        return jnp.where(there, value, 0).astype(F32)

    lane_c = (lax.broadcasted_iota(jnp.int32, (1, T), 1) & 8) > 0
    rows = []
    for r in range(3):
        for w in range(6):
            rows.append(jnp.where(lane_c, allowed(1, r, jnp.int32(w)), allowed(0, r, jnp.int32(w))))
    for slot_t in range(3):
        for slot_r in range(3):
            (r0, t0), (r1, t1) = position(slot_t, slot_r)
            r, t = jnp.where(core == 0, r0, r1), jnp.where(core == 0, t0, t1)
            seen = jnp.where(
                qc,
                jnp.where(kc, allowed(1, r, 2 * t + 1), allowed(1, r, 2 * t)),
                jnp.where(kc, allowed(0, r, 2 * t + 1), allowed(0, r, 2 * t)),
            )
            j = 3 * slot_t + slot_r
            bias_ref[:, j * T : (j + 1) * T] = (1.0 - seen) * OFF
    own = slice(4 * T, 5 * T)
    lanes = lax.broadcasted_iota(jnp.int32, (T, T), 1)
    stats = jnp.zeros((T, T), F32)
    for e in range(H):
        a, b = window(K0 + HD * e)
        q = head_only(win_ref[own, Q0 + a : Q0 + b], HD * e, a) if Q0 + b <= QKV else head_only(
            jnp.concatenate([win_ref[own, Q0 + a : QKV], jnp.zeros((T, Q0 + b - QKV), BF)], axis=1), HD * e, a)
        s = nt(q, win_ref[:, a:b]) * SCALE2 + bias_ref[...]
        peak = jnp.max(s, axis=1, keepdims=True)
        p = jnp.exp2(s - peak)
        total = jnp.sum(p, axis=1, keepdims=True)
        low = p.astype(BF)
        e_ref[e * T : (e + 1) * T, :] = low
        inv = 1.0 / total
        stats = jnp.where(lanes == e, peak + jnp.log2(total), stats)
        stats = jnp.where(lanes == 16 + e, inv, stats)
        a, b = window(V0 + HD * e)
        o = nn(low, win_ref[:, a:b]) * inv
        acc_ref[:, a - VB : b - VB] += head_only(o, V0 + HD * e, a)

    att = acc_ref[...].astype(BF)
    den = (x_ref[...].astype(F32) + nn(att, wn_ref[...])).astype(BF)
    den_ref[...] = den
    colors = nt(den, wpix_ref[...])
    filt = filt_ref[...]
    misfit = -meas_ref[...]
    for c in range(3):
        misfit = misfit + jnp.where(filt == c, colors[:, 64 * c : 64 * c + 64], 0.0)
    spread = jnp.concatenate([jnp.where(filt == c, misfit, 0.0) for c in range(3)], axis=1).astype(BF)
    og = nn(spread, wpix_ref[...])
    og_ref[...] = og
    up = nt(og.astype(BF), wn_ref[...]).astype(BF)
    pack_ref[0:T, :] = up
    prod = up.astype(F32) * att.astype(F32)
    for e in range(H):
        a, b = window(V0 + HD * e)
        inner = jnp.sum(head_only(prod[:, a - VB : b - VB], V0 + HD * e, a), axis=1, keepdims=True)
        stats = jnp.where(lanes == 8 + e, inner, stats)
    stat_ref[...] = stats
    turned = stats.T[0:16, :]
    high = turned.astype(BF)
    rest = turned - high.astype(F32)
    mid = rest.astype(BF)
    low = (rest - mid.astype(F32)).astype(BF)
    pack_ref[T : T + 16, :] = jnp.concatenate(
        [
            high, mid, low, jnp.concatenate(rows[:16], axis=0).astype(BF),
            jnp.concatenate(rows[16:] + [jnp.zeros((14, T), F32)], axis=0).astype(BF),
        ],
        axis=1,
    )


def query_kernel(win_ref, e_ref, up_ref, stat_ref, gq_ref, acc_ref):
    acc_ref[...] = jnp.zeros_like(acc_ref)
    for e in range(H):
        a, b = window(V0 + HD * e)
        up = head_only(up_ref[0:T, a - VB : b - VB], V0 + HD * e, a)
        dprob = nt(up, win_ref[:, a:b])
        p = e_ref[e * T : (e + 1) * T, :].astype(F32)
        ds = (p * (dprob - stat_ref[:, 8 + e : 9 + e])).astype(BF)
        a, b = window(K0 + HD * e)
        dq = nn(ds, win_ref[:, a:b]) * (stat_ref[:, 16 + e : 17 + e] * FACTOR)
        acc_ref[:, a:b] += head_only(dq, HD * e, a)
    gq_ref[...] = acc_ref[:, 0:HW].astype(BF)


def key_side(core_ref, win_ref, groups, gk_ref, gv_ref):
    own = slice(4 * T, 5 * T)
    kc = (lax.broadcasted_iota(jnp.int32, (T, T), 0) & 8) > 0
    second = core_ref[0].astype(F32)
    for t, pack_ref in groups:
        bias, stats, ups = [], [], []
        for r in range(3):
            base = r * 144
            ups.append(pack_ref[base : base + T, :])
            extra = pack_ref[base + T : base + T + 16, :].astype(F32)
            stats.append(extra[:, 0:128] + extra[:, 128:256] + extra[:, 256:384])
            seen = []
            for w in range(2):
                on = []
                for row, col in position(t, r):
                    i = (2 - row) * 6 + (2 - col) * 2 + w
                    on.append(extra[i : i + 1, 384:512] if i < 16 else extra[i - 16 : i - 15, 512:640])
                seen.append(on[0] * (1.0 - second) + on[1] * second)
            bias.append((1.0 - jnp.where(kc, seen[1], seen[0])) * OFF)
        bias = jnp.concatenate(bias, axis=1)
        stats = jnp.concatenate(stats, axis=1)
        ups = jnp.concatenate(ups, axis=0)
        q_rows = slice(t * 3 * T, (t + 1) * 3 * T)
        for e in range(H):
            a, b = window(K0 + HD * e)
            if Q0 + b <= QKV:
                q = win_ref[q_rows, Q0 + a : Q0 + b]
            else:
                q = jnp.concatenate([win_ref[q_rows, Q0 + a : QKV], jnp.zeros((3 * T, Q0 + b - QKV), BF)], axis=1)
            k = head_only(win_ref[own, a:b], HD * e, a)
            s = nt(k, q) * SCALE2 + bias
            p = jnp.exp2(s - stats[e : e + 1, :])
            c, d = window(V0 + HD * e)
            v = head_only(win_ref[own, c:d], V0 + HD * e, c)
            up = ups[:, c - VB : d - VB]
            ds = (p * (nt(v, up) - stats[8 + e : 9 + e, :])).astype(BF)
            gk_ref[:, a:b] += head_only(nn(ds, q), HD * e, a)
            gv_ref[:, c - VB : d - VB] += head_only(nn(p.astype(BF), up), V0 + HD * e, c)


def key_centre_kernel(core_ref, win_ref, pack_ref, gk_ref, gv_ref):
    gk_ref[...] = jnp.zeros_like(gk_ref)
    gv_ref[...] = jnp.zeros_like(gv_ref)
    key_side(core_ref, win_ref, ((1, pack_ref),), gk_ref, gv_ref)


def finish_kernel(
    core_ref, win_ref, packo_ref, packi_ref, gk0_ref, gv0_ref, gq_ref, order_ref, x_ref, gain_ref, og_ref,
    b0, b1, b2, b3, b4, b5, b6, b7,
    out_ref, gk_ref, gv_ref, w_ref,
):
    collect((b0, b1, b2, b3, b4, b5, b6, b7), 0, 144, w_ref)
    gk_ref[...] = gk0_ref[...]
    gv_ref[...] = gv0_ref[...]
    key_side(core_ref, win_ref, ((0, packo_ref), (2, packi_ref)), gk_ref, gv_ref)
    gk = (gk_ref[:, 0:HW] * FACTOR).astype(BF)
    gv = gv_ref[:, 64:640].astype(BF)
    grads = jnp.concatenate([gk, gv, gq_ref[...]], axis=1)
    moved = nt(grads, w_ref[...])
    high = moved.astype(BF)
    low = (moved - high.astype(F32)).astype(BF)
    both = nt(jnp.concatenate([high, low], axis=0), order_ref[...])
    grad = (both[0:T, :] + both[T : 2 * T, :]) * gain_ref[...]
    center, rstd = norm_parts(x_ref[...].astype(F32))
    xhat = center * rstd
    mean_g = jnp.mean(grad, axis=-1, keepdims=True)
    mean_gx = jnp.mean(grad * xhat, axis=-1, keepdims=True)
    out_ref[...] = rstd * (grad - mean_g - xhat * mean_gx) + og_ref[...]


def shaped(shape, dtype=BF):
    return jax.ShapeDtypeStruct(shape, dtype)


def shards_held(yh, z, x, core, block, second):
    cs = core ^ jnp.asarray((block >= 4).astype(np.int32))
    shift = np.array([0, 3, 1, 2] * 2)[block]
    xs = (x + jnp.where(cs == 0, jnp.asarray(shift), jnp.asarray(-shift))) & 3
    hops = jnp.where(second, 3 - xs, xs + 1)
    zs = (z + jnp.where(cs == 0, -hops, hops)) & 7
    other = jnp.logical_xor(second, (xs == 3) & (cs == 1)).astype(jnp.int32)
    return (yh ^ other) * 8 + zs


def weight_targets(yh, z, x, core):
    place = np.arange(D)
    block, row = place // 144, place % 144
    held = shards_held(yh, z, x, core, block, row >= 72)
    return (held * 72 + row % 72).astype(jnp.int32).reshape(1, D)


def out_targets(yh, z, x, core):
    place = np.arange(384)
    block, row = place // 48, place % 48
    held = shards_held(yh, z, x, core, block, row >= 24) * 36 + 64
    row = row % 24
    whole = held + row
    lower = jnp.where(row < 12, held + 24 + row, -1)
    upper = jnp.where(row >= 12, held + 12 + row, -1)
    return jnp.stack([whole, lower, upper]).astype(jnp.int32)


def device(yh, z, yl, x, core):
    return (((yh * 8 + z % 8) * 4 + yl) * 4 + x) * 2 + core


def fetch_routes():
    first, second = [], []
    for yh in range(2):
        for z in range(8):
            for yl in range(4):
                for x in range(4):
                    for core in range(2):
                        me = device(yh, z, yl, x, core)
                        way = 1 if core else -1
                        near, far = z + way * (x + 1), z + way * (3 - x)
                        if x == 3 and core == 1:
                            first.append((device(1 - yh, near, 3 - yl, x, core), me))
                            second.append((me, me))
                        else:
                            first.append((device(yh, near, yl, x, core), me))
                            second.append((device(1 - yh, far, 3 - yl, x, core), me))
    return first, second


def on_device(tokens, gain, w_query, w_key, w_value, w_out, w_pixel, measured, filter_color, block_mask):
    yh, z, xi, core = (lax.axis_index(n) for n in ("yh", "z", "x", "core"))
    which = core.reshape(1).astype(jnp.int32)
    x = tokens.reshape(T, D)
    gain = gain.reshape(1, D)
    south = [(2 * i, 2 * i + 2) for i in range(15)] + [(2 * i + 3, 2 * i + 1) for i in range(15)]
    north = [(j, i) for i, j in south]
    ring = [(2 * i, (2 * i + 2) % 8) for i in range(4)] + [((2 * i + 3) % 8, 2 * i + 1) for i in range(4)]
    back = [(j, i) for i, j in ring]
    border = [(2 * i + 1, (2 * i + 2) % 32) for i in range(16)]
    border = border + [(j, i) for i, j in border]
    lat, lon = ("yh", "z"), ("yl", "x", "core")
    first, second = fetch_routes()

    def swap(v):
        return lax.ppermute(v, "core", [(0, 1), (1, 0)])

    def along(v, perm):
        return lax.ppermute(v, ("x", "core"), perm)

    def columns(own):
        before = lax.ppermute(own, lat + ("core",), south)
        after = lax.ppermute(own, lat + ("core",), north)
        return jnp.concatenate([before, own, after], axis=0)

    def sides(column):
        return lax.ppermute(column, lon, border), swap(column)

    mine = pl.pallas_call(
        gather_kernel, out_shape=shaped((96, QKV)), in_specs=[HBM] * 4, out_specs=VMEM,
        scratch_shapes=[pltpu.VMEM((72, HW), BF)] * 3 + [pltpu.VMEM((36, D), BF), pltpu.SemaphoreType.DMA((4,))],
        compiler_params=params(8),
    )(w_key, w_value, w_query, w_out)
    one, two = lax.ppermute(mine, lat + lon, first), lax.ppermute(mine, lat + lon, second)
    fetched = jnp.concatenate([one[:72], two[:72], one[72:], two[72:]], axis=0)
    column = columns(x)
    outer, inner = sides(column)
    target = weight_targets(yh, z, xi, core)

    def ordering(target):
        return pl.pallas_call(
            order_kernel, out_shape=shaped((D, D)), in_specs=[VMEM], out_specs=VMEM, compiler_params=params(8),
            cost_estimate=pl.CostEstimate(flops=2_000_000_000, bytes_accessed=3_000_000, transcendentals=0),
        )(target)

    order = ordering(target)

    def hidden(v):
        return pl.pallas_call(
            hidden_kernel, out_shape=shaped((3 * T, D)), in_specs=[VMEM] * 3, out_specs=VMEM,
            compiler_params=params(16),
            cost_estimate=pl.CostEstimate(flops=3_000_000_000, bytes_accessed=5_000_000, transcendentals=0),
        )(v, gain, order)

    fetched, hc = lax.optimization_barrier((fetched, hidden(column)))
    right, left = along(fetched, ring), along(fetched, back)
    fetched_too = swap(fetched)
    right, left, hw, he, fetched_too = lax.optimization_barrier(
        (right, left, hidden(outer), hidden(inner), fetched_too)
    )
    across = jnp.concatenate([along(right[:96], ring), along(left[96:], back)], axis=0)
    blocks = (fetched, right, left, across, fetched_too, swap(right), swap(left), swap(across))

    win, wn = pl.pallas_call(
        project_kernel, out_shape=(shaped((9 * T, QKV)), shaped((640, D))),
        in_specs=[VMEM] * 12, out_specs=(VMEM,) * 2,
        scratch_shapes=[pltpu.VMEM((384, QKV), BF), pltpu.VMEM((D, QKV), BF)],
        compiler_params=params(24),
        cost_estimate=pl.CostEstimate(flops=6_000_000_000, bytes_accessed=8_000_000, transcendentals=0),
    )(out_targets(yh, z, xi, core), hw, hc, he, *blocks)
    e, den, og, pack, stat = pl.pallas_call(
        forward_kernel,
        out_shape=(
            shaped((H * T, 9 * T)), shaped((T, D)), shaped((T, D), F32), shaped((144, 640)), shaped((T, T), F32),
        ),
        in_specs=[SMEM] + [VMEM] * 6, out_specs=(VMEM,) * 5,
        scratch_shapes=[pltpu.VMEM((T, 9 * T), F32), pltpu.VMEM((T, 640), F32)],
        compiler_params=params(18),
        cost_estimate=pl.CostEstimate(flops=6_000_000_000, bytes_accessed=8_000_000, transcendentals=1_000_000),
    )(jnp.concatenate([block_mask.reshape(30), which]), win, wn, w_pixel.T, x, measured.reshape(T, 64), filter_color.reshape(T, 64))
    packs = columns(pack)
    gq = pl.pallas_call(
        query_kernel, out_shape=shaped((T, HW)), in_specs=[VMEM] * 4, out_specs=VMEM,
        scratch_shapes=[pltpu.VMEM((T, 640), F32)], compiler_params=params(16),
        cost_estimate=pl.CostEstimate(flops=4_000_000_000, bytes_accessed=6_000_000, transcendentals=0),
    )(win, e, pack, stat)
    packs, gq, target = lax.optimization_barrier((packs, gq, target))
    packs_outer, packs_inner = sides(packs)
    gk, gv = pl.pallas_call(
        key_centre_kernel, out_shape=(shaped((T, 640), F32),) * 2, in_specs=[SMEM] + [VMEM] * 2, out_specs=(VMEM,) * 2,
        compiler_params=params(16),
        cost_estimate=pl.CostEstimate(flops=4_000_000_000, bytes_accessed=6_000_000, transcendentals=0),
    )(which, win, packs)
    guidance = pl.pallas_call(
        finish_kernel, out_shape=shaped((T, D), F32), in_specs=[SMEM] + [VMEM] * 18, out_specs=VMEM,
        scratch_shapes=[pltpu.VMEM((T, 640), F32)] * 2 + [pltpu.VMEM((D, QKV), BF)],
        compiler_params=params(20),
    )(which, win, packs_outer, packs_inner, gk, gv, gq, ordering(target), x, gain, og, *blocks)
    return den.reshape(tokens.shape), guidance.reshape(tokens.shape)


def solution(mesh):
    split = Mesh(mesh.devices.reshape(2, 8, 4, 4, 2), ("yh", "z", "yl", "x", "core"))
    lat, lon = ("yh", "z"), ("yl", "x", "core")
    return jax.shard_map(
        on_device,
        mesh=split,
        in_specs=(
            P(lat, lon, None), P(), P(lat, None), P(lat, None), P(lat, None), P(lat, None), P(),
            P(lat, lon, None), P(lat, lon, None), P(lat, lon, None, None),
        ),
        out_specs=(P(lat, lon, None), P(lat, lon, None)),
        check_vma=False,
    )
```

```python
import functools

import jax
import jax.numpy as jnp
import numpy as np
from jax import lax
from jax.experimental import pallas as pl
from jax.experimental.pallas import tpu as pltpu
from jax.sharding import Mesh, PartitionSpec as P

H = 8
HD = 72
HW = 576
D = 1152
T = 128
QKV = 3 * HW
FACTOR = HD ** (-0.5)
SCALE2 = FACTOR * 1.4426950408889634
OFF = -1e30
BF = jnp.bfloat16
F32 = jnp.float32
VMEM = pl.BlockSpec(memory_space=pltpu.VMEM)
SMEM = pl.BlockSpec(memory_space=pltpu.SMEM)
ANY = pl.BlockSpec(memory_space=pl.ANY)
HBM = pl.BlockSpec(memory_space=pltpu.HBM)
K0, V0, Q0 = 0, HW, 2 * HW
VB = 512


def params(limit=40):
    return pltpu.CompilerParams(vmem_limit_bytes=limit * 1024 * 1024)


def nt(left, right):
    return lax.dot_general(left, right, (((1,), (1,)), ((), ())), preferred_element_type=F32)


def nn(left, right):
    return jnp.dot(left, right, preferred_element_type=F32)


def window(first):
    return first // 128 * 128, -(-(first + HD) // 128) * 128


def head_only(x, first, start):
    lane = lax.broadcasted_iota(jnp.int32, x.shape, 1) + start
    return jnp.where((lane >= first) & (lane < first + HD), x, jnp.zeros_like(x))


def norm_parts(x):
    center = x - jnp.mean(x, axis=-1, keepdims=True)
    rstd = lax.rsqrt(jnp.mean(center * center, axis=-1, keepdims=True) + 1e-6)
    return center, rstd


def order_kernel(target_ref, order_ref):
    rows = lax.broadcasted_iota(jnp.int32, (D, D), 0)
    order_ref[...] = jnp.where(rows == target_ref[...], 1.0, 0.0).astype(BF)


def hidden_kernel(x_ref, gain_ref, target_ref, out_ref, order_ref):
    order_kernel(target_ref, order_ref)
    for i in range(x_ref.shape[0] // T):
        center, rstd = norm_parts(x_ref[i * T : (i + 1) * T, :].astype(F32))
        hidden = (center * rstd * gain_ref[...]).astype(BF)
        out_ref[i * T : (i + 1) * T, :] = nn(hidden, order_ref[...]).astype(BF)


def collect(blocks, first, rows, w_ref):
    for i, block in enumerate(blocks):
        w_ref[rows * i : rows * (i + 1), :] = block[first : first + rows, :]


def position(slot_t, slot_r):
    turned = 2 - slot_r
    return (slot_r if slot_t == 1 else turned, slot_t), (turned if slot_t == 1 else slot_r, 2 - slot_t)


def project_kernel(
    place_ref, hw_ref, hc_ref, he_ref, b0, b1, b2, b3, b4, b5, b6, b7, win_ref, wn_ref, wo_ref, w_ref
):
    collect((b0, b1, b2, b3, b4, b5, b6, b7), 144, 48, wo_ref)
    collect((b0, b1, b2, b3, b4, b5, b6, b7), 0, 144, w_ref)
    for g, h_ref in enumerate((hw_ref, hc_ref, he_ref)):
        for part in range(3):
            s = slice(part * T, (part + 1) * T)
            win_ref[(g * 3 + part) * T : (g * 3 + part + 1) * T, :] = nn(h_ref[s, :], w_ref[...]).astype(BF)
    lane_of = lax.broadcasted_iota(jnp.int32, (640, 384), 0)
    whole, lower, upper = (
        jnp.where(lane_of == place_ref[i : i + 1, :], 1.0, 0.0).astype(BF) for i in range(3)
    )
    halves = wo_ref[:, D:QKV]
    wn_ref[...] = (
        nn(whole, wo_ref[:, 0:D]) + jnp.concatenate([nn(lower, halves), nn(upper, halves)], axis=1)
    ).astype(BF)


def forward_kernel(
    blocks_ref, win_ref, wn_ref, wpix_ref, x_ref, meas_ref, filt_ref,
    e_ref, den_ref, og_ref, pack_ref, stat_ref,
    bias_ref, acc_ref,
):
    acc_ref[...] = jnp.zeros_like(acc_ref)

    qc = (lax.broadcasted_iota(jnp.int32, (T, T), 0) & 8) > 0
    kc = (lax.broadcasted_iota(jnp.int32, (T, T), 1) & 8) > 0

    core = blocks_ref[30]

    def allowed(c, r, w):
        there = jnp.logical_and(w - c >= 0, w - c < 5)
        value = blocks_ref[(c * 3 + r) * 5 + jnp.clip(w - c, 0, 4)]
        return jnp.where(there, value, 0).astype(F32)

    lane_c = (lax.broadcasted_iota(jnp.int32, (1, T), 1) & 8) > 0
    rows = []
    for r in range(3):
        for w in range(6):
            rows.append(jnp.where(lane_c, allowed(1, r, jnp.int32(w)), allowed(0, r, jnp.int32(w))))
    for slot_t in range(3):
        for slot_r in range(3):
            (r0, t0), (r1, t1) = position(slot_t, slot_r)
            r, t = jnp.where(core == 0, r0, r1), jnp.where(core == 0, t0, t1)
            seen = jnp.where(
                qc,
                jnp.where(kc, allowed(1, r, 2 * t + 1), allowed(1, r, 2 * t)),
                jnp.where(kc, allowed(0, r, 2 * t + 1), allowed(0, r, 2 * t)),
            )
            j = 3 * slot_t + slot_r
            bias_ref[:, j * T : (j + 1) * T] = (1.0 - seen) * OFF
    own = slice(4 * T, 5 * T)
    lanes = lax.broadcasted_iota(jnp.int32, (T, T), 1)
    stats = jnp.zeros((T, T), F32)
    for e in range(H):
        a, b = window(K0 + HD * e)
        q = head_only(win_ref[own, Q0 + a : Q0 + b], HD * e, a) if Q0 + b <= QKV else head_only(
            jnp.concatenate([win_ref[own, Q0 + a : QKV], jnp.zeros((T, Q0 + b - QKV), BF)], axis=1), HD * e, a)
        s = nt(q, win_ref[:, a:b]) * SCALE2 + bias_ref[...]
        peak = jnp.max(s, axis=1, keepdims=True)
        p = jnp.exp2(s - peak)
        total = jnp.sum(p, axis=1, keepdims=True)
        low = p.astype(BF)
        e_ref[e * T : (e + 1) * T, :] = low
        inv = 1.0 / total
        stats = jnp.where(lanes == e, peak + jnp.log2(total), stats)
        stats = jnp.where(lanes == 16 + e, inv, stats)
        a, b = window(V0 + HD * e)
        o = nn(low, win_ref[:, a:b]) * inv
        acc_ref[:, a - VB : b - VB] += head_only(o, V0 + HD * e, a)

    att = acc_ref[...].astype(BF)
    den = (x_ref[...].astype(F32) + nn(att, wn_ref[...])).astype(BF)
    den_ref[...] = den
    colors = nt(den, wpix_ref[...])
    filt = filt_ref[...]
    misfit = -meas_ref[...]
    for c in range(3):
        misfit = misfit + jnp.where(filt == c, colors[:, 64 * c : 64 * c + 64], 0.0)
    spread = jnp.concatenate([jnp.where(filt == c, misfit, 0.0) for c in range(3)], axis=1).astype(BF)
    og = nn(spread, wpix_ref[...])
    og_ref[...] = og
    up = nt(og.astype(BF), wn_ref[...]).astype(BF)
    pack_ref[0:T, :] = up
    prod = up.astype(F32) * att.astype(F32)
    for e in range(H):
        a, b = window(V0 + HD * e)
        inner = jnp.sum(head_only(prod[:, a - VB : b - VB], V0 + HD * e, a), axis=1, keepdims=True)
        stats = jnp.where(lanes == 8 + e, inner, stats)
    stat_ref[...] = stats
    turned = stats.T[0:16, :]
    high = turned.astype(BF)
    rest = turned - high.astype(F32)
    mid = rest.astype(BF)
    low = (rest - mid.astype(F32)).astype(BF)
    pack_ref[T : T + 16, :] = jnp.concatenate(
        [
            high, mid, low, jnp.concatenate(rows[:16], axis=0).astype(BF),
            jnp.concatenate(rows[16:] + [jnp.zeros((14, T), F32)], axis=0).astype(BF),
        ],
        axis=1,
    )


def query_kernel(win_ref, e_ref, up_ref, stat_ref, gq_ref, acc_ref):
    acc_ref[...] = jnp.zeros_like(acc_ref)
    for e in range(H):
        a, b = window(V0 + HD * e)
        up = head_only(up_ref[0:T, a - VB : b - VB], V0 + HD * e, a)
        dprob = nt(up, win_ref[:, a:b])
        p = e_ref[e * T : (e + 1) * T, :].astype(F32)
        ds = (p * (dprob - stat_ref[:, 8 + e : 9 + e])).astype(BF)
        a, b = window(K0 + HD * e)
        dq = nn(ds, win_ref[:, a:b]) * (stat_ref[:, 16 + e : 17 + e] * FACTOR)
        acc_ref[:, a:b] += head_only(dq, HD * e, a)
    gq_ref[...] = acc_ref[:, 0:HW].astype(BF)


def key_side(core_ref, win_ref, tiles, gk_ref, gv_ref):
    own = slice(4 * T, 5 * T)
    kc = (lax.broadcasted_iota(jnp.int32, (T, T), 0) & 8) > 0
    second = core_ref[0].astype(F32)
    bias, stats, ups = [], [], []
    for t, r, pack_ref, base in tiles:
        ups.append(pack_ref[base : base + T, :])
        extra = pack_ref[base + T : base + T + 16, :].astype(F32)
        stats.append(extra[:, 0:128] + extra[:, 128:256] + extra[:, 256:384])
        seen = []
        for w in range(2):
            on = []
            for row, col in position(t, r):
                i = (2 - row) * 6 + (2 - col) * 2 + w
                on.append(extra[i : i + 1, 384:512] if i < 16 else extra[i - 16 : i - 15, 512:640])
            seen.append(on[0] * (1.0 - second) + on[1] * second)
        bias.append((1.0 - jnp.where(kc, seen[1], seen[0])) * OFF)
    bias = jnp.concatenate(bias, axis=1)
    stats = jnp.concatenate(stats, axis=1)
    ups = jnp.concatenate(ups, axis=0)
    count = len(tiles) * T

    def queries(a, b):
        return jnp.concatenate(
            [win_ref[(3 * t + r) * T : (3 * t + r + 1) * T, Q0 + a : Q0 + b] for t, r, _, _ in tiles], axis=0
        )

    for e in range(H):
        a, b = window(K0 + HD * e)
        if Q0 + b <= QKV:
            q = queries(a, b)
        else:
            q = jnp.concatenate([queries(a, HW), jnp.zeros((count, b - HW), BF)], axis=1)
        k = head_only(win_ref[own, a:b], HD * e, a)
        s = nt(k, q) * SCALE2 + bias
        p = jnp.exp2(s - stats[e : e + 1, :])
        c, d = window(V0 + HD * e)
        v = head_only(win_ref[own, c:d], V0 + HD * e, c)
        up = ups[:, c - VB : d - VB]
        ds = (p * (nt(v, up) - stats[8 + e : 9 + e, :])).astype(BF)
        gk_ref[:, a:b] += head_only(nn(ds, q), HD * e, a)
        gv_ref[:, c - VB : d - VB] += head_only(nn(p.astype(BF), up), V0 + HD * e, c)


def key_near_kernel(core_ref, win_ref, own_ref, before_ref, after_ref, outer_ref, inner_ref, gk_ref, gv_ref):
    gk_ref[...] = jnp.zeros_like(gk_ref)
    gv_ref[...] = jnp.zeros_like(gv_ref)
    tiles = (
        (1, 0, before_ref, 0), (1, 1, own_ref, 0), (1, 2, after_ref, 0), (0, 1, outer_ref, 0), (2, 1, inner_ref, 0)
    )
    key_side(core_ref, win_ref, tiles, gk_ref, gv_ref)


def finish_kernel(
    core_ref, win_ref, packo_ref, packi_ref, gk0_ref, gv0_ref, gq_ref, order_ref, x_ref, gain_ref, og_ref,
    b0, b1, b2, b3, b4, b5, b6, b7,
    out_ref, gk_ref, gv_ref, w_ref,
):
    collect((b0, b1, b2, b3, b4, b5, b6, b7), 0, 144, w_ref)
    gk_ref[...] = gk0_ref[...]
    gv_ref[...] = gv0_ref[...]
    tiles = ((0, 0, packo_ref, 0), (0, 2, packo_ref, 144), (2, 0, packi_ref, 0), (2, 2, packi_ref, 144))
    key_side(core_ref, win_ref, tiles, gk_ref, gv_ref)
    gk = (gk_ref[:, 0:HW] * FACTOR).astype(BF)
    gv = gv_ref[:, 64:640].astype(BF)
    grads = jnp.concatenate([gk, gv, gq_ref[...]], axis=1)
    moved = nt(grads, w_ref[...])
    high = moved.astype(BF)
    low = (moved - high.astype(F32)).astype(BF)
    both = nt(jnp.concatenate([high, low], axis=0), order_ref[...])
    grad = (both[0:T, :] + both[T : 2 * T, :]) * gain_ref[...]
    center, rstd = norm_parts(x_ref[...].astype(F32))
    xhat = center * rstd
    mean_g = jnp.mean(grad, axis=-1, keepdims=True)
    mean_gx = jnp.mean(grad * xhat, axis=-1, keepdims=True)
    out_ref[...] = rstd * (grad - mean_g - xhat * mean_gx) + og_ref[...]


def shaped(shape, dtype=BF):
    return jax.ShapeDtypeStruct(shape, dtype)


def shards_held(yh, z, x, core, block, second):
    cs = core ^ jnp.asarray((block >= 4).astype(np.int32))
    shift = np.array([0, 3, 1, 2] * 2)[block]
    xs = (x + jnp.where(cs == 0, jnp.asarray(shift), jnp.asarray(-shift))) & 3
    hops = jnp.where(second, 3 - xs, xs + 1)
    zs = (z + jnp.where(cs == 0, -hops, hops)) & 7
    other = jnp.logical_xor(second, (xs == 3) & (cs == 1)).astype(jnp.int32)
    return (yh ^ other) * 8 + zs


def weight_targets(yh, z, x, core):
    place = np.arange(D)
    block, row = place // 144, place % 144
    held = shards_held(yh, z, x, core, block, row >= 72)
    return (held * 72 + row % 72).astype(jnp.int32).reshape(1, D)


def out_targets(yh, z, x, core):
    place = np.arange(384)
    block, row = place // 48, place % 48
    held = shards_held(yh, z, x, core, block, row >= 24) * 36 + 64
    row = row % 24
    whole = held + row
    lower = jnp.where(row < 12, held + 24 + row, -1)
    upper = jnp.where(row >= 12, held + 12 + row, -1)
    return jnp.stack([whole, lower, upper]).astype(jnp.int32)


def device(yh, z, yl, x, core):
    return (((yh * 8 + z % 8) * 4 + yl) * 4 + x) * 2 + core


def fetch_routes():
    first, second = [], []
    for yh in range(2):
        for z in range(8):
            for yl in range(4):
                for x in range(4):
                    for core in range(2):
                        me = device(yh, z, yl, x, core)
                        way = 1 if core else -1
                        near, far = z + way * (x + 1), z + way * (3 - x)
                        if x == 3 and core == 1:
                            first.append((device(1 - yh, near, 3 - yl, x, core), me))
                            second.append((me, me))
                        else:
                            first.append((device(yh, near, yl, x, core), me))
                            second.append((device(1 - yh, far, 3 - yl, x, core), me))
    return first, second


def on_device(tokens, gain, w_query, w_key, w_value, w_out, w_pixel, measured, filter_color, block_mask):
    yh, z, xi, core = (lax.axis_index(n) for n in ("yh", "z", "x", "core"))
    which = core.reshape(1).astype(jnp.int32)
    x = tokens.reshape(T, D)
    gain = gain.reshape(1, D)
    south = [(2 * i, 2 * i + 2) for i in range(15)] + [(2 * i + 3, 2 * i + 1) for i in range(15)]
    north = [(j, i) for i, j in south]
    ring = [(2 * i, (2 * i + 2) % 8) for i in range(4)] + [((2 * i + 3) % 8, 2 * i + 1) for i in range(4)]
    back = [(j, i) for i, j in ring]
    border = [(2 * i + 1, (2 * i + 2) % 32) for i in range(16)]
    border = border + [(j, i) for i, j in border]
    lat, lon = ("yh", "z"), ("yl", "x", "core")
    first, second = fetch_routes()

    def swap(v):
        return lax.ppermute(v, "core", [(0, 1), (1, 0)])

    def along(v, perm):
        return lax.ppermute(v, ("x", "core"), perm)

    def rows_beside(own):
        return lax.ppermute(own, lat + ("core",), south), lax.ppermute(own, lat + ("core",), north)

    def sides(column):
        return lax.ppermute(column, lon, border), swap(column)

    def placed(v, rows, cols):
        return lax.pad(v, jnp.zeros((), BF), ((*rows, 0), (*cols, 0)))

    at_row = lax.broadcasted_iota(jnp.int32, (96, QKV), 0)
    at_col = lax.broadcasted_iota(jnp.int32, (96, QKV), 1)
    lefts = placed(w_out, (48, 12), (D, -HW))
    rights = placed(w_out, (60, 0), (HW, 0))
    mine = (
        placed(w_key, (0, 24), (0, 2 * HW)) + placed(w_value, (0, 24), (HW, HW))
        + placed(w_query, (0, 24), (2 * HW, 0)) + placed(w_out, (72, -12), (0, HW))
        + jnp.where(at_row >= 72, lefts, 0) + jnp.where((at_row >= 84) & (at_col >= D), rights, 0)
    )
    one, two = lax.ppermute(mine, lat + lon, first), lax.ppermute(mine, lat + lon, second)
    fetched = jnp.concatenate([one[:72], two[:72], one[72:], two[72:]], axis=0)
    before, after = rows_beside(x)
    column = jnp.concatenate([before, x, after], axis=0)
    outer, inner = sides(column)
    target = weight_targets(yh, z, xi, core)

    def ordering(target):
        return pl.pallas_call(
            order_kernel, out_shape=shaped((D, D)), in_specs=[VMEM], out_specs=VMEM, compiler_params=params(8),
            cost_estimate=pl.CostEstimate(flops=2_000_000_000, bytes_accessed=3_000_000, transcendentals=0),
        )(target)


    def hidden(v):
        return pl.pallas_call(
            hidden_kernel, out_shape=shaped((3 * T, D)), in_specs=[VMEM] * 3, out_specs=VMEM,
            scratch_shapes=[pltpu.VMEM((D, D), BF)], compiler_params=params(16),
            cost_estimate=pl.CostEstimate(flops=3_000_000_000, bytes_accessed=5_000_000, transcendentals=0),
        )(v, gain, target)

    fetched, hc = lax.optimization_barrier((fetched, hidden(column)))
    right, left = along(fetched, ring), along(fetched, back)
    right, left, he = lax.optimization_barrier((right, left, hidden(inner)))
    fetched_too = swap(fetched)
    upper, lower, hw = lax.optimization_barrier((along(right[:96], ring), along(left[96:], back), hidden(outer)))
    across = jnp.concatenate([upper, lower], axis=0)
    blocks = (fetched, right, left, across, fetched_too, swap(right), swap(left), swap(across))

    win, wn = pl.pallas_call(
        project_kernel, out_shape=(shaped((9 * T, QKV)), shaped((640, D))),
        in_specs=[VMEM] * 12, out_specs=(VMEM,) * 2,
        scratch_shapes=[pltpu.VMEM((384, QKV), BF), pltpu.VMEM((D, QKV), BF)],
        compiler_params=params(24),
        cost_estimate=pl.CostEstimate(flops=6_000_000_000, bytes_accessed=8_000_000, transcendentals=0),
    )(out_targets(yh, z, xi, core), hw, hc, he, *blocks)
    e, den, og, pack, stat = pl.pallas_call(
        forward_kernel,
        out_shape=(
            shaped((H * T, 9 * T)), shaped((T, D)), shaped((T, D), F32), shaped((144, 640)), shaped((T, T), F32),
        ),
        in_specs=[SMEM] + [VMEM] * 6, out_specs=(VMEM,) * 5,
        scratch_shapes=[pltpu.VMEM((T, 9 * T), F32), pltpu.VMEM((T, 640), F32)],
        compiler_params=params(18),
        cost_estimate=pl.CostEstimate(flops=6_000_000_000, bytes_accessed=8_000_000, transcendentals=1_000_000),
    )(jnp.concatenate([block_mask.reshape(30), which]), win, wn, w_pixel.T, x, measured.reshape(T, 64), filter_color.reshape(T, 64))
    before, after = rows_beside(pack)
    gq = pl.pallas_call(
        query_kernel, out_shape=shaped((T, HW)), in_specs=[VMEM] * 4, out_specs=VMEM,
        scratch_shapes=[pltpu.VMEM((T, 640), F32)], compiler_params=params(16),
        cost_estimate=pl.CostEstimate(flops=4_000_000_000, bytes_accessed=6_000_000, transcendentals=0),
    )(win, e, pack, stat)
    pack_late, gq = lax.optimization_barrier((pack, gq))
    near_outer, near_inner = sides(pack_late)
    corners, target = lax.optimization_barrier((jnp.concatenate([before, after], axis=0), target))
    packs_outer, packs_inner = sides(corners)
    gk, gv = pl.pallas_call(
        key_near_kernel, out_shape=(shaped((T, 640), F32),) * 2, in_specs=[SMEM] + [VMEM] * 6, out_specs=(VMEM,) * 2,
        compiler_params=params(16),
        cost_estimate=pl.CostEstimate(flops=4_000_000_000, bytes_accessed=6_000_000, transcendentals=0),
    )(which, win, pack, before, after, near_outer, near_inner)
    guidance = pl.pallas_call(
        finish_kernel, out_shape=shaped((T, D), F32), in_specs=[SMEM] + [VMEM] * 18, out_specs=VMEM,
        scratch_shapes=[pltpu.VMEM((T, 640), F32)] * 2 + [pltpu.VMEM((D, QKV), BF)],
        compiler_params=params(20),
    )(which, win, packs_outer, packs_inner, gk, gv, gq, ordering(target), x, gain, og, *blocks)
    return den.reshape(tokens.shape), guidance.reshape(tokens.shape)


def solution(mesh):
    split = Mesh(mesh.devices.reshape(2, 8, 4, 4, 2), ("yh", "z", "yl", "x", "core"))
    lat, lon = ("yh", "z"), ("yl", "x", "core")
    return jax.shard_map(
        on_device,
        mesh=split,
        in_specs=(
            P(lat, lon, None), P(), P(lat, None), P(lat, None), P(lat, None), P(lat, None), P(),
            P(lat, lon, None), P(lat, lon, None), P(lat, lon, None, None),
        ),
        out_specs=(P(lat, lon, None), P(lat, lon, None)),
        check_vma=False,
    )
```

```python
import functools

import jax
import jax.numpy as jnp
import numpy as np
from jax import lax
from jax.experimental import pallas as pl
from jax.experimental.pallas import tpu as pltpu
from jax.sharding import Mesh, PartitionSpec as P

H = 8
HD = 72
HW = 576
D = 1152
T = 128
QKV = 3 * HW
FACTOR = HD ** (-0.5)
SCALE2 = FACTOR * 1.4426950408889634
OFF = -1e30
BF = jnp.bfloat16
F32 = jnp.float32
VMEM = pl.BlockSpec(memory_space=pltpu.VMEM)
SMEM = pl.BlockSpec(memory_space=pltpu.SMEM)
ANY = pl.BlockSpec(memory_space=pl.ANY)
HBM = pl.BlockSpec(memory_space=pltpu.HBM)
K0, V0, Q0 = 0, HW, 2 * HW
VB = 512


def params(limit=40):
    return pltpu.CompilerParams(vmem_limit_bytes=limit * 1024 * 1024)


def nt(left, right):
    return lax.dot_general(left, right, (((1,), (1,)), ((), ())), preferred_element_type=F32)


def nn(left, right):
    return jnp.dot(left, right, preferred_element_type=F32)


def window(first):
    return first // 128 * 128, -(-(first + HD) // 128) * 128


def head_only(x, first, start):
    lane = lax.broadcasted_iota(jnp.int32, x.shape, 1) + start
    return jnp.where((lane >= first) & (lane < first + HD), x, jnp.zeros_like(x))


def norm_parts(x):
    center = x - jnp.mean(x, axis=-1, keepdims=True)
    rstd = lax.rsqrt(jnp.mean(center * center, axis=-1, keepdims=True) + 1e-6)
    return center, rstd


def order_kernel(target_ref, order_ref):
    rows = lax.broadcasted_iota(jnp.int32, (D, D), 0)
    order_ref[...] = jnp.where(rows == target_ref[...], 1.0, 0.0).astype(BF)


def hidden_kernel(x_ref, gain_ref, target_ref, out_ref, order_ref):
    order_kernel(target_ref, order_ref)
    for i in range(x_ref.shape[0] // T):
        center, rstd = norm_parts(x_ref[i * T : (i + 1) * T, :].astype(F32))
        hidden = (center * rstd * gain_ref[...]).astype(BF)
        out_ref[i * T : (i + 1) * T, :] = nn(hidden, order_ref[...]).astype(BF)


def collect(blocks, first, rows, w_ref):
    for i, block in enumerate(blocks):
        w_ref[rows * i : rows * (i + 1), :] = block[first : first + rows, :]


def position(slot_t, slot_r):
    turned = 2 - slot_r
    return (slot_r if slot_t == 1 else turned, slot_t), (turned if slot_t == 1 else slot_r, 2 - slot_t)


def project_kernel(
    place_ref, hw_ref, hc_ref, he_ref, b0, b1, b2, b3, b4, b5, b6, b7, win_ref, wn_ref, wo_ref, w_ref
):
    collect((b0, b1, b2, b3, b4, b5, b6, b7), 144, 48, wo_ref)
    collect((b0, b1, b2, b3, b4, b5, b6, b7), 0, 144, w_ref)
    for g, h_ref in enumerate((hw_ref, hc_ref, he_ref)):
        for part in range(3):
            s = slice(part * T, (part + 1) * T)
            win_ref[(g * 3 + part) * T : (g * 3 + part + 1) * T, :] = nn(h_ref[s, :], w_ref[...]).astype(BF)
    lane_of = lax.broadcasted_iota(jnp.int32, (640, 384), 0)
    whole, lower, upper = (
        jnp.where(lane_of == place_ref[i : i + 1, :], 1.0, 0.0).astype(BF) for i in range(3)
    )
    halves = wo_ref[:, D:QKV]
    wn_ref[...] = (
        nn(whole, wo_ref[:, 0:D]) + jnp.concatenate([nn(lower, halves), nn(upper, halves)], axis=1)
    ).astype(BF)


def forward_kernel(
    blocks_ref, win_ref, wn_ref, wpix_ref, x_ref, meas_ref, filt_ref,
    e_ref, den_ref, og_ref, pack_ref, stat_ref,
    bias_ref, acc_ref,
):
    acc_ref[...] = jnp.zeros_like(acc_ref)

    qc = (lax.broadcasted_iota(jnp.int32, (T, T), 0) & 8) > 0
    kc = (lax.broadcasted_iota(jnp.int32, (T, T), 1) & 8) > 0

    core = blocks_ref[30]

    def allowed(c, r, w):
        there = jnp.logical_and(w - c >= 0, w - c < 5)
        value = blocks_ref[(c * 3 + r) * 5 + jnp.clip(w - c, 0, 4)]
        return jnp.where(there, value, 0).astype(F32)

    lane_c = (lax.broadcasted_iota(jnp.int32, (1, T), 1) & 8) > 0
    rows = []
    for r in range(3):
        for w in range(6):
            rows.append(jnp.where(lane_c, allowed(1, r, jnp.int32(w)), allowed(0, r, jnp.int32(w))))
    for slot_t in range(3):
        for slot_r in range(3):
            (r0, t0), (r1, t1) = position(slot_t, slot_r)
            r, t = jnp.where(core == 0, r0, r1), jnp.where(core == 0, t0, t1)
            seen = jnp.where(
                qc,
                jnp.where(kc, allowed(1, r, 2 * t + 1), allowed(1, r, 2 * t)),
                jnp.where(kc, allowed(0, r, 2 * t + 1), allowed(0, r, 2 * t)),
            )
            j = 3 * slot_t + slot_r
            bias_ref[:, j * T : (j + 1) * T] = (1.0 - seen) * OFF
    own = slice(4 * T, 5 * T)
    lanes = lax.broadcasted_iota(jnp.int32, (T, T), 1)
    stats = jnp.zeros((T, T), F32)
    for e in range(H):
        a, b = window(K0 + HD * e)
        q = head_only(win_ref[own, Q0 + a : Q0 + b], HD * e, a) if Q0 + b <= QKV else head_only(
            jnp.concatenate([win_ref[own, Q0 + a : QKV], jnp.zeros((T, Q0 + b - QKV), BF)], axis=1), HD * e, a)
        s = nt(q, win_ref[:, a:b]) * SCALE2 + bias_ref[...]
        peak = jnp.max(s, axis=1, keepdims=True)
        p = jnp.exp2(s - peak)
        total = jnp.sum(p, axis=1, keepdims=True)
        low = p.astype(BF)
        e_ref[e * T : (e + 1) * T, :] = low
        inv = 1.0 / total
        stats = jnp.where(lanes == e, peak + jnp.log2(total), stats)
        stats = jnp.where(lanes == 16 + e, inv, stats)
        a, b = window(V0 + HD * e)
        o = nn(low, win_ref[:, a:b]) * inv
        acc_ref[:, a - VB : b - VB] += head_only(o, V0 + HD * e, a)

    att = acc_ref[...].astype(BF)
    den = (x_ref[...].astype(F32) + nn(att, wn_ref[...])).astype(BF)
    den_ref[...] = den
    colors = nt(den, wpix_ref[...])
    filt = filt_ref[...]
    misfit = -meas_ref[...]
    for c in range(3):
        misfit = misfit + jnp.where(filt == c, colors[:, 64 * c : 64 * c + 64], 0.0)
    spread = jnp.concatenate([jnp.where(filt == c, misfit, 0.0) for c in range(3)], axis=1).astype(BF)
    og = nn(spread, wpix_ref[...])
    og_ref[...] = og
    up = nt(og.astype(BF), wn_ref[...]).astype(BF)
    pack_ref[0:T, :] = up
    prod = up.astype(F32) * att.astype(F32)
    for e in range(H):
        a, b = window(V0 + HD * e)
        inner = jnp.sum(head_only(prod[:, a - VB : b - VB], V0 + HD * e, a), axis=1, keepdims=True)
        stats = jnp.where(lanes == 8 + e, inner, stats)
    stat_ref[...] = stats
    turned = stats.T[0:16, :]
    high = turned.astype(BF)
    rest = turned - high.astype(F32)
    mid = rest.astype(BF)
    low = (rest - mid.astype(F32)).astype(BF)
    pack_ref[T : T + 16, :] = jnp.concatenate(
        [
            high, mid, low, jnp.concatenate(rows[:16], axis=0).astype(BF),
            jnp.concatenate(rows[16:] + [jnp.zeros((14, T), F32)], axis=0).astype(BF),
        ],
        axis=1,
    )


def query_kernel(win_ref, e_ref, up_ref, stat_ref, gq_ref, acc_ref):
    acc_ref[...] = jnp.zeros_like(acc_ref)
    for e in range(H):
        a, b = window(V0 + HD * e)
        up = head_only(up_ref[0:T, a - VB : b - VB], V0 + HD * e, a)
        dprob = nt(up, win_ref[:, a:b])
        p = e_ref[e * T : (e + 1) * T, :].astype(F32)
        ds = (p * (dprob - stat_ref[:, 8 + e : 9 + e])).astype(BF)
        a, b = window(K0 + HD * e)
        dq = nn(ds, win_ref[:, a:b]) * (stat_ref[:, 16 + e : 17 + e] * FACTOR)
        acc_ref[:, a:b] += head_only(dq, HD * e, a)
    gq_ref[...] = acc_ref[:, 0:HW].astype(BF)


def key_side(core_ref, win_ref, tiles, gk_ref, gv_ref):
    own = slice(4 * T, 5 * T)
    kc = (lax.broadcasted_iota(jnp.int32, (T, T), 0) & 8) > 0
    second = core_ref[0].astype(F32)
    bias, stats, ups = [], [], []
    for t, r, pack_ref, base in tiles:
        ups.append(pack_ref[base : base + T, :])
        extra = pack_ref[base + T : base + T + 16, :].astype(F32)
        stats.append(extra[:, 0:128] + extra[:, 128:256] + extra[:, 256:384])
        seen = []
        for w in range(2):
            on = []
            for row, col in position(t, r):
                i = (2 - row) * 6 + (2 - col) * 2 + w
                on.append(extra[i : i + 1, 384:512] if i < 16 else extra[i - 16 : i - 15, 512:640])
            seen.append(on[0] * (1.0 - second) + on[1] * second)
        bias.append((1.0 - jnp.where(kc, seen[1], seen[0])) * OFF)
    bias = jnp.concatenate(bias, axis=1)
    stats = jnp.concatenate(stats, axis=1)
    ups = jnp.concatenate(ups, axis=0)
    count = len(tiles) * T

    def queries(a, b):
        return jnp.concatenate(
            [win_ref[(3 * t + r) * T : (3 * t + r + 1) * T, Q0 + a : Q0 + b] for t, r, _, _ in tiles], axis=0
        )

    for e in range(H):
        a, b = window(K0 + HD * e)
        if Q0 + b <= QKV:
            q = queries(a, b)
        else:
            q = jnp.concatenate([queries(a, HW), jnp.zeros((count, b - HW), BF)], axis=1)
        k = head_only(win_ref[own, a:b], HD * e, a)
        s = nt(k, q) * SCALE2 + bias
        p = jnp.exp2(s - stats[e : e + 1, :])
        c, d = window(V0 + HD * e)
        v = head_only(win_ref[own, c:d], V0 + HD * e, c)
        up = ups[:, c - VB : d - VB]
        ds = (p * (nt(v, up) - stats[8 + e : 9 + e, :])).astype(BF)
        gk_ref[:, a:b] += head_only(nn(ds, q), HD * e, a)
        gv_ref[:, c - VB : d - VB] += head_only(nn(p.astype(BF), up), V0 + HD * e, c)


def key_near_kernel(core_ref, win_ref, own_ref, before_ref, after_ref, outer_ref, inner_ref, gk_ref, gv_ref):
    gk_ref[...] = jnp.zeros_like(gk_ref)
    gv_ref[...] = jnp.zeros_like(gv_ref)
    tiles = (
        (1, 0, before_ref, 0), (1, 1, own_ref, 0), (1, 2, after_ref, 0), (0, 1, outer_ref, 0), (2, 1, inner_ref, 0)
    )
    key_side(core_ref, win_ref, tiles, gk_ref, gv_ref)


def finish_kernel(
    core_ref, win_ref, packo_ref, packi_ref, gk0_ref, gv0_ref, gq_ref, order_ref, x_ref, gain_ref, og_ref,
    b0, b1, b2, b3, b4, b5, b6, b7,
    out_ref, gk_ref, gv_ref, w_ref,
):
    collect((b0, b1, b2, b3, b4, b5, b6, b7), 0, 144, w_ref)
    gk_ref[...] = gk0_ref[...]
    gv_ref[...] = gv0_ref[...]
    tiles = ((0, 0, packo_ref, 0), (0, 2, packo_ref, 144), (2, 0, packi_ref, 0), (2, 2, packi_ref, 144))
    key_side(core_ref, win_ref, tiles, gk_ref, gv_ref)
    gk = (gk_ref[:, 0:HW] * FACTOR).astype(BF)
    gv = gv_ref[:, 64:640].astype(BF)
    grads = jnp.concatenate([gk, gv, gq_ref[...]], axis=1)
    moved = nt(grads, w_ref[...])
    high = moved.astype(BF)
    low = (moved - high.astype(F32)).astype(BF)
    both = nt(jnp.concatenate([high, low], axis=0), order_ref[...])
    grad = (both[0:T, :] + both[T : 2 * T, :]) * gain_ref[...]
    center, rstd = norm_parts(x_ref[...].astype(F32))
    xhat = center * rstd
    mean_g = jnp.mean(grad, axis=-1, keepdims=True)
    mean_gx = jnp.mean(grad * xhat, axis=-1, keepdims=True)
    out_ref[...] = rstd * (grad - mean_g - xhat * mean_gx) + og_ref[...]


def shaped(shape, dtype=BF):
    return jax.ShapeDtypeStruct(shape, dtype)


def shards_held(yh, z, x, core, block, second):
    cs = core ^ jnp.asarray((block >= 4).astype(np.int32))
    shift = np.array([0, 3, 1, 2] * 2)[block]
    xs = (x + jnp.where(cs == 0, jnp.asarray(shift), jnp.asarray(-shift))) & 3
    hops = jnp.where(second, 3 - xs, xs + 1)
    zs = (z + jnp.where(cs == 0, -hops, hops)) & 7
    other = jnp.logical_xor(second, (xs == 3) & (cs == 1)).astype(jnp.int32)
    return (yh ^ other) * 8 + zs


def weight_targets(yh, z, x, core):
    place = np.arange(D)
    block, row = place // 144, place % 144
    held = shards_held(yh, z, x, core, block, row >= 72)
    return (held * 72 + row % 72).astype(jnp.int32).reshape(1, D)


def out_targets(yh, z, x, core):
    place = np.arange(384)
    block, row = place // 48, place % 48
    held = shards_held(yh, z, x, core, block, row >= 24) * 36 + 64
    row = row % 24
    whole = held + row
    lower = jnp.where(row < 12, held + 24 + row, -1)
    upper = jnp.where(row >= 12, held + 12 + row, -1)
    return jnp.stack([whole, lower, upper]).astype(jnp.int32)


def device(yh, z, yl, x, core):
    return (((yh * 8 + z % 8) * 4 + yl) * 4 + x) * 2 + core


def fetch_routes():
    first, second = [], []
    for yh in range(2):
        for z in range(8):
            for yl in range(4):
                for x in range(4):
                    for core in range(2):
                        me = device(yh, z, yl, x, core)
                        way = 1 if core else -1
                        near, far = z + way * (x + 1), z + way * (3 - x)
                        if x == 3 and core == 1:
                            first.append((device(1 - yh, near, 3 - yl, x, core), me))
                            second.append((me, me))
                        else:
                            first.append((device(yh, near, yl, x, core), me))
                            second.append((device(1 - yh, far, 3 - yl, x, core), me))
    return first, second


def on_device(tokens, gain, w_query, w_key, w_value, w_out, w_pixel, measured, filter_color, block_mask):
    yh, z, xi, core = (lax.axis_index(n) for n in ("yh", "z", "x", "core"))
    which = core.reshape(1).astype(jnp.int32)
    x = tokens.reshape(T, D)
    gain = gain.reshape(1, D)
    south = [(2 * i, 2 * i + 2) for i in range(15)] + [(2 * i + 3, 2 * i + 1) for i in range(15)]
    north = [(j, i) for i, j in south]
    ring = [(2 * i, (2 * i + 2) % 8) for i in range(4)] + [((2 * i + 3) % 8, 2 * i + 1) for i in range(4)]
    back = [(j, i) for i, j in ring]
    border = [(2 * i + 1, (2 * i + 2) % 32) for i in range(16)]
    border = border + [(j, i) for i, j in border]
    lat, lon = ("yh", "z"), ("yl", "x", "core")
    first, second = fetch_routes()

    def swap(v):
        return lax.ppermute(v, "core", [(0, 1), (1, 0)])

    def along(v, perm):
        return lax.ppermute(v, ("x", "core"), perm)

    def rows_beside(own):
        return lax.ppermute(own, lat + ("core",), south), lax.ppermute(own, lat + ("core",), north)

    def sides(column):
        return lax.ppermute(column, lon, border), swap(column)

    def placed(v, rows, cols):
        return lax.pad(v, jnp.zeros((), BF), ((*rows, 0), (*cols, 0)))

    at_row = lax.broadcasted_iota(jnp.int32, (96, QKV), 0)
    at_col = lax.broadcasted_iota(jnp.int32, (96, QKV), 1)
    lefts = placed(w_out, (48, 12), (D, -HW))
    rights = placed(w_out, (60, 0), (HW, 0))
    mine = (
        placed(w_key, (0, 24), (0, 2 * HW)) + placed(w_value, (0, 24), (HW, HW))
        + placed(w_query, (0, 24), (2 * HW, 0)) + placed(w_out, (72, -12), (0, HW))
        + jnp.where(at_row >= 72, lefts, 0) + jnp.where((at_row >= 84) & (at_col >= D), rights, 0)
    )
    one, two = lax.ppermute(mine, lat + lon, first), lax.ppermute(mine, lat + lon, second)
    fetched = jnp.concatenate([one[:72], two[:72], one[72:], two[72:]], axis=0)
    before, after = rows_beside(x)
    column = jnp.concatenate([before, x, after], axis=0)
    outer, inner = sides(column)
    target = weight_targets(yh, z, xi, core)

    def ordering(target):
        return pl.pallas_call(
            order_kernel, out_shape=shaped((D, D)), in_specs=[VMEM], out_specs=VMEM, compiler_params=params(8),
            cost_estimate=pl.CostEstimate(flops=2_000_000_000, bytes_accessed=3_000_000, transcendentals=0),
        )(target)


    def hidden(v):
        return pl.pallas_call(
            hidden_kernel, out_shape=shaped((3 * T, D)), in_specs=[VMEM] * 3, out_specs=VMEM,
            scratch_shapes=[pltpu.VMEM((D, D), BF)], compiler_params=params(16),
            cost_estimate=pl.CostEstimate(flops=3_000_000_000, bytes_accessed=5_000_000, transcendentals=0),
        )(v, gain, target)

    fetched, hc = lax.optimization_barrier((fetched, hidden(column)))
    right, left = along(fetched, ring), along(fetched, back)
    right, left, he, outer = lax.optimization_barrier((right, left, hidden(inner), outer))
    fetched_too = swap(fetched)
    across, hw = lax.optimization_barrier((along(right, ring), hidden(outer)))
    blocks = (fetched, right, left, across, fetched_too, swap(right), swap(left), swap(across))

    win, wn = pl.pallas_call(
        project_kernel, out_shape=(shaped((9 * T, QKV)), shaped((640, D))),
        in_specs=[VMEM] * 12, out_specs=(VMEM,) * 2,
        scratch_shapes=[pltpu.VMEM((384, QKV), BF), pltpu.VMEM((D, QKV), BF)],
        compiler_params=params(24),
        cost_estimate=pl.CostEstimate(flops=6_000_000_000, bytes_accessed=8_000_000, transcendentals=0),
    )(out_targets(yh, z, xi, core), hw, hc, he, *blocks)
    e, den, og, pack, stat = pl.pallas_call(
        forward_kernel,
        out_shape=(
            shaped((H * T, 9 * T)), shaped((T, D)), shaped((T, D), F32), shaped((144, 640)), shaped((T, T), F32),
        ),
        in_specs=[SMEM] + [VMEM] * 6, out_specs=(VMEM,) * 5,
        scratch_shapes=[pltpu.VMEM((T, 9 * T), F32), pltpu.VMEM((T, 640), F32)],
        compiler_params=params(18),
        cost_estimate=pl.CostEstimate(flops=6_000_000_000, bytes_accessed=8_000_000, transcendentals=1_000_000),
    )(jnp.concatenate([block_mask.reshape(30), which]), win, wn, w_pixel.T, x, measured.reshape(T, 64), filter_color.reshape(T, 64))
    before, after = rows_beside(pack)
    near_outer, near_inner = sides(pack)
    corners, target, stat_late = lax.optimization_barrier((jnp.concatenate([before, after], axis=0), target, stat))
    packs_outer, packs_inner = sides(corners)
    gq = pl.pallas_call(
        query_kernel, out_shape=shaped((T, HW)), in_specs=[VMEM] * 4, out_specs=VMEM,
        scratch_shapes=[pltpu.VMEM((T, 640), F32)], compiler_params=params(16),
        cost_estimate=pl.CostEstimate(flops=4_000_000_000, bytes_accessed=6_000_000, transcendentals=0),
    )(win, e, pack, stat_late)
    gk, gv = pl.pallas_call(
        key_near_kernel, out_shape=(shaped((T, 640), F32),) * 2, in_specs=[SMEM] + [VMEM] * 6, out_specs=(VMEM,) * 2,
        compiler_params=params(16),
        cost_estimate=pl.CostEstimate(flops=4_000_000_000, bytes_accessed=6_000_000, transcendentals=0),
    )(which, win, pack, before, after, near_outer, near_inner)
    guidance = pl.pallas_call(
        finish_kernel, out_shape=shaped((T, D), F32), in_specs=[SMEM] + [VMEM] * 18, out_specs=VMEM,
        scratch_shapes=[pltpu.VMEM((T, 640), F32)] * 2 + [pltpu.VMEM((D, QKV), BF)],
        compiler_params=params(20),
    )(which, win, packs_outer, packs_inner, gk, gv, gq, ordering(target), x, gain, og, *blocks)
    return den.reshape(tokens.shape), guidance.reshape(tokens.shape)


def solution(mesh):
    split = Mesh(mesh.devices.reshape(2, 8, 4, 4, 2), ("yh", "z", "yl", "x", "core"))
    lat, lon = ("yh", "z"), ("yl", "x", "core")
    return jax.shard_map(
        on_device,
        mesh=split,
        in_specs=(
            P(lat, lon, None), P(), P(lat, None), P(lat, None), P(lat, None), P(lat, None), P(),
            P(lat, lon, None), P(lat, lon, None), P(lat, lon, None, None),
        ),
        out_specs=(P(lat, lon, None), P(lat, lon, None)),
        check_vma=False,
    )
```

```python
import functools

import jax
import jax.numpy as jnp
import numpy as np
from jax import lax
from jax.experimental import pallas as pl
from jax.experimental.pallas import tpu as pltpu
from jax.sharding import Mesh, PartitionSpec as P

H = 8
HD = 72
HW = 576
D = 1152
T = 128
QKV = 3 * HW
FACTOR = HD ** (-0.5)
SCALE2 = FACTOR * 1.4426950408889634
OFF = -1e30
BF = jnp.bfloat16
F32 = jnp.float32
VMEM = pl.BlockSpec(memory_space=pltpu.VMEM)
SMEM = pl.BlockSpec(memory_space=pltpu.SMEM)
ANY = pl.BlockSpec(memory_space=pl.ANY)
HBM = pl.BlockSpec(memory_space=pltpu.HBM)
K0, V0, Q0 = 0, HW, 2 * HW
VB = 512


def params(limit=40):
    return pltpu.CompilerParams(vmem_limit_bytes=limit * 1024 * 1024)


def nt(left, right):
    return lax.dot_general(left, right, (((1,), (1,)), ((), ())), preferred_element_type=F32)


def nn(left, right):
    return jnp.dot(left, right, preferred_element_type=F32)


def window(first):
    return first // 128 * 128, -(-(first + HD) // 128) * 128


def head_only(x, first, start):
    lane = lax.broadcasted_iota(jnp.int32, x.shape, 1) + start
    return jnp.where((lane >= first) & (lane < first + HD), x, jnp.zeros_like(x))


def norm_parts(x):
    center = x - jnp.mean(x, axis=-1, keepdims=True)
    rstd = lax.rsqrt(jnp.mean(center * center, axis=-1, keepdims=True) + 1e-6)
    return center, rstd


def order_kernel(target_ref, order_ref):
    rows = lax.broadcasted_iota(jnp.int32, (D, D), 0)
    order_ref[...] = jnp.where(rows == target_ref[...], 1.0, 0.0).astype(BF)


def hidden_kernel(x_ref, gain_ref, target_ref, out_ref, order_ref):
    order_kernel(target_ref, order_ref)
    for i in range(x_ref.shape[0] // T):
        center, rstd = norm_parts(x_ref[i * T : (i + 1) * T, :].astype(F32))
        hidden = (center * rstd * gain_ref[...]).astype(BF)
        out_ref[i * T : (i + 1) * T, :] = nn(hidden, order_ref[...]).astype(BF)


def collect(blocks, first, rows, w_ref):
    for i, block in enumerate(blocks):
        w_ref[rows * i : rows * (i + 1), :] = block[first : first + rows, :]


def position(slot_t, slot_r):
    turned = 2 - slot_r
    return (slot_r if slot_t == 1 else turned, slot_t), (turned if slot_t == 1 else slot_r, 2 - slot_t)


def project_kernel(
    place_ref, hw_ref, hc_ref, he_ref, b0, b1, b2, b3, b4, b5, b6, b7, win_ref, wn_ref, wo_ref, w_ref
):
    collect((b0, b1, b2, b3, b4, b5, b6, b7), 144, 48, wo_ref)
    collect((b0, b1, b2, b3, b4, b5, b6, b7), 0, 144, w_ref)
    for g, h_ref in enumerate((hw_ref, hc_ref, he_ref)):
        for part in range(3):
            s = slice(part * T, (part + 1) * T)
            win_ref[(g * 3 + part) * T : (g * 3 + part + 1) * T, :] = nn(h_ref[s, :], w_ref[...]).astype(BF)
    lane_of = lax.broadcasted_iota(jnp.int32, (640, 384), 0)
    whole, lower, upper = (
        jnp.where(lane_of == place_ref[i : i + 1, :], 1.0, 0.0).astype(BF) for i in range(3)
    )
    halves = wo_ref[:, D:QKV]
    wn_ref[...] = (
        nn(whole, wo_ref[:, 0:D]) + jnp.concatenate([nn(lower, halves), nn(upper, halves)], axis=1)
    ).astype(BF)


def forward_kernel(
    blocks_ref, win_ref, wn_ref, wpix_ref, x_ref, meas_ref, filt_ref,
    e_ref, den_ref, og_ref, pack_ref, stat_ref,
    bias_ref, acc_ref,
):
    acc_ref[...] = jnp.zeros_like(acc_ref)

    qc = (lax.broadcasted_iota(jnp.int32, (T, T), 0) & 8) > 0
    kc = (lax.broadcasted_iota(jnp.int32, (T, T), 1) & 8) > 0

    core = blocks_ref[30]

    def allowed(c, r, w):
        there = jnp.logical_and(w - c >= 0, w - c < 5)
        value = blocks_ref[(c * 3 + r) * 5 + jnp.clip(w - c, 0, 4)]
        return jnp.where(there, value, 0).astype(F32)

    lane_c = (lax.broadcasted_iota(jnp.int32, (1, T), 1) & 8) > 0
    rows = []
    for r in range(3):
        for w in range(6):
            rows.append(jnp.where(lane_c, allowed(1, r, jnp.int32(w)), allowed(0, r, jnp.int32(w))))
    for slot_t in range(3):
        for slot_r in range(3):
            (r0, t0), (r1, t1) = position(slot_t, slot_r)
            r, t = jnp.where(core == 0, r0, r1), jnp.where(core == 0, t0, t1)
            seen = jnp.where(
                qc,
                jnp.where(kc, allowed(1, r, 2 * t + 1), allowed(1, r, 2 * t)),
                jnp.where(kc, allowed(0, r, 2 * t + 1), allowed(0, r, 2 * t)),
            )
            j = 3 * slot_t + slot_r
            bias_ref[:, j * T : (j + 1) * T] = (1.0 - seen) * OFF
    own = slice(4 * T, 5 * T)
    lanes = lax.broadcasted_iota(jnp.int32, (T, T), 1)
    stats = jnp.zeros((T, T), F32)
    for e in range(H):
        a, b = window(K0 + HD * e)
        q = head_only(win_ref[own, Q0 + a : Q0 + b], HD * e, a) if Q0 + b <= QKV else head_only(
            jnp.concatenate([win_ref[own, Q0 + a : QKV], jnp.zeros((T, Q0 + b - QKV), BF)], axis=1), HD * e, a)
        s = nt(q, win_ref[:, a:b]) * SCALE2 + bias_ref[...]
        peak = jnp.max(s, axis=1, keepdims=True)
        p = jnp.exp2(s - peak)
        total = jnp.sum(p, axis=1, keepdims=True)
        low = p.astype(BF)
        e_ref[e * T : (e + 1) * T, :] = low
        inv = 1.0 / total
        stats = jnp.where(lanes == e, peak + jnp.log2(total), stats)
        stats = jnp.where(lanes == 16 + e, inv, stats)
        a, b = window(V0 + HD * e)
        o = nn(low, win_ref[:, a:b]) * inv
        acc_ref[:, a - VB : b - VB] += head_only(o, V0 + HD * e, a)

    att = acc_ref[...].astype(BF)
    den = (x_ref[...].astype(F32) + nn(att, wn_ref[...])).astype(BF)
    den_ref[...] = den
    colors = nt(den, wpix_ref[...])
    filt = filt_ref[...]
    misfit = -meas_ref[...]
    for c in range(3):
        misfit = misfit + jnp.where(filt == c, colors[:, 64 * c : 64 * c + 64], 0.0)
    spread = jnp.concatenate([jnp.where(filt == c, misfit, 0.0) for c in range(3)], axis=1).astype(BF)
    og = nn(spread, wpix_ref[...])
    og_ref[...] = og
    up = nt(og.astype(BF), wn_ref[...]).astype(BF)
    pack_ref[0:T, :] = up
    prod = up.astype(F32) * att.astype(F32)
    for e in range(H):
        a, b = window(V0 + HD * e)
        inner = jnp.sum(head_only(prod[:, a - VB : b - VB], V0 + HD * e, a), axis=1, keepdims=True)
        stats = jnp.where(lanes == 8 + e, inner, stats)
    stat_ref[...] = stats
    turned = stats.T[0:16, :]
    high = turned.astype(BF)
    rest = turned - high.astype(F32)
    mid = rest.astype(BF)
    low = (rest - mid.astype(F32)).astype(BF)
    pack_ref[T : T + 16, :] = jnp.concatenate(
        [
            high, mid, low, jnp.concatenate(rows[:16], axis=0).astype(BF),
            jnp.concatenate(rows[16:] + [jnp.zeros((14, T), F32)], axis=0).astype(BF),
        ],
        axis=1,
    )


def query_kernel(win_ref, e_ref, up_ref, stat_ref, gq_ref, acc_ref):
    acc_ref[...] = jnp.zeros_like(acc_ref)
    for e in range(H):
        a, b = window(V0 + HD * e)
        up = head_only(up_ref[0:T, a - VB : b - VB], V0 + HD * e, a)
        dprob = nt(up, win_ref[:, a:b])
        p = e_ref[e * T : (e + 1) * T, :].astype(F32)
        ds = (p * (dprob - stat_ref[:, 8 + e : 9 + e])).astype(BF)
        a, b = window(K0 + HD * e)
        dq = nn(ds, win_ref[:, a:b]) * (stat_ref[:, 16 + e : 17 + e] * FACTOR)
        acc_ref[:, a:b] += head_only(dq, HD * e, a)
    gq_ref[...] = acc_ref[:, 0:HW].astype(BF)


def key_side(core_ref, win_ref, tiles, gk_ref, gv_ref):
    own = slice(4 * T, 5 * T)
    kc = (lax.broadcasted_iota(jnp.int32, (T, T), 0) & 8) > 0
    second = core_ref[0].astype(F32)
    bias, stats, ups = [], [], []
    for t, r, pack_ref, base in tiles:
        ups.append(pack_ref[base : base + T, :])
        extra = pack_ref[base + T : base + T + 16, :].astype(F32)
        stats.append(extra[:, 0:128] + extra[:, 128:256] + extra[:, 256:384])
        seen = []
        for w in range(2):
            on = []
            for row, col in position(t, r):
                i = (2 - row) * 6 + (2 - col) * 2 + w
                on.append(extra[i : i + 1, 384:512] if i < 16 else extra[i - 16 : i - 15, 512:640])
            seen.append(on[0] * (1.0 - second) + on[1] * second)
        bias.append((1.0 - jnp.where(kc, seen[1], seen[0])) * OFF)
    bias = jnp.concatenate(bias, axis=1)
    stats = jnp.concatenate(stats, axis=1)
    ups = jnp.concatenate(ups, axis=0)
    count = len(tiles) * T

    def queries(a, b):
        return jnp.concatenate(
            [win_ref[(3 * t + r) * T : (3 * t + r + 1) * T, Q0 + a : Q0 + b] for t, r, _, _ in tiles], axis=0
        )

    for e in range(H):
        a, b = window(K0 + HD * e)
        if Q0 + b <= QKV:
            q = queries(a, b)
        else:
            q = jnp.concatenate([queries(a, HW), jnp.zeros((count, b - HW), BF)], axis=1)
        k = head_only(win_ref[own, a:b], HD * e, a)
        s = nt(k, q) * SCALE2 + bias
        p = jnp.exp2(s - stats[e : e + 1, :])
        c, d = window(V0 + HD * e)
        v = head_only(win_ref[own, c:d], V0 + HD * e, c)
        up = ups[:, c - VB : d - VB]
        ds = (p * (nt(v, up) - stats[8 + e : 9 + e, :])).astype(BF)
        gk_ref[:, a:b] += head_only(nn(ds, q), HD * e, a)
        gv_ref[:, c - VB : d - VB] += head_only(nn(p.astype(BF), up), V0 + HD * e, c)


def key_near_kernel(core_ref, win_ref, own_ref, before_ref, after_ref, outer_ref, inner_ref, gk_ref, gv_ref):
    gk_ref[...] = jnp.zeros_like(gk_ref)
    gv_ref[...] = jnp.zeros_like(gv_ref)
    tiles = (
        (1, 0, before_ref, 0), (1, 1, own_ref, 0), (1, 2, after_ref, 0), (0, 1, outer_ref, 0), (2, 1, inner_ref, 0)
    )
    key_side(core_ref, win_ref, tiles, gk_ref, gv_ref)


def finish_kernel(
    core_ref, win_ref, packo_ref, packi_ref, gk0_ref, gv0_ref, gq_ref, order_ref, x_ref, gain_ref, og_ref,
    b0, b1, b2, b3, b4, b5, b6, b7,
    out_ref, gk_ref, gv_ref, w_ref,
):
    collect((b0, b1, b2, b3, b4, b5, b6, b7), 0, 144, w_ref)
    gk_ref[...] = gk0_ref[...]
    gv_ref[...] = gv0_ref[...]
    tiles = ((0, 0, packo_ref, 0), (0, 2, packo_ref, 144), (2, 0, packi_ref, 0), (2, 2, packi_ref, 144))
    key_side(core_ref, win_ref, tiles, gk_ref, gv_ref)
    gk = (gk_ref[:, 0:HW] * FACTOR).astype(BF)
    gv = gv_ref[:, 64:640].astype(BF)
    grads = jnp.concatenate([gk, gv, gq_ref[...]], axis=1)
    moved = nt(grads, w_ref[...])
    high = moved.astype(BF)
    low = (moved - high.astype(F32)).astype(BF)
    both = nt(jnp.concatenate([high, low], axis=0), order_ref[...])
    grad = (both[0:T, :] + both[T : 2 * T, :]) * gain_ref[...]
    center, rstd = norm_parts(x_ref[...].astype(F32))
    xhat = center * rstd
    mean_g = jnp.mean(grad, axis=-1, keepdims=True)
    mean_gx = jnp.mean(grad * xhat, axis=-1, keepdims=True)
    out_ref[...] = rstd * (grad - mean_g - xhat * mean_gx) + og_ref[...]


def shaped(shape, dtype=BF):
    return jax.ShapeDtypeStruct(shape, dtype)


def shards_held(yh, z, x, core, block, second):
    cs = core ^ jnp.asarray((block >= 4).astype(np.int32))
    shift = np.array([0, 3, 1, 2] * 2)[block]
    xs = (x + jnp.where(cs == 0, jnp.asarray(shift), jnp.asarray(-shift))) & 3
    hops = jnp.where(second, 3 - xs, xs + 1)
    zs = (z + jnp.where(cs == 0, -hops, hops)) & 7
    other = jnp.logical_xor(second, (xs == 3) & (cs == 1)).astype(jnp.int32)
    return (yh ^ other) * 8 + zs


def weight_targets(yh, z, x, core):
    place = np.arange(D)
    block, row = place // 144, place % 144
    held = shards_held(yh, z, x, core, block, row >= 72)
    return (held * 72 + row % 72).astype(jnp.int32).reshape(1, D)


def out_targets(yh, z, x, core):
    place = np.arange(384)
    block, row = place // 48, place % 48
    held = shards_held(yh, z, x, core, block, row >= 24) * 36 + 64
    row = row % 24
    whole = held + row
    lower = jnp.where(row < 12, held + 24 + row, -1)
    upper = jnp.where(row >= 12, held + 12 + row, -1)
    return jnp.stack([whole, lower, upper]).astype(jnp.int32)


def device(yh, z, yl, x, core):
    return (((yh * 8 + z % 8) * 4 + yl) * 4 + x) * 2 + core


def fetch_routes():
    first, second = [], []
    for yh in range(2):
        for z in range(8):
            for yl in range(4):
                for x in range(4):
                    for core in range(2):
                        me = device(yh, z, yl, x, core)
                        way = 1 if core else -1
                        near, far = z + way * (x + 1), z + way * (3 - x)
                        if x == 3 and core == 1:
                            first.append((device(1 - yh, near, 3 - yl, x, core), me))
                            second.append((me, me))
                        else:
                            first.append((device(yh, near, yl, x, core), me))
                            second.append((device(1 - yh, far, 3 - yl, x, core), me))
    return first, second


def on_device(tokens, gain, w_query, w_key, w_value, w_out, w_pixel, measured, filter_color, block_mask):
    yh, z, xi, core = (lax.axis_index(n) for n in ("yh", "z", "x", "core"))
    which = core.reshape(1).astype(jnp.int32)
    x = tokens.reshape(T, D)
    gain = gain.reshape(1, D)
    south = [(2 * i, 2 * i + 2) for i in range(15)] + [(2 * i + 3, 2 * i + 1) for i in range(15)]
    north = [(j, i) for i, j in south]
    ring = [(2 * i, (2 * i + 2) % 8) for i in range(4)] + [((2 * i + 3) % 8, 2 * i + 1) for i in range(4)]
    back = [(j, i) for i, j in ring]
    border = [(2 * i + 1, (2 * i + 2) % 32) for i in range(16)]
    border = border + [(j, i) for i, j in border]
    lat, lon = ("yh", "z"), ("yl", "x", "core")
    first, second = fetch_routes()

    def swap(v):
        return lax.ppermute(v, "core", [(0, 1), (1, 0)])

    def along(v, perm):
        return lax.ppermute(v, ("x", "core"), perm)

    def rows_beside(own):
        return lax.ppermute(own, lat + ("core",), south), lax.ppermute(own, lat + ("core",), north)

    def sides(column):
        return lax.ppermute(column, lon, border), swap(column)

    def placed(v, rows, cols):
        return lax.pad(v, jnp.zeros((), BF), ((*rows, 0), (*cols, 0)))

    at_row = lax.broadcasted_iota(jnp.int32, (96, QKV), 0)
    at_col = lax.broadcasted_iota(jnp.int32, (96, QKV), 1)
    lefts = placed(w_out, (48, 12), (D, -HW))
    rights = placed(w_out, (60, 0), (HW, 0))
    mine = (
        placed(w_key, (0, 24), (0, 2 * HW)) + placed(w_value, (0, 24), (HW, HW))
        + placed(w_query, (0, 24), (2 * HW, 0)) + placed(w_out, (72, -12), (0, HW))
        + jnp.where(at_row >= 72, lefts, 0) + jnp.where((at_row >= 84) & (at_col >= D), rights, 0)
    )
    one, two = lax.ppermute(mine, lat + lon, first), lax.ppermute(mine, lat + lon, second)
    before, after = rows_beside(x)
    column = jnp.concatenate([before, x, after], axis=0)
    outer, inner = sides(column)
    target = weight_targets(yh, z, xi, core)

    def ordering(target):
        return pl.pallas_call(
            order_kernel, out_shape=shaped((D, D)), in_specs=[VMEM], out_specs=VMEM, compiler_params=params(8),
            cost_estimate=pl.CostEstimate(flops=2_000_000_000, bytes_accessed=3_000_000, transcendentals=0),
        )(target)


    def hidden(v):
        return pl.pallas_call(
            hidden_kernel, out_shape=shaped((3 * T, D)), in_specs=[VMEM] * 3, out_specs=VMEM,
            scratch_shapes=[pltpu.VMEM((D, D), BF)], compiler_params=params(16),
            cost_estimate=pl.CostEstimate(flops=3_000_000_000, bytes_accessed=5_000_000, transcendentals=0),
        )(v, gain, target)

    two, hc = lax.optimization_barrier((two, hidden(column)))

    def block(p, q):
        return jnp.concatenate([p[:72], q[:72], p[72:], q[72:]], axis=0)

    right_one, left_one = along(one, ring), along(one, back)
    right_two, left_two = along(two, ring), along(two, back)
    across_one = along(right_one, ring)
    right_two, left_two, he, outer = lax.optimization_barrier((right_two, left_two, hidden(inner), outer))
    across_two, hw = lax.optimization_barrier((along(right_two, ring), hidden(outer)))
    held = (block(one, two), block(right_one, right_two), block(left_one, left_two), block(across_one, across_two))
    blocks = held + tuple(swap(v) for v in held)

    win, wn = pl.pallas_call(
        project_kernel, out_shape=(shaped((9 * T, QKV)), shaped((640, D))),
        in_specs=[VMEM] * 12, out_specs=(VMEM,) * 2,
        scratch_shapes=[pltpu.VMEM((384, QKV), BF), pltpu.VMEM((D, QKV), BF)],
        compiler_params=params(24),
        cost_estimate=pl.CostEstimate(flops=6_000_000_000, bytes_accessed=8_000_000, transcendentals=0),
    )(out_targets(yh, z, xi, core), hw, hc, he, *blocks)
    e, den, og, pack, stat = pl.pallas_call(
        forward_kernel,
        out_shape=(
            shaped((H * T, 9 * T)), shaped((T, D)), shaped((T, D), F32), shaped((144, 640)), shaped((T, T), F32),
        ),
        in_specs=[SMEM] + [VMEM] * 6, out_specs=(VMEM,) * 5,
        scratch_shapes=[pltpu.VMEM((T, 9 * T), F32), pltpu.VMEM((T, 640), F32)],
        compiler_params=params(18),
        cost_estimate=pl.CostEstimate(flops=6_000_000_000, bytes_accessed=8_000_000, transcendentals=1_000_000),
    )(jnp.concatenate([block_mask.reshape(30), which]), win, wn, w_pixel.T, x, measured.reshape(T, 64), filter_color.reshape(T, 64))
    before, after = rows_beside(pack)
    near_outer, near_inner = sides(pack)
    corners, target, stat_late = lax.optimization_barrier((jnp.concatenate([before, after], axis=0), target, stat))
    packs_outer, packs_inner = sides(corners)
    gq = pl.pallas_call(
        query_kernel, out_shape=shaped((T, HW)), in_specs=[VMEM] * 4, out_specs=VMEM,
        scratch_shapes=[pltpu.VMEM((T, 640), F32)], compiler_params=params(16),
        cost_estimate=pl.CostEstimate(flops=4_000_000_000, bytes_accessed=6_000_000, transcendentals=0),
    )(win, e, pack, stat_late)
    gk, gv = pl.pallas_call(
        key_near_kernel, out_shape=(shaped((T, 640), F32),) * 2, in_specs=[SMEM] + [VMEM] * 6, out_specs=(VMEM,) * 2,
        compiler_params=params(16),
        cost_estimate=pl.CostEstimate(flops=4_000_000_000, bytes_accessed=6_000_000, transcendentals=0),
    )(which, win, pack, before, after, near_outer, near_inner)
    guidance = pl.pallas_call(
        finish_kernel, out_shape=shaped((T, D), F32), in_specs=[SMEM] + [VMEM] * 18, out_specs=VMEM,
        scratch_shapes=[pltpu.VMEM((T, 640), F32)] * 2 + [pltpu.VMEM((D, QKV), BF)],
        compiler_params=params(20),
    )(which, win, packs_outer, packs_inner, gk, gv, gq, ordering(target), x, gain, og, *blocks)
    return den.reshape(tokens.shape), guidance.reshape(tokens.shape)


def solution(mesh):
    split = Mesh(mesh.devices.reshape(2, 8, 4, 4, 2), ("yh", "z", "yl", "x", "core"))
    lat, lon = ("yh", "z"), ("yl", "x", "core")
    return jax.shard_map(
        on_device,
        mesh=split,
        in_specs=(
            P(lat, lon, None), P(), P(lat, None), P(lat, None), P(lat, None), P(lat, None), P(),
            P(lat, lon, None), P(lat, lon, None), P(lat, lon, None, None),
        ),
        out_specs=(P(lat, lon, None), P(lat, lon, None)),
        check_vma=False,
    )
```

```python
import functools

import jax
import jax.numpy as jnp
import numpy as np
from jax import lax
from jax.experimental import pallas as pl
from jax.experimental.pallas import tpu as pltpu
from jax.sharding import Mesh, PartitionSpec as P

H = 8
HD = 72
HW = 576
D = 1152
T = 128
QKV = 3 * HW
FACTOR = HD ** (-0.5)
SCALE2 = FACTOR * 1.4426950408889634
OFF = -1e30
BF = jnp.bfloat16
F32 = jnp.float32
VMEM = pl.BlockSpec(memory_space=pltpu.VMEM)
SMEM = pl.BlockSpec(memory_space=pltpu.SMEM)
ANY = pl.BlockSpec(memory_space=pl.ANY)
HBM = pl.BlockSpec(memory_space=pltpu.HBM)
K0, V0, Q0 = 0, HW, 2 * HW
VB = 512


def params(limit=40):
    return pltpu.CompilerParams(vmem_limit_bytes=limit * 1024 * 1024)


def nt(left, right):
    return lax.dot_general(left, right, (((1,), (1,)), ((), ())), preferred_element_type=F32)


def nn(left, right):
    return jnp.dot(left, right, preferred_element_type=F32)


def window(first):
    start = first // 128 * 128
    return start, start + 256


def stacked(x, first, start):
    return jnp.concatenate([head_only(x, first, start), head_only(x, first + HD, start)], axis=0)


def unstacked(x, first, start):
    return head_only(x[0:T, :], first, start) + head_only(x[T : 2 * T, :], first + HD, start)


def head_only(x, first, start):
    lane = lax.broadcasted_iota(jnp.int32, x.shape, 1) + start
    return jnp.where((lane >= first) & (lane < first + HD), x, jnp.zeros_like(x))


def norm_parts(x):
    center = x - jnp.mean(x, axis=-1, keepdims=True)
    rstd = lax.rsqrt(jnp.mean(center * center, axis=-1, keepdims=True) + 1e-6)
    return center, rstd


def order_kernel(target_ref, order_ref):
    rows = lax.broadcasted_iota(jnp.int32, (D, D), 0)
    order_ref[...] = jnp.where(rows == target_ref[...], 1.0, 0.0).astype(BF)


def hidden_kernel(x_ref, gain_ref, target_ref, out_ref, order_ref):
    order_kernel(target_ref, order_ref)
    for i in range(x_ref.shape[0] // T):
        center, rstd = norm_parts(x_ref[i * T : (i + 1) * T, :].astype(F32))
        hidden = (center * rstd * gain_ref[...]).astype(BF)
        out_ref[i * T : (i + 1) * T, :] = nn(hidden, order_ref[...]).astype(BF)


def collect(blocks, first, rows, w_ref):
    for i, block in enumerate(blocks):
        w_ref[rows * i : rows * (i + 1), :] = block[first : first + rows, :]


def position(slot_t, slot_r):
    turned = 2 - slot_r
    return (slot_r if slot_t == 1 else turned, slot_t), (turned if slot_t == 1 else slot_r, 2 - slot_t)


def project_kernel(
    place_ref, hw_ref, hc_ref, he_ref, b0, b1, b2, b3, b4, b5, b6, b7, win_ref, wn_ref, wo_ref, w_ref
):
    collect((b0, b1, b2, b3, b4, b5, b6, b7), 144, 48, wo_ref)
    collect((b0, b1, b2, b3, b4, b5, b6, b7), 0, 144, w_ref)
    for g, h_ref in enumerate((hw_ref, hc_ref, he_ref)):
        for part in range(3):
            s = slice(part * T, (part + 1) * T)
            win_ref[(g * 3 + part) * T : (g * 3 + part + 1) * T, :] = nn(h_ref[s, :], w_ref[...]).astype(BF)
    lane_of = lax.broadcasted_iota(jnp.int32, (640, 384), 0)
    whole, lower, upper = (
        jnp.where(lane_of == place_ref[i : i + 1, :], 1.0, 0.0).astype(BF) for i in range(3)
    )
    halves = wo_ref[:, D:QKV]
    wn_ref[...] = (
        nn(whole, wo_ref[:, 0:D]) + jnp.concatenate([nn(lower, halves), nn(upper, halves)], axis=1)
    ).astype(BF)


def forward_kernel(
    blocks_ref, win_ref, wn_ref, wpix_ref, x_ref, meas_ref, filt_ref,
    e_ref, den_ref, og_ref, pack_ref, stat_ref,
    bias_ref, acc_ref,
):
    acc_ref[...] = jnp.zeros_like(acc_ref)

    qc = (lax.broadcasted_iota(jnp.int32, (T, T), 0) & 8) > 0
    kc = (lax.broadcasted_iota(jnp.int32, (T, T), 1) & 8) > 0

    core = blocks_ref[30]

    def allowed(c, r, w):
        there = jnp.logical_and(w - c >= 0, w - c < 5)
        value = blocks_ref[(c * 3 + r) * 5 + jnp.clip(w - c, 0, 4)]
        return jnp.where(there, value, 0).astype(F32)

    lane_c = (lax.broadcasted_iota(jnp.int32, (1, T), 1) & 8) > 0
    rows = []
    for r in range(3):
        for w in range(6):
            rows.append(jnp.where(lane_c, allowed(1, r, jnp.int32(w)), allowed(0, r, jnp.int32(w))))
    for slot_t in range(3):
        for slot_r in range(3):
            (r0, t0), (r1, t1) = position(slot_t, slot_r)
            r, t = jnp.where(core == 0, r0, r1), jnp.where(core == 0, t0, t1)
            seen = jnp.where(
                qc,
                jnp.where(kc, allowed(1, r, 2 * t + 1), allowed(1, r, 2 * t)),
                jnp.where(kc, allowed(0, r, 2 * t + 1), allowed(0, r, 2 * t)),
            )
            j = 3 * slot_t + slot_r
            bias_ref[:, j * T : (j + 1) * T] = (1.0 - seen) * OFF
    own = slice(4 * T, 5 * T)
    lanes = lax.broadcasted_iota(jnp.int32, (T, T), 1)
    stats = jnp.zeros((T, T), F32)
    for e in range(0, H, 2):
        a, b = window(K0 + HD * e)
        q = win_ref[own, Q0 + a : min(Q0 + b, QKV)]
        if Q0 + b > QKV:
            q = jnp.concatenate([q, jnp.zeros((T, Q0 + b - QKV), BF)], axis=1)
        scores = nt(stacked(q, HD * e, a), win_ref[:, a:b])
        lows, invs = [], []
        for i in range(2):
            s = scores[i * T : (i + 1) * T, :] * SCALE2 + bias_ref[...]
            peak = jnp.max(s, axis=1, keepdims=True)
            p = jnp.exp2(s - peak)
            total = jnp.sum(p, axis=1, keepdims=True)
            inv = 1.0 / total
            stats = jnp.where(lanes == e + i, peak + jnp.log2(total), stats)
            stats = jnp.where(lanes == 16 + e + i, inv, stats)
            lows.append(p.astype(BF))
            invs.append(inv)
        low = jnp.concatenate(lows, axis=0)
        e_ref[e * T : (e + 2) * T, :] = low
        a, b = window(V0 + HD * e)
        o = nn(low, win_ref[:, a:b]) * jnp.concatenate(invs, axis=0)
        acc_ref[:, a - VB : b - VB] += unstacked(o, V0 + HD * e, a)

    att = acc_ref[...].astype(BF)
    den = (x_ref[...].astype(F32) + nn(att, wn_ref[...])).astype(BF)
    den_ref[...] = den
    colors = nt(den, wpix_ref[...])
    filt = filt_ref[...]
    misfit = -meas_ref[...]
    for c in range(3):
        misfit = misfit + jnp.where(filt == c, colors[:, 64 * c : 64 * c + 64], 0.0)
    spread = jnp.concatenate([jnp.where(filt == c, misfit, 0.0) for c in range(3)], axis=1).astype(BF)
    og = nn(spread, wpix_ref[...])
    og_ref[...] = og
    up = nt(og.astype(BF), wn_ref[...]).astype(BF)
    pack_ref[0:T, :] = up
    prod = up.astype(F32) * att.astype(F32)
    for e in range(H):
        a, b = window(V0 + HD * (e - e % 2))
        inner = jnp.sum(head_only(prod[:, a - VB : b - VB], V0 + HD * e, a), axis=1, keepdims=True)
        stats = jnp.where(lanes == 8 + e, inner, stats)
    stat_ref[...] = stats
    turned = stats.T[0:16, :]
    high = turned.astype(BF)
    rest = turned - high.astype(F32)
    mid = rest.astype(BF)
    low = (rest - mid.astype(F32)).astype(BF)
    pack_ref[T : T + 16, :] = jnp.concatenate(
        [
            high, mid, low, jnp.concatenate(rows[:16], axis=0).astype(BF),
            jnp.concatenate(rows[16:] + [jnp.zeros((14, T), F32)], axis=0).astype(BF),
        ],
        axis=1,
    )


def query_kernel(win_ref, e_ref, up_ref, stat_ref, gq_ref, acc_ref):
    acc_ref[...] = jnp.zeros_like(acc_ref)
    for e in range(0, H, 2):
        a, b = window(V0 + HD * e)
        up = stacked(up_ref[0:T, a - VB : b - VB], V0 + HD * e, a)
        dprob = nt(up, win_ref[:, a:b])
        p = e_ref[e * T : (e + 2) * T, :].astype(F32)
        inner = jnp.concatenate([stat_ref[:, 8 + e : 9 + e], stat_ref[:, 9 + e : 10 + e]], axis=0)
        inv = jnp.concatenate([stat_ref[:, 16 + e : 17 + e], stat_ref[:, 17 + e : 18 + e]], axis=0)
        ds = (p * (dprob - inner)).astype(BF)
        a, b = window(K0 + HD * e)
        dq = nn(ds, win_ref[:, a:b]) * (inv * FACTOR)
        acc_ref[:, a:b] += unstacked(dq, HD * e, a)
    gq_ref[...] = acc_ref[:, 0:HW].astype(BF)


def key_side(core_ref, win_ref, tiles, gk_ref, gv_ref):
    own = slice(4 * T, 5 * T)
    kc = (lax.broadcasted_iota(jnp.int32, (T, T), 0) & 8) > 0
    second = core_ref[0].astype(F32)
    bias, stats, ups = [], [], []
    for t, r, pack_ref, base in tiles:
        ups.append(pack_ref[base : base + T, :])
        extra = pack_ref[base + T : base + T + 16, :].astype(F32)
        stats.append(extra[:, 0:128] + extra[:, 128:256] + extra[:, 256:384])
        seen = []
        for w in range(2):
            on = []
            for row, col in position(t, r):
                i = (2 - row) * 6 + (2 - col) * 2 + w
                on.append(extra[i : i + 1, 384:512] if i < 16 else extra[i - 16 : i - 15, 512:640])
            seen.append(on[0] * (1.0 - second) + on[1] * second)
        bias.append((1.0 - jnp.where(kc, seen[1], seen[0])) * OFF)
    bias = jnp.concatenate(bias, axis=1)
    stats = jnp.concatenate(stats, axis=1)
    ups = jnp.concatenate(ups, axis=0)
    count = len(tiles) * T

    def queries(a, b):
        return jnp.concatenate(
            [win_ref[(3 * t + r) * T : (3 * t + r + 1) * T, Q0 + a : Q0 + b] for t, r, _, _ in tiles], axis=0
        )

    for e in range(0, H, 2):
        a, b = window(K0 + HD * e)
        if Q0 + b <= QKV:
            q = queries(a, b)
        else:
            q = jnp.concatenate([queries(a, HW), jnp.zeros((count, b - HW), BF)], axis=1)
        c, d = window(V0 + HD * e)
        up = ups[:, c - VB : d - VB]
        scores = nt(stacked(win_ref[own, a:b], HD * e, a), q)
        dprob = nt(stacked(win_ref[own, c:d], V0 + HD * e, c), up)
        ps, dss = [], []
        for i in range(2):
            rows = slice(i * T, (i + 1) * T)
            p = jnp.exp2(scores[rows, :] * SCALE2 + bias - stats[e + i : e + i + 1, :])
            ps.append(p.astype(BF))
            dss.append((p * (dprob[rows, :] - stats[8 + e + i : 9 + e + i, :])).astype(BF))
        gk_ref[:, a:b] += unstacked(nn(jnp.concatenate(dss, axis=0), q), HD * e, a)
        gv_ref[:, c - VB : d - VB] += unstacked(nn(jnp.concatenate(ps, axis=0), up), V0 + HD * e, c)


def key_near_kernel(core_ref, win_ref, own_ref, before_ref, after_ref, outer_ref, inner_ref, gk_ref, gv_ref):
    gk_ref[...] = jnp.zeros_like(gk_ref)
    gv_ref[...] = jnp.zeros_like(gv_ref)
    tiles = (
        (1, 0, before_ref, 0), (1, 1, own_ref, 0), (1, 2, after_ref, 0), (0, 1, outer_ref, 0), (2, 1, inner_ref, 0)
    )
    key_side(core_ref, win_ref, tiles, gk_ref, gv_ref)


def finish_kernel(
    core_ref, win_ref, packo_ref, packi_ref, gk0_ref, gv0_ref, gq_ref, order_ref, x_ref, gain_ref, og_ref,
    b0, b1, b2, b3, b4, b5, b6, b7,
    out_ref, gk_ref, gv_ref, w_ref,
):
    collect((b0, b1, b2, b3, b4, b5, b6, b7), 0, 144, w_ref)
    gk_ref[...] = gk0_ref[...]
    gv_ref[...] = gv0_ref[...]
    tiles = ((0, 0, packo_ref, 0), (0, 2, packo_ref, 144), (2, 0, packi_ref, 0), (2, 2, packi_ref, 144))
    key_side(core_ref, win_ref, tiles, gk_ref, gv_ref)
    gk = (gk_ref[:, 0:HW] * FACTOR).astype(BF)
    gv = gv_ref[:, 64:640].astype(BF)
    grads = jnp.concatenate([gk, gv, gq_ref[...]], axis=1)
    moved = nt(grads, w_ref[...])
    high = moved.astype(BF)
    low = (moved - high.astype(F32)).astype(BF)
    both = nt(jnp.concatenate([high, low], axis=0), order_ref[...])
    grad = (both[0:T, :] + both[T : 2 * T, :]) * gain_ref[...]
    center, rstd = norm_parts(x_ref[...].astype(F32))
    xhat = center * rstd
    mean_g = jnp.mean(grad, axis=-1, keepdims=True)
    mean_gx = jnp.mean(grad * xhat, axis=-1, keepdims=True)
    out_ref[...] = rstd * (grad - mean_g - xhat * mean_gx) + og_ref[...]


def shaped(shape, dtype=BF):
    return jax.ShapeDtypeStruct(shape, dtype)


def shards_held(yh, z, x, core, block, second):
    cs = core ^ jnp.asarray((block >= 4).astype(np.int32))
    shift = np.array([0, 3, 1, 2] * 2)[block]
    xs = (x + jnp.where(cs == 0, jnp.asarray(shift), jnp.asarray(-shift))) & 3
    hops = jnp.where(second, 3 - xs, xs + 1)
    zs = (z + jnp.where(cs == 0, -hops, hops)) & 7
    other = jnp.logical_xor(second, (xs == 3) & (cs == 1)).astype(jnp.int32)
    return (yh ^ other) * 8 + zs


def weight_targets(yh, z, x, core):
    place = np.arange(D)
    block, row = place // 144, place % 144
    held = shards_held(yh, z, x, core, block, row >= 72)
    return (held * 72 + row % 72).astype(jnp.int32).reshape(1, D)


def out_targets(yh, z, x, core):
    place = np.arange(384)
    block, row = place // 48, place % 48
    held = shards_held(yh, z, x, core, block, row >= 24) * 36 + 64
    row = row % 24
    whole = held + row
    lower = jnp.where(row < 12, held + 24 + row, -1)
    upper = jnp.where(row >= 12, held + 12 + row, -1)
    return jnp.stack([whole, lower, upper]).astype(jnp.int32)


def device(yh, z, yl, x, core):
    return (((yh * 8 + z % 8) * 4 + yl) * 4 + x) * 2 + core


def fetch_routes():
    first, second = [], []
    for yh in range(2):
        for z in range(8):
            for yl in range(4):
                for x in range(4):
                    for core in range(2):
                        me = device(yh, z, yl, x, core)
                        way = 1 if core else -1
                        near, far = z + way * (x + 1), z + way * (3 - x)
                        if x == 3 and core == 1:
                            first.append((device(1 - yh, near, 3 - yl, x, core), me))
                            second.append((me, me))
                        else:
                            first.append((device(yh, near, yl, x, core), me))
                            second.append((device(1 - yh, far, 3 - yl, x, core), me))
    return first, second


def on_device(tokens, gain, w_query, w_key, w_value, w_out, w_pixel, measured, filter_color, block_mask):
    yh, z, xi, core = (lax.axis_index(n) for n in ("yh", "z", "x", "core"))
    which = core.reshape(1).astype(jnp.int32)
    x = tokens.reshape(T, D)
    gain = gain.reshape(1, D)
    south = [(2 * i, 2 * i + 2) for i in range(15)] + [(2 * i + 3, 2 * i + 1) for i in range(15)]
    north = [(j, i) for i, j in south]
    ring = [(2 * i, (2 * i + 2) % 8) for i in range(4)] + [((2 * i + 3) % 8, 2 * i + 1) for i in range(4)]
    back = [(j, i) for i, j in ring]
    border = [(2 * i + 1, (2 * i + 2) % 32) for i in range(16)]
    border = border + [(j, i) for i, j in border]
    lat, lon = ("yh", "z"), ("yl", "x", "core")
    first, second = fetch_routes()

    def swap(v):
        return lax.ppermute(v, "core", [(0, 1), (1, 0)])

    def along(v, perm):
        return lax.ppermute(v, ("x", "core"), perm)

    def rows_beside(own):
        return lax.ppermute(own, lat + ("core",), south), lax.ppermute(own, lat + ("core",), north)

    def sides(column):
        return lax.ppermute(column, lon, border), swap(column)

    def placed(v, rows, cols):
        return lax.pad(v, jnp.zeros((), BF), ((*rows, 0), (*cols, 0)))

    at_row = lax.broadcasted_iota(jnp.int32, (96, QKV), 0)
    at_col = lax.broadcasted_iota(jnp.int32, (96, QKV), 1)
    lefts = placed(w_out, (48, 12), (D, -HW))
    rights = placed(w_out, (60, 0), (HW, 0))
    mine = (
        placed(w_key, (0, 24), (0, 2 * HW)) + placed(w_value, (0, 24), (HW, HW))
        + placed(w_query, (0, 24), (2 * HW, 0)) + placed(w_out, (72, -12), (0, HW))
        + jnp.where(at_row >= 72, lefts, 0) + jnp.where((at_row >= 84) & (at_col >= D), rights, 0)
    )
    one, two = lax.ppermute(mine, lat + lon, first), lax.ppermute(mine, lat + lon, second)
    fetched = jnp.concatenate([one[:72], two[:72], one[72:], two[72:]], axis=0)
    before, after = rows_beside(x)
    column = jnp.concatenate([before, x, after], axis=0)
    outer, inner = sides(column)
    target = weight_targets(yh, z, xi, core)

    def ordering(target):
        return pl.pallas_call(
            order_kernel, out_shape=shaped((D, D)), in_specs=[VMEM], out_specs=VMEM, compiler_params=params(8),
            cost_estimate=pl.CostEstimate(flops=2_000_000_000, bytes_accessed=3_000_000, transcendentals=0),
        )(target)


    def hidden(v):
        return pl.pallas_call(
            hidden_kernel, out_shape=shaped((3 * T, D)), in_specs=[VMEM] * 3, out_specs=VMEM,
            scratch_shapes=[pltpu.VMEM((D, D), BF)], compiler_params=params(16),
            cost_estimate=pl.CostEstimate(flops=3_000_000_000, bytes_accessed=5_000_000, transcendentals=0),
        )(v, gain, target)

    fetched, hc = lax.optimization_barrier((fetched, hidden(column)))
    right, left = along(fetched, ring), along(fetched, back)
    right, left, he, outer = lax.optimization_barrier((right, left, hidden(inner), outer))
    fetched_too = swap(fetched)
    across, hw = lax.optimization_barrier((along(right, ring), hidden(outer)))
    blocks = (fetched, right, left, across, fetched_too, swap(right), swap(left), swap(across))

    win, wn = pl.pallas_call(
        project_kernel, out_shape=(shaped((9 * T, QKV)), shaped((640, D))),
        in_specs=[VMEM] * 12, out_specs=(VMEM,) * 2,
        scratch_shapes=[pltpu.VMEM((384, QKV), BF), pltpu.VMEM((D, QKV), BF)],
        compiler_params=params(24),
        cost_estimate=pl.CostEstimate(flops=6_000_000_000, bytes_accessed=8_000_000, transcendentals=0),
    )(out_targets(yh, z, xi, core), hw, hc, he, *blocks)
    e, den, og, pack, stat = pl.pallas_call(
        forward_kernel,
        out_shape=(
            shaped((H * T, 9 * T)), shaped((T, D)), shaped((T, D), F32), shaped((144, 640)), shaped((T, T), F32),
        ),
        in_specs=[SMEM] + [VMEM] * 6, out_specs=(VMEM,) * 5,
        scratch_shapes=[pltpu.VMEM((T, 9 * T), F32), pltpu.VMEM((T, 640), F32)],
        compiler_params=params(18),
        cost_estimate=pl.CostEstimate(flops=6_000_000_000, bytes_accessed=8_000_000, transcendentals=1_000_000),
    )(jnp.concatenate([block_mask.reshape(30), which]), win, wn, w_pixel.T, x, measured.reshape(T, 64), filter_color.reshape(T, 64))
    before, after = rows_beside(pack)
    near_outer, near_inner = sides(pack)
    corners, target, stat_late = lax.optimization_barrier((jnp.concatenate([before, after], axis=0), target, stat))
    packs_outer, packs_inner = sides(corners)
    gq = pl.pallas_call(
        query_kernel, out_shape=shaped((T, HW)), in_specs=[VMEM] * 4, out_specs=VMEM,
        scratch_shapes=[pltpu.VMEM((T, 640), F32)], compiler_params=params(16),
        cost_estimate=pl.CostEstimate(flops=4_000_000_000, bytes_accessed=6_000_000, transcendentals=0),
    )(win, e, pack, stat_late)
    gk, gv = pl.pallas_call(
        key_near_kernel, out_shape=(shaped((T, 640), F32),) * 2, in_specs=[SMEM] + [VMEM] * 6, out_specs=(VMEM,) * 2,
        compiler_params=params(16),
        cost_estimate=pl.CostEstimate(flops=4_000_000_000, bytes_accessed=6_000_000, transcendentals=0),
    )(which, win, pack, before, after, near_outer, near_inner)
    guidance = pl.pallas_call(
        finish_kernel, out_shape=shaped((T, D), F32), in_specs=[SMEM] + [VMEM] * 18, out_specs=VMEM,
        scratch_shapes=[pltpu.VMEM((T, 640), F32)] * 2 + [pltpu.VMEM((D, QKV), BF)],
        compiler_params=params(20),
    )(which, win, packs_outer, packs_inner, gk, gv, gq, ordering(target), x, gain, og, *blocks)
    return den.reshape(tokens.shape), guidance.reshape(tokens.shape)


def solution(mesh):
    split = Mesh(mesh.devices.reshape(2, 8, 4, 4, 2), ("yh", "z", "yl", "x", "core"))
    lat, lon = ("yh", "z"), ("yl", "x", "core")
    return jax.shard_map(
        on_device,
        mesh=split,
        in_specs=(
            P(lat, lon, None), P(), P(lat, None), P(lat, None), P(lat, None), P(lat, None), P(),
            P(lat, lon, None), P(lat, lon, None), P(lat, lon, None, None),
        ),
        out_specs=(P(lat, lon, None), P(lat, lon, None)),
        check_vma=False,
    )
```

```python
import functools

import jax
import jax.numpy as jnp
import numpy as np
from jax import lax
from jax.experimental import pallas as pl
from jax.experimental.pallas import tpu as pltpu
from jax.sharding import Mesh, PartitionSpec as P

H = 8
HD = 72
HW = 576
D = 1152
T = 128
QKV = 3 * HW
FACTOR = HD ** (-0.5)
SCALE2 = FACTOR * 1.4426950408889634
OFF = -1e30
BF = jnp.bfloat16
F32 = jnp.float32
VMEM = pl.BlockSpec(memory_space=pltpu.VMEM)
SMEM = pl.BlockSpec(memory_space=pltpu.SMEM)
ANY = pl.BlockSpec(memory_space=pl.ANY)
HBM = pl.BlockSpec(memory_space=pltpu.HBM)
K0, V0, Q0 = 0, HW, 2 * HW
VB = 512


def params(limit=40):
    return pltpu.CompilerParams(vmem_limit_bytes=limit * 1024 * 1024)


def nt(left, right):
    return lax.dot_general(left, right, (((1,), (1,)), ((), ())), preferred_element_type=F32)


def nn(left, right):
    return jnp.dot(left, right, preferred_element_type=F32)


def window(first):
    start = first // 128 * 128
    return start, start + 256


def stacked(x, first, start):
    return jnp.concatenate([head_only(x, first, start), head_only(x, first + HD, start)], axis=0)


def unstacked(x, first, start):
    return head_only(x[0:T, :], first, start) + head_only(x[T : 2 * T, :], first + HD, start)


def head_only(x, first, start):
    lane = lax.broadcasted_iota(jnp.int32, x.shape, 1) + start
    return jnp.where((lane >= first) & (lane < first + HD), x, jnp.zeros_like(x))


def norm_parts(x):
    center = x - jnp.mean(x, axis=-1, keepdims=True)
    rstd = lax.rsqrt(jnp.mean(center * center, axis=-1, keepdims=True) + 1e-6)
    return center, rstd


def order_kernel(target_ref, order_ref):
    rows = lax.broadcasted_iota(jnp.int32, (D, D), 0)
    order_ref[...] = jnp.where(rows == target_ref[...], 1.0, 0.0).astype(BF)


def hidden_kernel(x_ref, gain_ref, target_ref, out_ref, order_ref):
    order_kernel(target_ref, order_ref)
    for i in range(x_ref.shape[0] // T):
        center, rstd = norm_parts(x_ref[i * T : (i + 1) * T, :].astype(F32))
        hidden = (center * rstd * gain_ref[...]).astype(BF)
        out_ref[i * T : (i + 1) * T, :] = nn(hidden, order_ref[...]).astype(BF)


def collect(blocks, first, rows, w_ref):
    for i, block in enumerate(blocks):
        w_ref[rows * i : rows * (i + 1), :] = block[first : first + rows, :]


def position(slot_t, slot_r):
    turned = 2 - slot_r
    return (slot_r if slot_t == 1 else turned, slot_t), (turned if slot_t == 1 else slot_r, 2 - slot_t)


def project_kernel(
    place_ref, hw_ref, hc_ref, he_ref, b0, b1, b2, b3, b4, b5, b6, b7, win_ref, wn_ref, wo_ref, w_ref
):
    collect((b0, b1, b2, b3, b4, b5, b6, b7), 144, 48, wo_ref)
    collect((b0, b1, b2, b3, b4, b5, b6, b7), 0, 144, w_ref)
    for g, h_ref in enumerate((hw_ref, hc_ref, he_ref)):
        for part in range(3):
            s = slice(part * T, (part + 1) * T)
            win_ref[(g * 3 + part) * T : (g * 3 + part + 1) * T, :] = nn(h_ref[s, :], w_ref[...]).astype(BF)
    lane_of = lax.broadcasted_iota(jnp.int32, (640, 384), 0)
    whole, lower, upper = (
        jnp.where(lane_of == place_ref[i : i + 1, :], 1.0, 0.0).astype(BF) for i in range(3)
    )
    halves = wo_ref[:, D:QKV]
    wn_ref[...] = (
        nn(whole, wo_ref[:, 0:D]) + jnp.concatenate([nn(lower, halves), nn(upper, halves)], axis=1)
    ).astype(BF)


def forward_kernel(
    blocks_ref, win_ref, wn_ref, wpix_ref, x_ref, meas_ref, filt_ref,
    e_ref, den_ref, og_ref, pack_ref, stat_ref,
    bias_ref, acc_ref,
):
    acc_ref[...] = jnp.zeros_like(acc_ref)

    qc = (lax.broadcasted_iota(jnp.int32, (T, T), 0) & 8) > 0
    kc = (lax.broadcasted_iota(jnp.int32, (T, T), 1) & 8) > 0

    core = blocks_ref[30]

    def allowed(c, r, w):
        there = jnp.logical_and(w - c >= 0, w - c < 5)
        value = blocks_ref[(c * 3 + r) * 5 + jnp.clip(w - c, 0, 4)]
        return jnp.where(there, value, 0).astype(F32)

    lane_c = (lax.broadcasted_iota(jnp.int32, (1, T), 1) & 8) > 0
    rows = []
    for r in range(3):
        for w in range(6):
            rows.append(jnp.where(lane_c, allowed(1, r, jnp.int32(w)), allowed(0, r, jnp.int32(w))))
    for slot_t in range(3):
        for slot_r in range(3):
            (r0, t0), (r1, t1) = position(slot_t, slot_r)
            r, t = jnp.where(core == 0, r0, r1), jnp.where(core == 0, t0, t1)
            seen = jnp.where(
                qc,
                jnp.where(kc, allowed(1, r, 2 * t + 1), allowed(1, r, 2 * t)),
                jnp.where(kc, allowed(0, r, 2 * t + 1), allowed(0, r, 2 * t)),
            )
            j = 3 * slot_t + slot_r
            bias_ref[:, j * T : (j + 1) * T] = (1.0 - seen) * OFF
    own = slice(4 * T, 5 * T)
    lanes = lax.broadcasted_iota(jnp.int32, (T, T), 1)
    stats = jnp.zeros((T, T), F32)
    for e in range(0, H, 2):
        a, b = window(K0 + HD * e)
        q = win_ref[own, Q0 + a : min(Q0 + b, QKV)]
        if Q0 + b > QKV:
            q = jnp.concatenate([q, jnp.zeros((T, Q0 + b - QKV), BF)], axis=1)
        scores = nt(stacked(q, HD * e, a), win_ref[:, a:b])
        lows, invs = [], []
        for i in range(2):
            s = scores[i * T : (i + 1) * T, :] * SCALE2 + bias_ref[...]
            peak = jnp.max(s, axis=1, keepdims=True)
            p = jnp.exp2(s - peak)
            total = jnp.sum(p, axis=1, keepdims=True)
            inv = 1.0 / total
            stats = jnp.where(lanes == e + i, peak + jnp.log2(total), stats)
            stats = jnp.where(lanes == 16 + e + i, inv, stats)
            lows.append(p.astype(BF))
            invs.append(inv)
        low = jnp.concatenate(lows, axis=0)
        e_ref[e * T : (e + 2) * T, :] = low
        a, b = window(V0 + HD * e)
        o = nn(low, win_ref[:, a:b]) * jnp.concatenate(invs, axis=0)
        acc_ref[:, a - VB : b - VB] += unstacked(o, V0 + HD * e, a)

    att = acc_ref[...].astype(BF)
    den = (x_ref[...].astype(F32) + nn(att, wn_ref[...])).astype(BF)
    den_ref[...] = den
    colors = nt(den, wpix_ref[...])
    filt = filt_ref[...]
    misfit = -meas_ref[...]
    for c in range(3):
        misfit = misfit + jnp.where(filt == c, colors[:, 64 * c : 64 * c + 64], 0.0)
    spread = jnp.concatenate([jnp.where(filt == c, misfit, 0.0) for c in range(3)], axis=1).astype(BF)
    og = nn(spread, wpix_ref[...])
    og_ref[...] = og
    up = nt(og.astype(BF), wn_ref[...]).astype(BF)
    pack_ref[0:T, :] = up
    prod = up.astype(F32) * att.astype(F32)
    for e in range(H):
        a, b = window(V0 + HD * (e - e % 2))
        inner = jnp.sum(head_only(prod[:, a - VB : b - VB], V0 + HD * e, a), axis=1, keepdims=True)
        stats = jnp.where(lanes == 8 + e, inner, stats)
    stat_ref[...] = stats
    turned = stats.T[0:16, :]
    high = turned.astype(BF)
    rest = turned - high.astype(F32)
    mid = rest.astype(BF)
    low = (rest - mid.astype(F32)).astype(BF)
    pack_ref[T : T + 16, :] = jnp.concatenate(
        [
            high, mid, low, jnp.concatenate(rows[:16], axis=0).astype(BF),
            jnp.concatenate(rows[16:] + [jnp.zeros((14, T), F32)], axis=0).astype(BF),
        ],
        axis=1,
    )


def query_kernel(win_ref, e_ref, up_ref, stat_ref, gq_ref, acc_ref):
    acc_ref[...] = jnp.zeros_like(acc_ref)
    for e in range(0, H, 2):
        a, b = window(V0 + HD * e)
        up = stacked(up_ref[0:T, a - VB : b - VB], V0 + HD * e, a)
        dprob = nt(up, win_ref[:, a:b])
        p = e_ref[e * T : (e + 2) * T, :].astype(F32)
        inner = jnp.concatenate([stat_ref[:, 8 + e : 9 + e], stat_ref[:, 9 + e : 10 + e]], axis=0)
        inv = jnp.concatenate([stat_ref[:, 16 + e : 17 + e], stat_ref[:, 17 + e : 18 + e]], axis=0)
        ds = (p * (dprob - inner)).astype(BF)
        a, b = window(K0 + HD * e)
        dq = nn(ds, win_ref[:, a:b]) * (inv * FACTOR)
        acc_ref[:, a:b] += unstacked(dq, HD * e, a)
    gq_ref[...] = acc_ref[:, 0:HW].astype(BF)


def key_side(core_ref, win_ref, tiles, gk_ref, gv_ref):
    own = slice(4 * T, 5 * T)
    kc = (lax.broadcasted_iota(jnp.int32, (T, T), 0) & 8) > 0
    second = core_ref[0].astype(F32)
    bias, stats, ups = [], [], []
    for t, r, pack_ref, base in tiles:
        ups.append(pack_ref[base : base + T, :])
        extra = pack_ref[base + T : base + T + 16, :].astype(F32)
        stats.append(extra[:, 0:128] + extra[:, 128:256] + extra[:, 256:384])
        seen = []
        for w in range(2):
            on = []
            for row, col in position(t, r):
                i = (2 - row) * 6 + (2 - col) * 2 + w
                on.append(extra[i : i + 1, 384:512] if i < 16 else extra[i - 16 : i - 15, 512:640])
            seen.append(on[0] * (1.0 - second) + on[1] * second)
        bias.append((1.0 - jnp.where(kc, seen[1], seen[0])) * OFF)
    bias = jnp.concatenate(bias, axis=1)
    stats = jnp.concatenate(stats, axis=1)
    ups = jnp.concatenate(ups, axis=0)
    count = len(tiles) * T

    def queries(a, b):
        return jnp.concatenate(
            [win_ref[(3 * t + r) * T : (3 * t + r + 1) * T, Q0 + a : Q0 + b] for t, r, _, _ in tiles], axis=0
        )

    for e in range(0, H, 2):
        a, b = window(K0 + HD * e)
        if Q0 + b <= QKV:
            q = queries(a, b)
        else:
            q = jnp.concatenate([queries(a, HW), jnp.zeros((count, b - HW), BF)], axis=1)
        c, d = window(V0 + HD * e)
        up = ups[:, c - VB : d - VB]
        scores = nt(stacked(win_ref[own, a:b], HD * e, a), q)
        dprob = nt(stacked(win_ref[own, c:d], V0 + HD * e, c), up)
        ps, dss = [], []
        for i in range(2):
            rows = slice(i * T, (i + 1) * T)
            p = jnp.exp2(scores[rows, :] * SCALE2 + bias - stats[e + i : e + i + 1, :])
            ps.append(p.astype(BF))
            dss.append((p * (dprob[rows, :] - stats[8 + e + i : 9 + e + i, :])).astype(BF))
        gk_ref[:, a:b] += unstacked(nn(jnp.concatenate(dss, axis=0), q), HD * e, a)
        gv_ref[:, c - VB : d - VB] += unstacked(nn(jnp.concatenate(ps, axis=0), up), V0 + HD * e, c)


def key_near_kernel(core_ref, win_ref, own_ref, before_ref, after_ref, outer_ref, inner_ref, gk_ref, gv_ref):
    gk_ref[...] = jnp.zeros_like(gk_ref)
    gv_ref[...] = jnp.zeros_like(gv_ref)
    tiles = (
        (1, 0, before_ref, 0), (1, 1, own_ref, 0), (1, 2, after_ref, 0), (0, 1, outer_ref, 0), (2, 1, inner_ref, 0)
    )
    key_side(core_ref, win_ref, tiles, gk_ref, gv_ref)


def finish_kernel(
    core_ref, win_ref, packo_ref, packi_ref, gk0_ref, gv0_ref, gq_ref, order_ref, x_ref, gain_ref, og_ref,
    b0, b1, b2, b3, b4, b5, b6, b7,
    out_ref, gk_ref, gv_ref, w_ref,
):
    collect((b0, b1, b2, b3, b4, b5, b6, b7), 0, 144, w_ref)
    gk_ref[...] = gk0_ref[...]
    gv_ref[...] = gv0_ref[...]
    tiles = ((0, 0, packo_ref, 0), (0, 2, packo_ref, 144), (2, 0, packi_ref, 0), (2, 2, packi_ref, 144))
    key_side(core_ref, win_ref, tiles, gk_ref, gv_ref)
    gk = (gk_ref[:, 0:HW] * FACTOR).astype(BF)
    gv = gv_ref[:, 64:640].astype(BF)
    grads = jnp.concatenate([gk, gv, gq_ref[...]], axis=1)
    moved = nt(grads, w_ref[...])
    high = moved.astype(BF)
    low = (moved - high.astype(F32)).astype(BF)
    both = nt(jnp.concatenate([high, low], axis=0), order_ref[...])
    grad = (both[0:T, :] + both[T : 2 * T, :]) * gain_ref[...]
    center, rstd = norm_parts(x_ref[...].astype(F32))
    xhat = center * rstd
    mean_g = jnp.mean(grad, axis=-1, keepdims=True)
    mean_gx = jnp.mean(grad * xhat, axis=-1, keepdims=True)
    out_ref[...] = rstd * (grad - mean_g - xhat * mean_gx) + og_ref[...]


def shaped(shape, dtype=BF):
    return jax.ShapeDtypeStruct(shape, dtype)


def shards_held(yh, z, x, core, block, second):
    cs = core ^ jnp.asarray((block >= 4).astype(np.int32))
    shift = np.array([0, 3, 1, 2] * 2)[block]
    xs = (x + jnp.where(cs == 0, jnp.asarray(shift), jnp.asarray(-shift))) & 3
    hops = jnp.where(second, 3 - xs, xs + 1)
    zs = (z + jnp.where(cs == 0, -hops, hops)) & 7
    other = jnp.logical_xor(second, (xs == 3) & (cs == 1)).astype(jnp.int32)
    return (yh ^ other) * 8 + zs


def weight_targets(yh, z, x, core):
    place = np.arange(D)
    block, row = place // 144, place % 144
    held = shards_held(yh, z, x, core, block, row >= 72)
    return (held * 72 + row % 72).astype(jnp.int32).reshape(1, D)


def out_targets(yh, z, x, core):
    place = np.arange(384)
    block, row = place // 48, place % 48
    held = shards_held(yh, z, x, core, block, row >= 24) * 36 + 64
    row = row % 24
    whole = held + row
    lower = jnp.where(row < 12, held + 24 + row, -1)
    upper = jnp.where(row >= 12, held + 12 + row, -1)
    return jnp.stack([whole, lower, upper]).astype(jnp.int32)


def device(yh, z, yl, x, core):
    return (((yh * 8 + z % 8) * 4 + yl) * 4 + x) * 2 + core


def fetch_routes():
    first, second = [], []
    for yh in range(2):
        for z in range(8):
            for yl in range(4):
                for x in range(4):
                    for core in range(2):
                        me = device(yh, z, yl, x, core)
                        way = 1 if core else -1
                        near, far = z + way * (x + 1), z + way * (3 - x)
                        if x == 3 and core == 1:
                            first.append((device(1 - yh, near, 3 - yl, x, core), me))
                            second.append((me, me))
                        else:
                            first.append((device(yh, near, yl, x, core), me))
                            second.append((device(1 - yh, far, 3 - yl, x, core), me))
    return first, second


def on_device(tokens, gain, w_query, w_key, w_value, w_out, w_pixel, measured, filter_color, block_mask):
    yh, z, xi, core = (lax.axis_index(n) for n in ("yh", "z", "x", "core"))
    which = core.reshape(1).astype(jnp.int32)
    x = tokens.reshape(T, D)
    gain = gain.reshape(1, D)
    south = [(2 * i, 2 * i + 2) for i in range(15)] + [(2 * i + 3, 2 * i + 1) for i in range(15)]
    north = [(j, i) for i, j in south]
    ring = [(2 * i, (2 * i + 2) % 8) for i in range(4)] + [((2 * i + 3) % 8, 2 * i + 1) for i in range(4)]
    back = [(j, i) for i, j in ring]
    border = [(2 * i + 1, (2 * i + 2) % 32) for i in range(16)]
    border = border + [(j, i) for i, j in border]
    lat, lon = ("yh", "z"), ("yl", "x", "core")
    first, second = fetch_routes()

    def swap(v):
        return lax.ppermute(v, "core", [(0, 1), (1, 0)])

    def along(v, perm):
        return lax.ppermute(v, ("x", "core"), perm)

    def rows_beside(own):
        return lax.ppermute(own, lat + ("core",), south), lax.ppermute(own, lat + ("core",), north)

    def sides(column):
        return lax.ppermute(column, lon, border), swap(column)

    def placed(v, rows, cols):
        return lax.pad(v, jnp.zeros((), BF), ((*rows, 0), (*cols, 0)))

    at_row = lax.broadcasted_iota(jnp.int32, (96, QKV), 0)
    at_col = lax.broadcasted_iota(jnp.int32, (96, QKV), 1)
    lefts = placed(w_out, (48, 12), (D, -HW))
    rights = placed(w_out, (60, 0), (HW, 0))
    mine = (
        placed(w_key, (0, 24), (0, 2 * HW)) + placed(w_value, (0, 24), (HW, HW))
        + placed(w_query, (0, 24), (2 * HW, 0)) + placed(w_out, (72, -12), (0, HW))
        + jnp.where(at_row >= 72, lefts, 0) + jnp.where((at_row >= 84) & (at_col >= D), rights, 0)
    )
    one, two = lax.ppermute(mine, lat + lon, first), lax.ppermute(mine, lat + lon, second)
    fetched = jnp.concatenate([one[:72], two[:72], one[72:], two[72:]], axis=0)
    before, after = rows_beside(x)
    column = jnp.concatenate([before, x, after], axis=0)
    outer, inner = sides(column)
    target = weight_targets(yh, z, xi, core)

    def ordering(target):
        return pl.pallas_call(
            order_kernel, out_shape=shaped((D, D)), in_specs=[VMEM], out_specs=VMEM, compiler_params=params(8),
            cost_estimate=pl.CostEstimate(flops=2_000_000_000, bytes_accessed=3_000_000, transcendentals=0),
        )(target)


    def hidden(v):
        return pl.pallas_call(
            hidden_kernel, out_shape=shaped((3 * T, D)), in_specs=[VMEM] * 3, out_specs=VMEM,
            scratch_shapes=[pltpu.VMEM((D, D), BF)], compiler_params=params(16),
            cost_estimate=pl.CostEstimate(flops=3_000_000_000, bytes_accessed=5_000_000, transcendentals=0),
        )(v, gain, target)

    right, left = along(fetched, ring), along(fetched, back)
    right, left, he, outer = lax.optimization_barrier((right, left, hidden(inner), outer))
    fetched_too = swap(fetched)
    across, hw, hc = lax.optimization_barrier((along(right, ring), hidden(outer), hidden(column)))
    blocks = (fetched, right, left, across, fetched_too, swap(right), swap(left), swap(across))

    win, wn = pl.pallas_call(
        project_kernel, out_shape=(shaped((9 * T, QKV)), shaped((640, D))),
        in_specs=[VMEM] * 12, out_specs=(VMEM,) * 2,
        scratch_shapes=[pltpu.VMEM((384, QKV), BF), pltpu.VMEM((D, QKV), BF)],
        compiler_params=params(24),
        cost_estimate=pl.CostEstimate(flops=6_000_000_000, bytes_accessed=8_000_000, transcendentals=0),
    )(out_targets(yh, z, xi, core), hw, hc, he, *blocks)
    e, den, og, pack, stat = pl.pallas_call(
        forward_kernel,
        out_shape=(
            shaped((H * T, 9 * T)), shaped((T, D)), shaped((T, D), F32), shaped((144, 640)), shaped((T, T), F32),
        ),
        in_specs=[SMEM] + [VMEM] * 6, out_specs=(VMEM,) * 5,
        scratch_shapes=[pltpu.VMEM((T, 9 * T), F32), pltpu.VMEM((T, 640), F32)],
        compiler_params=params(18),
        cost_estimate=pl.CostEstimate(flops=6_000_000_000, bytes_accessed=8_000_000, transcendentals=1_000_000),
    )(jnp.concatenate([block_mask.reshape(30), which]), win, wn, w_pixel.T, x, measured.reshape(T, 64), filter_color.reshape(T, 64))
    before, after = rows_beside(pack)
    near_outer, near_inner = sides(pack)
    corners, target, stat_late = lax.optimization_barrier((jnp.concatenate([before, after], axis=0), target, stat))
    packs_outer, packs_inner = sides(corners)
    gq = pl.pallas_call(
        query_kernel, out_shape=shaped((T, HW)), in_specs=[VMEM] * 4, out_specs=VMEM,
        scratch_shapes=[pltpu.VMEM((T, 640), F32)], compiler_params=params(16),
        cost_estimate=pl.CostEstimate(flops=4_000_000_000, bytes_accessed=6_000_000, transcendentals=0),
    )(win, e, pack, stat_late)
    gk, gv = pl.pallas_call(
        key_near_kernel, out_shape=(shaped((T, 640), F32),) * 2, in_specs=[SMEM] + [VMEM] * 6, out_specs=(VMEM,) * 2,
        compiler_params=params(16),
        cost_estimate=pl.CostEstimate(flops=4_000_000_000, bytes_accessed=6_000_000, transcendentals=0),
    )(which, win, pack, before, after, near_outer, near_inner)
    guidance = pl.pallas_call(
        finish_kernel, out_shape=shaped((T, D), F32), in_specs=[SMEM] + [VMEM] * 18, out_specs=VMEM,
        scratch_shapes=[pltpu.VMEM((T, 640), F32)] * 2 + [pltpu.VMEM((D, QKV), BF)],
        compiler_params=params(20),
    )(which, win, packs_outer, packs_inner, gk, gv, gq, ordering(target), x, gain, og, *blocks)
    return den.reshape(tokens.shape), guidance.reshape(tokens.shape)


def solution(mesh):
    split = Mesh(mesh.devices.reshape(2, 8, 4, 4, 2), ("yh", "z", "yl", "x", "core"))
    lat, lon = ("yh", "z"), ("yl", "x", "core")
    return jax.shard_map(
        on_device,
        mesh=split,
        in_specs=(
            P(lat, lon, None), P(), P(lat, None), P(lat, None), P(lat, None), P(lat, None), P(),
            P(lat, lon, None), P(lat, lon, None), P(lat, lon, None, None),
        ),
        out_specs=(P(lat, lon, None), P(lat, lon, None)),
        check_vma=False,
    )
```

```python
import functools

import jax
import jax.numpy as jnp
import numpy as np
from jax import lax
from jax.experimental import pallas as pl
from jax.experimental.pallas import tpu as pltpu
from jax.sharding import Mesh, PartitionSpec as P

H = 8
HD = 72
HW = 576
D = 1152
T = 128
QKV = 3 * HW
FACTOR = HD ** (-0.5)
SCALE2 = FACTOR * 1.4426950408889634
OFF = -1e30
BF = jnp.bfloat16
F32 = jnp.float32
VMEM = pl.BlockSpec(memory_space=pltpu.VMEM)
SMEM = pl.BlockSpec(memory_space=pltpu.SMEM)
ANY = pl.BlockSpec(memory_space=pl.ANY)
HBM = pl.BlockSpec(memory_space=pltpu.HBM)
K0, V0, Q0 = 0, HW, 2 * HW
VB = 512


def params(limit=40):
    return pltpu.CompilerParams(vmem_limit_bytes=limit * 1024 * 1024)


def nt(left, right):
    return lax.dot_general(left, right, (((1,), (1,)), ((), ())), preferred_element_type=F32)


def nn(left, right):
    return jnp.dot(left, right, preferred_element_type=F32)


def window(first):
    start = first // 128 * 128
    return start, start + 256


def stacked(x, first, start):
    return jnp.concatenate([head_only(x, first, start), head_only(x, first + HD, start)], axis=0)


def unstacked(x, first, start):
    return head_only(x[0:T, :], first, start) + head_only(x[T : 2 * T, :], first + HD, start)


def head_only(x, first, start):
    lane = lax.broadcasted_iota(jnp.int32, x.shape, 1) + start
    return jnp.where((lane >= first) & (lane < first + HD), x, jnp.zeros_like(x))


def norm_parts(x):
    center = x - jnp.mean(x, axis=-1, keepdims=True)
    rstd = lax.rsqrt(jnp.mean(center * center, axis=-1, keepdims=True) + 1e-6)
    return center, rstd


def order_kernel(target_ref, order_ref):
    rows = lax.broadcasted_iota(jnp.int32, (D, D), 0)
    order_ref[...] = jnp.where(rows == target_ref[...], 1.0, 0.0).astype(BF)


def hidden_kernel(x_ref, gain_ref, target_ref, out_ref, order_ref):
    order_kernel(target_ref, order_ref)
    for i in range(x_ref.shape[0] // T):
        center, rstd = norm_parts(x_ref[i * T : (i + 1) * T, :].astype(F32))
        hidden = (center * rstd * gain_ref[...]).astype(BF)
        out_ref[i * T : (i + 1) * T, :] = nn(hidden, order_ref[...]).astype(BF)


def collect(blocks, first, rows, w_ref):
    for i, block in enumerate(blocks):
        w_ref[rows * i : rows * (i + 1), :] = block[first : first + rows, :]


def position(slot_t, slot_r):
    turned = 2 - slot_r
    return (slot_r if slot_t == 1 else turned, slot_t), (turned if slot_t == 1 else slot_r, 2 - slot_t)


def project_kernel(
    place_ref, hw_ref, hc_ref, he_ref, b0, b1, b2, b3, b4, b5, b6, b7, win_ref, wn_ref, wo_ref, w_ref
):
    collect((b0, b1, b2, b3, b4, b5, b6, b7), 144, 48, wo_ref)
    collect((b0, b1, b2, b3, b4, b5, b6, b7), 0, 144, w_ref)
    for g, h_ref in enumerate((hw_ref, hc_ref, he_ref)):
        for part in range(3):
            s = slice(part * T, (part + 1) * T)
            win_ref[(g * 3 + part) * T : (g * 3 + part + 1) * T, :] = nn(h_ref[s, :], w_ref[...]).astype(BF)
    lane_of = lax.broadcasted_iota(jnp.int32, (640, 384), 0)
    whole, lower, upper = (
        jnp.where(lane_of == place_ref[i : i + 1, :], 1.0, 0.0).astype(BF) for i in range(3)
    )
    halves = nn(jnp.concatenate([lower, upper], axis=0), wo_ref[:, D:QKV])
    wn_ref[...] = (
        nn(whole, wo_ref[:, 0:D]) + jnp.concatenate([halves[0:640, :], halves[640:1280, :]], axis=1)
    ).astype(BF)


def forward_kernel(
    blocks_ref, win_ref, wn_ref, wpix_ref, x_ref, meas_ref, filt_ref,
    e_ref, den_ref, og_ref, pack_ref, stat_ref,
    bias_ref, acc_ref,
):
    acc_ref[...] = jnp.zeros_like(acc_ref)

    qc = (lax.broadcasted_iota(jnp.int32, (T, T), 0) & 8) > 0
    kc = (lax.broadcasted_iota(jnp.int32, (T, T), 1) & 8) > 0

    core = blocks_ref[30]

    table = {
        (c, r, w): blocks_ref[(c * 3 + r) * 5 + w - c].astype(F32) if 0 <= w - c < 5 else jnp.float32(0.0)
        for c in range(2)
        for r in range(3)
        for w in range(6)
    }

    lane_c = (lax.broadcasted_iota(jnp.int32, (1, T), 1) & 8) > 0
    rows = []
    for r in range(3):
        for w in range(6):
            rows.append(jnp.where(lane_c, table[1, r, w], table[0, r, w]))
    for slot_t in range(3):
        for slot_r in range(3):
            (r0, t0), (r1, t1) = position(slot_t, slot_r)
            (m00, m01), (m10, m11) = [
                [jnp.where(core == 0, table[c, r0, 2 * t0 + w], table[c, r1, 2 * t1 + w]) for w in range(2)]
                for c in range(2)
            ]
            seen = jnp.where(qc, jnp.where(kc, m11, m10), jnp.where(kc, m01, m00))
            j = 3 * slot_t + slot_r
            bias_ref[:, j * T : (j + 1) * T] = (1.0 - seen) * OFF
    own = slice(4 * T, 5 * T)
    lanes = lax.broadcasted_iota(jnp.int32, (T, T), 1)
    stats = jnp.zeros((T, T), F32)
    for e in range(0, H, 2):
        a, b = window(K0 + HD * e)
        q = win_ref[own, Q0 + a : min(Q0 + b, QKV)]
        if Q0 + b > QKV:
            q = jnp.concatenate([q, jnp.zeros((T, Q0 + b - QKV), BF)], axis=1)
        scores = nt(stacked(q, HD * e, a), win_ref[:, a:b])
        lows, invs = [], []
        for i in range(2):
            s = scores[i * T : (i + 1) * T, :] * SCALE2 + bias_ref[...]
            peak = jnp.max(s, axis=1, keepdims=True)
            p = jnp.exp2(s - peak)
            total = jnp.sum(p, axis=1, keepdims=True)
            inv = 1.0 / total
            stats = jnp.where(lanes == e + i, peak + jnp.log2(total), stats)
            stats = jnp.where(lanes == 16 + e + i, inv, stats)
            lows.append(p.astype(BF))
            invs.append(inv)
        low = jnp.concatenate(lows, axis=0)
        e_ref[e * T : (e + 2) * T, :] = low
        a, b = window(V0 + HD * e)
        o = nn(low, win_ref[:, a:b]) * jnp.concatenate(invs, axis=0)
        acc_ref[:, a - VB : b - VB] += unstacked(o, V0 + HD * e, a)

    att = acc_ref[...].astype(BF)
    den = (x_ref[...].astype(F32) + nn(att, wn_ref[...])).astype(BF)
    den_ref[...] = den
    colors = nt(den, wpix_ref[...])
    filt = filt_ref[...]
    misfit = -meas_ref[...]
    for c in range(3):
        misfit = misfit + jnp.where(filt == c, colors[:, 64 * c : 64 * c + 64], 0.0)
    spread = jnp.concatenate([jnp.where(filt == c, misfit, 0.0) for c in range(3)], axis=1).astype(BF)
    og = nn(spread, wpix_ref[...])
    og_ref[...] = og
    up = nt(og.astype(BF), wn_ref[...]).astype(BF)
    pack_ref[0:T, :] = up
    prod = up.astype(F32) * att.astype(F32)
    for e in range(H):
        a, b = window(V0 + HD * (e - e % 2))
        inner = jnp.sum(head_only(prod[:, a - VB : b - VB], V0 + HD * e, a), axis=1, keepdims=True)
        stats = jnp.where(lanes == 8 + e, inner, stats)
    stat_ref[...] = stats
    turned = stats.T[0:16, :]
    high = turned.astype(BF)
    rest = turned - high.astype(F32)
    mid = rest.astype(BF)
    low = (rest - mid.astype(F32)).astype(BF)
    pack_ref[T : T + 16, :] = jnp.concatenate(
        [
            high, mid, low, jnp.concatenate(rows[:16], axis=0).astype(BF),
            jnp.concatenate(rows[16:] + [jnp.zeros((14, T), F32)], axis=0).astype(BF),
        ],
        axis=1,
    )


def query_kernel(win_ref, e_ref, up_ref, stat_ref, gq_ref, acc_ref):
    acc_ref[...] = jnp.zeros_like(acc_ref)
    for e in range(0, H, 2):
        a, b = window(V0 + HD * e)
        up = stacked(up_ref[0:T, a - VB : b - VB], V0 + HD * e, a)
        dprob = nt(up, win_ref[:, a:b])
        p = e_ref[e * T : (e + 2) * T, :].astype(F32)
        inner = jnp.concatenate([stat_ref[:, 8 + e : 9 + e], stat_ref[:, 9 + e : 10 + e]], axis=0)
        inv = jnp.concatenate([stat_ref[:, 16 + e : 17 + e], stat_ref[:, 17 + e : 18 + e]], axis=0)
        ds = (p * (dprob - inner)).astype(BF)
        a, b = window(K0 + HD * e)
        dq = nn(ds, win_ref[:, a:b]) * (inv * FACTOR)
        acc_ref[:, a:b] += unstacked(dq, HD * e, a)
    gq_ref[...] = acc_ref[:, 0:HW].astype(BF)


def key_side(core_ref, win_ref, tiles, gk_ref, gv_ref):
    own = slice(4 * T, 5 * T)
    kc = (lax.broadcasted_iota(jnp.int32, (T, T), 0) & 8) > 0
    second = core_ref[0].astype(F32)
    bias, stats, ups = [], [], []
    for t, r, pack_ref, base in tiles:
        ups.append(pack_ref[base : base + T, :])
        extra = pack_ref[base + T : base + T + 16, :].astype(F32)
        stats.append(extra[:, 0:128] + extra[:, 128:256] + extra[:, 256:384])
        seen = []
        for w in range(2):
            on = []
            for row, col in position(t, r):
                i = (2 - row) * 6 + (2 - col) * 2 + w
                on.append(extra[i : i + 1, 384:512] if i < 16 else extra[i - 16 : i - 15, 512:640])
            seen.append(on[0] * (1.0 - second) + on[1] * second)
        bias.append((1.0 - jnp.where(kc, seen[1], seen[0])) * OFF)
    bias = jnp.concatenate(bias, axis=1)
    stats = jnp.concatenate(stats, axis=1)
    ups = jnp.concatenate(ups, axis=0)
    count = len(tiles) * T

    def queries(a, b):
        return jnp.concatenate(
            [win_ref[(3 * t + r) * T : (3 * t + r + 1) * T, Q0 + a : Q0 + b] for t, r, _, _ in tiles], axis=0
        )

    for e in range(0, H, 2):
        a, b = window(K0 + HD * e)
        if Q0 + b <= QKV:
            q = queries(a, b)
        else:
            q = jnp.concatenate([queries(a, HW), jnp.zeros((count, b - HW), BF)], axis=1)
        c, d = window(V0 + HD * e)
        up = ups[:, c - VB : d - VB]
        scores = nt(stacked(win_ref[own, a:b], HD * e, a), q)
        dprob = nt(stacked(win_ref[own, c:d], V0 + HD * e, c), up)
        ps, dss = [], []
        for i in range(2):
            rows = slice(i * T, (i + 1) * T)
            p = jnp.exp2(scores[rows, :] * SCALE2 + bias - stats[e + i : e + i + 1, :])
            ps.append(p.astype(BF))
            dss.append((p * (dprob[rows, :] - stats[8 + e + i : 9 + e + i, :])).astype(BF))
        gk_ref[:, a:b] += unstacked(nn(jnp.concatenate(dss, axis=0), q), HD * e, a)
        gv_ref[:, c - VB : d - VB] += unstacked(nn(jnp.concatenate(ps, axis=0), up), V0 + HD * e, c)


def key_near_kernel(core_ref, win_ref, own_ref, before_ref, after_ref, outer_ref, inner_ref, gk_ref, gv_ref):
    gk_ref[...] = jnp.zeros_like(gk_ref)
    gv_ref[...] = jnp.zeros_like(gv_ref)
    tiles = (
        (1, 0, before_ref, 0), (1, 1, own_ref, 0), (1, 2, after_ref, 0), (0, 1, outer_ref, 0), (2, 1, inner_ref, 0)
    )
    key_side(core_ref, win_ref, tiles, gk_ref, gv_ref)


def finish_kernel(
    core_ref, win_ref, packo_ref, packi_ref, gk0_ref, gv0_ref, gq_ref, order_ref, x_ref, gain_ref, og_ref,
    b0, b1, b2, b3, b4, b5, b6, b7,
    out_ref, gk_ref, gv_ref, w_ref,
):
    collect((b0, b1, b2, b3, b4, b5, b6, b7), 0, 144, w_ref)
    gk_ref[...] = gk0_ref[...]
    gv_ref[...] = gv0_ref[...]
    tiles = ((0, 0, packo_ref, 0), (0, 2, packo_ref, 144), (2, 0, packi_ref, 0), (2, 2, packi_ref, 144))
    key_side(core_ref, win_ref, tiles, gk_ref, gv_ref)
    gk = (gk_ref[:, 0:HW] * FACTOR).astype(BF)
    gv = gv_ref[:, 64:640].astype(BF)
    grads = jnp.concatenate([gk, gv, gq_ref[...]], axis=1)
    moved = nt(grads, w_ref[...])
    high = moved.astype(BF)
    low = (moved - high.astype(F32)).astype(BF)
    both = nt(jnp.concatenate([high, low], axis=0), order_ref[...])
    grad = (both[0:T, :] + both[T : 2 * T, :]) * gain_ref[...]
    center, rstd = norm_parts(x_ref[...].astype(F32))
    xhat = center * rstd
    mean_g = jnp.mean(grad, axis=-1, keepdims=True)
    mean_gx = jnp.mean(grad * xhat, axis=-1, keepdims=True)
    out_ref[...] = rstd * (grad - mean_g - xhat * mean_gx) + og_ref[...]


def shaped(shape, dtype=BF):
    return jax.ShapeDtypeStruct(shape, dtype)


def shards_held(yh, z, x, core, block, second):
    cs = core ^ jnp.asarray((block >= 4).astype(np.int32))
    shift = np.array([0, 3, 1, 2] * 2)[block]
    xs = (x + jnp.where(cs == 0, jnp.asarray(shift), jnp.asarray(-shift))) & 3
    hops = jnp.where(second, 3 - xs, xs + 1)
    zs = (z + jnp.where(cs == 0, -hops, hops)) & 7
    other = jnp.logical_xor(second, (xs == 3) & (cs == 1)).astype(jnp.int32)
    return (yh ^ other) * 8 + zs


def weight_targets(yh, z, x, core):
    place = np.arange(D)
    block, row = place // 144, place % 144
    held = shards_held(yh, z, x, core, block, row >= 72)
    return (held * 72 + row % 72).astype(jnp.int32).reshape(1, D)


def out_targets(yh, z, x, core):
    place = np.arange(384)
    block, row = place // 48, place % 48
    held = shards_held(yh, z, x, core, block, row >= 24) * 36 + 64
    row = row % 24
    whole = held + row
    lower = jnp.where(row < 12, held + 24 + row, -1)
    upper = jnp.where(row >= 12, held + 12 + row, -1)
    return jnp.stack([whole, lower, upper]).astype(jnp.int32)


def device(yh, z, yl, x, core):
    return (((yh * 8 + z % 8) * 4 + yl) * 4 + x) * 2 + core


def fetch_routes():
    first, second = [], []
    for yh in range(2):
        for z in range(8):
            for yl in range(4):
                for x in range(4):
                    for core in range(2):
                        me = device(yh, z, yl, x, core)
                        way = 1 if core else -1
                        near, far = z + way * (x + 1), z + way * (3 - x)
                        if x == 3 and core == 1:
                            first.append((device(1 - yh, near, 3 - yl, x, core), me))
                            second.append((me, me))
                        else:
                            first.append((device(yh, near, yl, x, core), me))
                            second.append((device(1 - yh, far, 3 - yl, x, core), me))
    return first, second


def on_device(tokens, gain, w_query, w_key, w_value, w_out, w_pixel, measured, filter_color, block_mask):
    yh, z, xi, core = (lax.axis_index(n) for n in ("yh", "z", "x", "core"))
    which = core.reshape(1).astype(jnp.int32)
    x = tokens.reshape(T, D)
    gain = gain.reshape(1, D)
    south = [(2 * i, 2 * i + 2) for i in range(15)] + [(2 * i + 3, 2 * i + 1) for i in range(15)]
    north = [(j, i) for i, j in south]
    ring = [(2 * i, (2 * i + 2) % 8) for i in range(4)] + [((2 * i + 3) % 8, 2 * i + 1) for i in range(4)]
    back = [(j, i) for i, j in ring]
    border = [(2 * i + 1, (2 * i + 2) % 32) for i in range(16)]
    border = border + [(j, i) for i, j in border]
    lat, lon = ("yh", "z"), ("yl", "x", "core")
    first, second = fetch_routes()

    def swap(v):
        return lax.ppermute(v, "core", [(0, 1), (1, 0)])

    def along(v, perm):
        return lax.ppermute(v, ("x", "core"), perm)

    def rows_beside(own):
        return lax.ppermute(own, lat + ("core",), south), lax.ppermute(own, lat + ("core",), north)

    def sides(column):
        return lax.ppermute(column, lon, border), swap(column)

    def placed(v, rows, cols):
        return lax.pad(v, jnp.zeros((), BF), ((*rows, 0), (*cols, 0)))

    at_row = lax.broadcasted_iota(jnp.int32, (96, QKV), 0)
    at_col = lax.broadcasted_iota(jnp.int32, (96, QKV), 1)
    lefts = placed(w_out, (48, 12), (D, -HW))
    rights = placed(w_out, (60, 0), (HW, 0))
    mine = (
        placed(w_key, (0, 24), (0, 2 * HW)) + placed(w_value, (0, 24), (HW, HW))
        + placed(w_query, (0, 24), (2 * HW, 0)) + placed(w_out, (72, -12), (0, HW))
        + jnp.where(at_row >= 72, lefts, 0) + jnp.where((at_row >= 84) & (at_col >= D), rights, 0)
    )
    one, two = lax.ppermute(mine, lat + lon, first), lax.ppermute(mine, lat + lon, second)
    fetched = jnp.concatenate([one[:72], two[:72], one[72:], two[72:]], axis=0)
    before, after = rows_beside(x)
    column = jnp.concatenate([before, x, after], axis=0)
    outer, inner = sides(column)
    target = weight_targets(yh, z, xi, core)

    def ordering(target):
        return pl.pallas_call(
            order_kernel, out_shape=shaped((D, D)), in_specs=[VMEM], out_specs=VMEM, compiler_params=params(8),
            cost_estimate=pl.CostEstimate(flops=2_000_000_000, bytes_accessed=3_000_000, transcendentals=0),
        )(target)


    def hidden(v):
        return pl.pallas_call(
            hidden_kernel, out_shape=shaped((3 * T, D)), in_specs=[VMEM] * 3, out_specs=VMEM,
            scratch_shapes=[pltpu.VMEM((D, D), BF)], compiler_params=params(16),
            cost_estimate=pl.CostEstimate(flops=3_000_000_000, bytes_accessed=5_000_000, transcendentals=0),
        )(v, gain, target)

    fetched, hc = lax.optimization_barrier((fetched, hidden(column)))
    right, left = along(fetched, ring), along(fetched, back)
    right, left, he, outer = lax.optimization_barrier((right, left, hidden(inner), outer))
    fetched_too = swap(fetched)
    across, hw = lax.optimization_barrier((along(right, ring), hidden(outer)))
    blocks = (fetched, right, left, across, fetched_too, swap(right), swap(left), swap(across))

    win, wn = pl.pallas_call(
        project_kernel, out_shape=(shaped((9 * T, QKV)), shaped((640, D))),
        in_specs=[VMEM] * 12, out_specs=(VMEM,) * 2,
        scratch_shapes=[pltpu.VMEM((384, QKV), BF), pltpu.VMEM((D, QKV), BF)],
        compiler_params=params(24),
        cost_estimate=pl.CostEstimate(flops=6_000_000_000, bytes_accessed=8_000_000, transcendentals=0),
    )(out_targets(yh, z, xi, core), hw, hc, he, *blocks)
    e, den, og, pack, stat = pl.pallas_call(
        forward_kernel,
        out_shape=(
            shaped((H * T, 9 * T)), shaped((T, D)), shaped((T, D), F32), shaped((144, 640)), shaped((T, T), F32),
        ),
        in_specs=[SMEM] + [VMEM] * 6, out_specs=(VMEM,) * 5,
        scratch_shapes=[pltpu.VMEM((T, 9 * T), F32), pltpu.VMEM((T, 640), F32)],
        compiler_params=params(18),
        cost_estimate=pl.CostEstimate(flops=6_000_000_000, bytes_accessed=8_000_000, transcendentals=1_000_000),
    )(jnp.concatenate([block_mask.reshape(30), which]), win, wn, w_pixel.T, x, measured.reshape(T, 64), filter_color.reshape(T, 64))
    before, after = rows_beside(pack)
    near_outer, near_inner = sides(pack)
    corners, target, stat_late = lax.optimization_barrier((jnp.concatenate([before, after], axis=0), target, stat))
    packs_outer, packs_inner = sides(corners)
    gq = pl.pallas_call(
        query_kernel, out_shape=shaped((T, HW)), in_specs=[VMEM] * 4, out_specs=VMEM,
        scratch_shapes=[pltpu.VMEM((T, 640), F32)], compiler_params=params(16),
        cost_estimate=pl.CostEstimate(flops=4_000_000_000, bytes_accessed=6_000_000, transcendentals=0),
    )(win, e, pack, stat_late)
    gk, gv = pl.pallas_call(
        key_near_kernel, out_shape=(shaped((T, 640), F32),) * 2, in_specs=[SMEM] + [VMEM] * 6, out_specs=(VMEM,) * 2,
        compiler_params=params(16),
        cost_estimate=pl.CostEstimate(flops=4_000_000_000, bytes_accessed=6_000_000, transcendentals=0),
    )(which, win, pack, before, after, near_outer, near_inner)
    guidance = pl.pallas_call(
        finish_kernel, out_shape=shaped((T, D), F32), in_specs=[SMEM] + [VMEM] * 18, out_specs=VMEM,
        scratch_shapes=[pltpu.VMEM((T, 640), F32)] * 2 + [pltpu.VMEM((D, QKV), BF)],
        compiler_params=params(20),
    )(which, win, packs_outer, packs_inner, gk, gv, gq, ordering(target), x, gain, og, *blocks)
    return den.reshape(tokens.shape), guidance.reshape(tokens.shape)


def solution(mesh):
    split = Mesh(mesh.devices.reshape(2, 8, 4, 4, 2), ("yh", "z", "yl", "x", "core"))
    lat, lon = ("yh", "z"), ("yl", "x", "core")
    return jax.shard_map(
        on_device,
        mesh=split,
        in_specs=(
            P(lat, lon, None), P(), P(lat, None), P(lat, None), P(lat, None), P(lat, None), P(),
            P(lat, lon, None), P(lat, lon, None), P(lat, lon, None, None),
        ),
        out_specs=(P(lat, lon, None), P(lat, lon, None)),
        check_vma=False,
    )
```

```python
import functools

import jax
import jax.numpy as jnp
import numpy as np
from jax import lax
from jax.experimental import pallas as pl
from jax.experimental.pallas import tpu as pltpu
from jax.sharding import Mesh, PartitionSpec as P

H = 8
HD = 72
HW = 576
D = 1152
T = 128
QKV = 3 * HW
FACTOR = HD ** (-0.5)
SCALE2 = FACTOR * 1.4426950408889634
OFF = -1e30
BF = jnp.bfloat16
F32 = jnp.float32
VMEM = pl.BlockSpec(memory_space=pltpu.VMEM)
SMEM = pl.BlockSpec(memory_space=pltpu.SMEM)
ANY = pl.BlockSpec(memory_space=pl.ANY)
HBM = pl.BlockSpec(memory_space=pltpu.HBM)
K0, V0, Q0 = 0, HW, 2 * HW
VB = 512


def params(limit=40):
    return pltpu.CompilerParams(vmem_limit_bytes=limit * 1024 * 1024)


def nt(left, right):
    return lax.dot_general(left, right, (((1,), (1,)), ((), ())), preferred_element_type=F32)


def nn(left, right):
    return jnp.dot(left, right, preferred_element_type=F32)


def window(first):
    start = first // 128 * 128
    return start, start + 256


def stacked(x, first, start):
    return jnp.concatenate([head_only(x, first, start), head_only(x, first + HD, start)], axis=0)


def unstacked(x, first, start):
    return head_only(x[0:T, :], first, start) + head_only(x[T : 2 * T, :], first + HD, start)


def head_only(x, first, start):
    lane = lax.broadcasted_iota(jnp.int32, x.shape, 1) + start
    return jnp.where((lane >= first) & (lane < first + HD), x, jnp.zeros_like(x))


def norm_parts(x):
    center = x - jnp.mean(x, axis=-1, keepdims=True)
    rstd = lax.rsqrt(jnp.mean(center * center, axis=-1, keepdims=True) + 1e-6)
    return center, rstd


def order_kernel(target_ref, order_ref):
    rows = lax.broadcasted_iota(jnp.int32, (D, D), 0)
    order_ref[...] = jnp.where(rows == target_ref[...], 1.0, 0.0).astype(BF)


def hidden_kernel(x_ref, gain_ref, target_ref, out_ref, order_ref):
    order_kernel(target_ref, order_ref)
    for i in range(x_ref.shape[0] // T):
        center, rstd = norm_parts(x_ref[i * T : (i + 1) * T, :].astype(F32))
        hidden = (center * rstd * gain_ref[...]).astype(BF)
        out_ref[i * T : (i + 1) * T, :] = nn(hidden, order_ref[...]).astype(BF)


def collect(blocks, first, rows, w_ref):
    for i, block in enumerate(blocks):
        w_ref[rows * i : rows * (i + 1), :] = block[first : first + rows, :]


def position(slot_t, slot_r):
    turned = 2 - slot_r
    return (slot_r if slot_t == 1 else turned, slot_t), (turned if slot_t == 1 else slot_r, 2 - slot_t)


def project_kernel(
    place_ref, hw_ref, hc_ref, he_ref, b0, b1, b2, b3, b4, b5, b6, b7, win_ref, wn_ref, wo_ref, w_ref
):
    collect((b0, b1, b2, b3, b4, b5, b6, b7), 144, 48, wo_ref)
    collect((b0, b1, b2, b3, b4, b5, b6, b7), 0, 144, w_ref)
    for g, h_ref in enumerate((hw_ref, hc_ref, he_ref)):
        for part in range(3):
            s = slice(part * T, (part + 1) * T)
            win_ref[(g * 3 + part) * T : (g * 3 + part + 1) * T, :] = nn(h_ref[s, :], w_ref[...]).astype(BF)
    lane_of = lax.broadcasted_iota(jnp.int32, (640, 384), 0)
    whole, lower, upper = (
        jnp.where(lane_of == place_ref[i : i + 1, :], 1.0, 0.0).astype(BF) for i in range(3)
    )
    halves = nn(jnp.concatenate([lower, upper], axis=0), wo_ref[:, D:QKV])
    wn_ref[...] = (
        nn(whole, wo_ref[:, 0:D]) + jnp.concatenate([halves[0:640, :], halves[640:1280, :]], axis=1)
    ).astype(BF)


def forward_kernel(
    blocks_ref, win_ref, wn_ref, wpix_ref, x_ref, meas_ref, filt_ref,
    e_ref, den_ref, og_ref, pack_ref, stat_ref,
    bias_ref, acc_ref,
):
    acc_ref[...] = jnp.zeros_like(acc_ref)

    qc = (lax.broadcasted_iota(jnp.int32, (T, T), 0) & 8) > 0
    kc = (lax.broadcasted_iota(jnp.int32, (T, T), 1) & 8) > 0

    core = blocks_ref[30]

    table = {
        (c, r, w): blocks_ref[(c * 3 + r) * 5 + w - c].astype(F32) if 0 <= w - c < 5 else jnp.float32(0.0)
        for c in range(2)
        for r in range(3)
        for w in range(6)
    }

    lane_c = (lax.broadcasted_iota(jnp.int32, (1, T), 1) & 8) > 0
    rows = []
    for r in range(3):
        for w in range(6):
            rows.append(jnp.where(lane_c, table[1, r, w], table[0, r, w]))
    for slot_t in range(3):
        for slot_r in range(3):
            (r0, t0), (r1, t1) = position(slot_t, slot_r)
            (m00, m01), (m10, m11) = [
                [jnp.where(core == 0, table[c, r0, 2 * t0 + w], table[c, r1, 2 * t1 + w]) for w in range(2)]
                for c in range(2)
            ]
            seen = jnp.where(qc, jnp.where(kc, m11, m10), jnp.where(kc, m01, m00))
            j = 3 * slot_t + slot_r
            bias_ref[:, j * T : (j + 1) * T] = (1.0 - seen) * OFF
    own = slice(4 * T, 5 * T)
    lanes = lax.broadcasted_iota(jnp.int32, (T, T), 1)
    stats = jnp.zeros((T, T), F32)
    for e in range(0, H, 2):
        a, b = window(K0 + HD * e)
        q = win_ref[own, Q0 + a : min(Q0 + b, QKV)]
        if Q0 + b > QKV:
            q = jnp.concatenate([q, jnp.zeros((T, Q0 + b - QKV), BF)], axis=1)
        scores = nt(stacked(q, HD * e, a), win_ref[:, a:b])
        lows, invs = [], []
        for i in range(2):
            s = scores[i * T : (i + 1) * T, :] * SCALE2 + bias_ref[...]
            peak = jnp.max(s, axis=1, keepdims=True)
            p = jnp.exp2(s - peak)
            total = jnp.sum(p, axis=1, keepdims=True)
            inv = 1.0 / total
            stats = jnp.where(lanes == e + i, peak + jnp.log2(total), stats)
            stats = jnp.where(lanes == 16 + e + i, inv, stats)
            lows.append(p.astype(BF))
            invs.append(inv)
        low = jnp.concatenate(lows, axis=0)
        e_ref[e * T : (e + 2) * T, :] = low
        a, b = window(V0 + HD * e)
        o = nn(low, win_ref[:, a:b]) * jnp.concatenate(invs, axis=0)
        acc_ref[:, a - VB : b - VB] += unstacked(o, V0 + HD * e, a)

    att = acc_ref[...].astype(BF)
    den = (x_ref[...].astype(F32) + nn(att, wn_ref[...])).astype(BF)
    den_ref[...] = den
    colors = nt(den, wpix_ref[...])
    filt = filt_ref[...]
    misfit = -meas_ref[...]
    for c in range(3):
        misfit = misfit + jnp.where(filt == c, colors[:, 64 * c : 64 * c + 64], 0.0)
    spread = jnp.concatenate([jnp.where(filt == c, misfit, 0.0) for c in range(3)], axis=1).astype(BF)
    og = nn(spread, wpix_ref[...])
    og_ref[...] = og
    up = nt(og.astype(BF), wn_ref[...]).astype(BF)
    pack_ref[0:T, :] = up
    prod = up.astype(F32) * att.astype(F32)
    for e in range(H):
        a, b = window(V0 + HD * (e - e % 2))
        inner = jnp.sum(head_only(prod[:, a - VB : b - VB], V0 + HD * e, a), axis=1, keepdims=True)
        stats = jnp.where(lanes == 8 + e, inner, stats)
    stat_ref[...] = stats
    turned = stats.T[0:16, :]
    high = turned.astype(BF)
    rest = turned - high.astype(F32)
    mid = rest.astype(BF)
    low = (rest - mid.astype(F32)).astype(BF)
    pack_ref[T : T + 16, :] = jnp.concatenate(
        [
            high, mid, low, jnp.concatenate(rows[:16], axis=0).astype(BF),
            jnp.concatenate(rows[16:] + [jnp.zeros((14, T), F32)], axis=0).astype(BF),
        ],
        axis=1,
    )


def query_kernel(win_ref, e_ref, up_ref, stat_ref, gq_ref, acc_ref):
    acc_ref[...] = jnp.zeros_like(acc_ref)
    for e in range(0, H, 2):
        a, b = window(V0 + HD * e)
        up = stacked(up_ref[0:T, a - VB : b - VB], V0 + HD * e, a)
        dprob = nt(up, win_ref[:, a:b])
        p = e_ref[e * T : (e + 2) * T, :].astype(F32)
        inner = jnp.concatenate([stat_ref[:, 8 + e : 9 + e], stat_ref[:, 9 + e : 10 + e]], axis=0)
        inv = jnp.concatenate([stat_ref[:, 16 + e : 17 + e], stat_ref[:, 17 + e : 18 + e]], axis=0)
        ds = (p * (dprob - inner)).astype(BF)
        a, b = window(K0 + HD * e)
        dq = nn(ds, win_ref[:, a:b]) * (inv * FACTOR)
        acc_ref[:, a:b] += unstacked(dq, HD * e, a)
    gq_ref[...] = acc_ref[:, 0:HW].astype(BF)


def key_side(core_ref, win_ref, tiles, gk_ref, gv_ref):
    own = slice(4 * T, 5 * T)
    kc = (lax.broadcasted_iota(jnp.int32, (T, T), 0) & 8) > 0
    second = core_ref[0].astype(F32)
    bias, stats, ups = [], [], []
    for t, r, pack_ref, base in tiles:
        ups.append(pack_ref[base : base + T, :])
        extra = pack_ref[base + T : base + T + 16, :].astype(F32)
        stats.append(extra[:, 0:128] + extra[:, 128:256] + extra[:, 256:384])
        seen = []
        for w in range(2):
            on = []
            for row, col in position(t, r):
                i = (2 - row) * 6 + (2 - col) * 2 + w
                on.append(extra[i : i + 1, 384:512] if i < 16 else extra[i - 16 : i - 15, 512:640])
            seen.append(on[0] * (1.0 - second) + on[1] * second)
        bias.append((1.0 - jnp.where(kc, seen[1], seen[0])) * OFF)
    bias = jnp.concatenate(bias, axis=1)
    stats = jnp.concatenate(stats, axis=1)
    ups = jnp.concatenate(ups, axis=0)
    count = len(tiles) * T

    def queries(a, b):
        return jnp.concatenate(
            [win_ref[(3 * t + r) * T : (3 * t + r + 1) * T, Q0 + a : Q0 + b] for t, r, _, _ in tiles], axis=0
        )

    for e in range(0, H, 2):
        a, b = window(K0 + HD * e)
        if Q0 + b <= QKV:
            q = queries(a, b)
        else:
            q = jnp.concatenate([queries(a, HW), jnp.zeros((count, b - HW), BF)], axis=1)
        c, d = window(V0 + HD * e)
        up = ups[:, c - VB : d - VB]
        scores = nt(stacked(win_ref[own, a:b], HD * e, a), q)
        dprob = nt(stacked(win_ref[own, c:d], V0 + HD * e, c), up)
        ps, dss = [], []
        for i in range(2):
            rows = slice(i * T, (i + 1) * T)
            p = jnp.exp2(scores[rows, :] * SCALE2 + bias - stats[e + i : e + i + 1, :])
            ps.append(p.astype(BF))
            dss.append((p * (dprob[rows, :] - stats[8 + e + i : 9 + e + i, :])).astype(BF))
        gk_ref[:, a:b] += unstacked(nn(jnp.concatenate(dss, axis=0), q), HD * e, a)
        gv_ref[:, c - VB : d - VB] += unstacked(nn(jnp.concatenate(ps, axis=0), up), V0 + HD * e, c)


def key_near_kernel(core_ref, win_ref, own_ref, inner_ref, gk_ref, gv_ref):
    gk_ref[...] = jnp.zeros_like(gk_ref)
    gv_ref[...] = jnp.zeros_like(gv_ref)
    tiles = [(t, r, ref, 144 * r) for t, ref in ((1, own_ref), (2, inner_ref)) for r in range(3)]
    key_side(core_ref, win_ref, tiles, gk_ref, gv_ref)


def finish_kernel(
    core_ref, win_ref, outer_ref, gk0_ref, gv0_ref, gq_ref, order_ref, x_ref, gain_ref, og_ref,
    b0, b1, b2, b3, b4, b5, b6, b7,
    out_ref, gk_ref, gv_ref, w_ref,
):
    collect((b0, b1, b2, b3, b4, b5, b6, b7), 0, 144, w_ref)
    gk_ref[...] = gk0_ref[...]
    gv_ref[...] = gv0_ref[...]
    key_side(core_ref, win_ref, [(0, r, outer_ref, 144 * r) for r in range(3)], gk_ref, gv_ref)
    gk = (gk_ref[:, 0:HW] * FACTOR).astype(BF)
    gv = gv_ref[:, 64:640].astype(BF)
    grads = jnp.concatenate([gk, gv, gq_ref[...]], axis=1)
    moved = nt(grads, w_ref[...])
    high = moved.astype(BF)
    low = (moved - high.astype(F32)).astype(BF)
    both = nt(jnp.concatenate([high, low], axis=0), order_ref[...])
    grad = (both[0:T, :] + both[T : 2 * T, :]) * gain_ref[...]
    center, rstd = norm_parts(x_ref[...].astype(F32))
    xhat = center * rstd
    mean_g = jnp.mean(grad, axis=-1, keepdims=True)
    mean_gx = jnp.mean(grad * xhat, axis=-1, keepdims=True)
    out_ref[...] = rstd * (grad - mean_g - xhat * mean_gx) + og_ref[...]


def shaped(shape, dtype=BF):
    return jax.ShapeDtypeStruct(shape, dtype)


def shards_held(yh, z, x, core, block, second):
    cs = core ^ jnp.asarray((block >= 4).astype(np.int32))
    shift = np.array([0, 3, 1, 2] * 2)[block]
    xs = (x + jnp.where(cs == 0, jnp.asarray(shift), jnp.asarray(-shift))) & 3
    hops = jnp.where(second, 3 - xs, xs + 1)
    zs = (z + jnp.where(cs == 0, -hops, hops)) & 7
    other = jnp.logical_xor(second, (xs == 3) & (cs == 1)).astype(jnp.int32)
    return (yh ^ other) * 8 + zs


def weight_targets(yh, z, x, core):
    place = np.arange(D)
    block, row = place // 144, place % 144
    held = shards_held(yh, z, x, core, block, row >= 72)
    return (held * 72 + row % 72).astype(jnp.int32).reshape(1, D)


def out_targets(yh, z, x, core):
    place = np.arange(384)
    block, row = place // 48, place % 48
    held = shards_held(yh, z, x, core, block, row >= 24) * 36 + 64
    row = row % 24
    whole = held + row
    lower = jnp.where(row < 12, held + 24 + row, -1)
    upper = jnp.where(row >= 12, held + 12 + row, -1)
    return jnp.stack([whole, lower, upper]).astype(jnp.int32)


def device(yh, z, yl, x, core):
    return (((yh * 8 + z % 8) * 4 + yl) * 4 + x) * 2 + core


def fetch_routes():
    first, second = [], []
    for yh in range(2):
        for z in range(8):
            for yl in range(4):
                for x in range(4):
                    for core in range(2):
                        me = device(yh, z, yl, x, core)
                        way = 1 if core else -1
                        near, far = z + way * (x + 1), z + way * (3 - x)
                        if x == 3 and core == 1:
                            first.append((device(1 - yh, near, 3 - yl, x, core), me))
                            second.append((me, me))
                        else:
                            first.append((device(yh, near, yl, x, core), me))
                            second.append((device(1 - yh, far, 3 - yl, x, core), me))
    return first, second


def on_device(tokens, gain, w_query, w_key, w_value, w_out, w_pixel, measured, filter_color, block_mask):
    yh, z, xi, core = (lax.axis_index(n) for n in ("yh", "z", "x", "core"))
    which = core.reshape(1).astype(jnp.int32)
    x = tokens.reshape(T, D)
    gain = gain.reshape(1, D)
    south = [(2 * i, 2 * i + 2) for i in range(15)] + [(2 * i + 3, 2 * i + 1) for i in range(15)]
    north = [(j, i) for i, j in south]
    ring = [(2 * i, (2 * i + 2) % 8) for i in range(4)] + [((2 * i + 3) % 8, 2 * i + 1) for i in range(4)]
    back = [(j, i) for i, j in ring]
    border = [(2 * i + 1, (2 * i + 2) % 32) for i in range(16)]
    border = border + [(j, i) for i, j in border]
    lat, lon = ("yh", "z"), ("yl", "x", "core")
    first, second = fetch_routes()

    def swap(v):
        return lax.ppermute(v, "core", [(0, 1), (1, 0)])

    def along(v, perm):
        return lax.ppermute(v, ("x", "core"), perm)

    def rows_beside(own):
        return lax.ppermute(own, lat + ("core",), south), lax.ppermute(own, lat + ("core",), north)

    def sides(column):
        return lax.ppermute(column, lon, border), swap(column)

    def placed(v, rows, cols):
        return lax.pad(v, jnp.zeros((), BF), ((*rows, 0), (*cols, 0)))

    at_row = lax.broadcasted_iota(jnp.int32, (96, QKV), 0)
    at_col = lax.broadcasted_iota(jnp.int32, (96, QKV), 1)
    lefts = placed(w_out, (48, 12), (D, -HW))
    rights = placed(w_out, (60, 0), (HW, 0))
    mine = (
        placed(w_key, (0, 24), (0, 2 * HW)) + placed(w_value, (0, 24), (HW, HW))
        + placed(w_query, (0, 24), (2 * HW, 0)) + placed(w_out, (72, -12), (0, HW))
        + jnp.where(at_row >= 72, lefts, 0) + jnp.where((at_row >= 84) & (at_col >= D), rights, 0)
    )
    one, two = lax.ppermute(mine, lat + lon, first), lax.ppermute(mine, lat + lon, second)
    fetched = jnp.concatenate([one[:72], two[:72], one[72:], two[72:]], axis=0)
    before, after = rows_beside(x)
    column = jnp.concatenate([before, x, after], axis=0)
    outer, inner = sides(column)
    target = weight_targets(yh, z, xi, core)

    def ordering(target):
        return pl.pallas_call(
            order_kernel, out_shape=shaped((D, D)), in_specs=[VMEM], out_specs=VMEM, compiler_params=params(8),
            cost_estimate=pl.CostEstimate(flops=2_000_000_000, bytes_accessed=3_000_000, transcendentals=0),
        )(target)


    def hidden(v):
        return pl.pallas_call(
            hidden_kernel, out_shape=shaped((3 * T, D)), in_specs=[VMEM] * 3, out_specs=VMEM,
            scratch_shapes=[pltpu.VMEM((D, D), BF)], compiler_params=params(16),
            cost_estimate=pl.CostEstimate(flops=3_000_000_000, bytes_accessed=5_000_000, transcendentals=0),
        )(v, gain, target)

    fetched, hc = lax.optimization_barrier((fetched, hidden(column)))
    right, left = along(fetched, ring), along(fetched, back)
    right, left, he, outer = lax.optimization_barrier((right, left, hidden(inner), outer))
    fetched_too = swap(fetched)
    across, hw = lax.optimization_barrier((along(right, ring), hidden(outer)))
    blocks = (fetched, right, left, across, fetched_too, swap(right), swap(left), swap(across))

    win, wn = pl.pallas_call(
        project_kernel, out_shape=(shaped((9 * T, QKV)), shaped((640, D))),
        in_specs=[VMEM] * 12, out_specs=(VMEM,) * 2,
        scratch_shapes=[pltpu.VMEM((384, QKV), BF), pltpu.VMEM((D, QKV), BF)],
        compiler_params=params(24),
        cost_estimate=pl.CostEstimate(flops=6_000_000_000, bytes_accessed=8_000_000, transcendentals=0),
    )(out_targets(yh, z, xi, core), hw, hc, he, *blocks)
    e, den, og, pack, stat = pl.pallas_call(
        forward_kernel,
        out_shape=(
            shaped((H * T, 9 * T)), shaped((T, D)), shaped((T, D), F32), shaped((144, 640)), shaped((T, T), F32),
        ),
        in_specs=[SMEM] + [VMEM] * 6, out_specs=(VMEM,) * 5,
        scratch_shapes=[pltpu.VMEM((T, 9 * T), F32), pltpu.VMEM((T, 640), F32)],
        compiler_params=params(18),
        cost_estimate=pl.CostEstimate(flops=6_000_000_000, bytes_accessed=8_000_000, transcendentals=1_000_000),
    )(jnp.concatenate([block_mask.reshape(30), which]), win, wn, w_pixel.T, x, measured.reshape(T, 64), filter_color.reshape(T, 64))
    before, after = rows_beside(pack)
    packs, stat, target = lax.optimization_barrier((jnp.concatenate([before, pack, after], axis=0), stat, target))
    packs_outer = lax.ppermute(packs, lon, border)
    gq = pl.pallas_call(
        query_kernel, out_shape=shaped((T, HW)), in_specs=[VMEM] * 4, out_specs=VMEM,
        scratch_shapes=[pltpu.VMEM((T, 640), F32)], compiler_params=params(16),
        cost_estimate=pl.CostEstimate(flops=4_000_000_000, bytes_accessed=6_000_000, transcendentals=0),
    )(win, e, pack, stat)
    gq, packs_late = lax.optimization_barrier((gq, packs))
    packs_inner = swap(packs_late)
    gk, gv = pl.pallas_call(
        key_near_kernel, out_shape=(shaped((T, 640), F32),) * 2, in_specs=[SMEM] + [VMEM] * 3, out_specs=(VMEM,) * 2,
        compiler_params=params(16),
        cost_estimate=pl.CostEstimate(flops=4_000_000_000, bytes_accessed=6_000_000, transcendentals=0),
    )(which, win, packs, packs_inner)
    guidance = pl.pallas_call(
        finish_kernel, out_shape=shaped((T, D), F32), in_specs=[SMEM] + [VMEM] * 17, out_specs=VMEM,
        scratch_shapes=[pltpu.VMEM((T, 640), F32)] * 2 + [pltpu.VMEM((D, QKV), BF)],
        compiler_params=params(20),
    )(which, win, packs_outer, gk, gv, gq, ordering(target), x, gain, og, *blocks)
    return den.reshape(tokens.shape), guidance.reshape(tokens.shape)


def solution(mesh):
    split = Mesh(mesh.devices.reshape(2, 8, 4, 4, 2), ("yh", "z", "yl", "x", "core"))
    lat, lon = ("yh", "z"), ("yl", "x", "core")
    return jax.shard_map(
        on_device,
        mesh=split,
        in_specs=(
            P(lat, lon, None), P(), P(lat, None), P(lat, None), P(lat, None), P(lat, None), P(),
            P(lat, lon, None), P(lat, lon, None), P(lat, lon, None, None),
        ),
        out_specs=(P(lat, lon, None), P(lat, lon, None)),
        check_vma=False,
    )
```
